32 devices in a mesh: blk: 8 (over z, y), repl: 4 (over x, core).
Axes of the slice: x: 2, y: 2, z: 4, core: 2. Of those that a mesh axis runs over, the one named last changes fastest.
Arguments:
- feats: bfloat16 [16384, 512], P(('blk', 'repl')), may hold values from -6 to 6
- weight: bfloat16 [512, 512], replicated, may hold values from -0.25 to 0.25
- tile_vals: bfloat16 [128, 8, 128, 128], P(('blk', 'repl')), may hold values from -0.25 to 0.25
- tile_cols: int32 [128, 8], P(('blk', 'repl')), may hold values from 0 to 127, as said below
- tile_count: int32 [128], P(('blk', 'repl')), may hold values from 2 to 8, as said below
- cotangent: bfloat16 [16384, 512], P(('blk', 'repl')), may hold values from -6 to 6
Outputs:
- output: bfloat16 [16384, 512], P(('blk', 'repl'))
- weight_grad: float32 [512, 512], replicated
- feat_grad: bfloat16 [16384, 512], P(('blk', 'repl'))
The draws below stay inside these ranges and needn't reach their ends.
Inputs may be any that keep to these rules, and one draw needn't show every extreme that they name: `tile_cols`: slot 0 of block row k names k itself. Every named column block lies in a panel (of 2048 nodes, block row k being in panel k * 128 // 2048) at most 2 panels away from its row's panel, counted around a closed cycle of panels. `tile_count`: slots at and after a block row's count are not part of the adjacency.
All inputs are finite; a program needn't handle non-finite values.
Results may differ from the reference program's by a relative error of at most 0.011.
Values may be sent and summed in bfloat16 or wider, within the bound.
No kernel may reach another device: no remote copies, remote signals or barrier semaphores. Data moves between devices by JAX's collectives and lax.ppermute only.
A program may use at most 128 MiB of HBM per device.

```python
import math
import jax
import jax.numpy as jnp

F = 512
TILE = 128
SLOTS = 8
REACH = 2
NODES = 16384
PANEL = 2048
BLOCKS = 128


def draw_tile_cols(key, part):
    panel_blocks = PANEL // TILE
    panel_count = BLOCKS // panel_blocks
    first_key, second_key, third_key = jax.random.split(key, 3)
    block_row = jnp.arange(BLOCKS, dtype=jnp.int32)
    home_panel = block_row // panel_blocks
    offset = jax.random.randint(first_key, (BLOCKS, SLOTS), -REACH, REACH + 1)
    far_side = jnp.where(jax.random.randint(second_key, (BLOCKS,), 0, 2) == 0, -REACH, REACH)
    offset = offset.at[:, 1].set(far_side)
    inside = jax.random.randint(third_key, (BLOCKS, SLOTS), 0, panel_blocks)
    columns = (home_panel[:, None] + offset) % panel_count * panel_blocks + inside
    columns = columns.at[:, 0].set(block_row)
    return columns.astype(jnp.int32)


def draw_tile_count(key, part):
    panel_blocks = PANEL // TILE
    panel_count = BLOCKS // panel_blocks
    first_key, second_key, third_key = jax.random.split(key, 3)
    ceiling = jax.random.randint(first_key, (panel_count,), 3, SLOTS + 1)
    counts = jax.random.randint(second_key, (BLOCKS,), 2, SLOTS + 1)
    block_row = jnp.arange(BLOCKS, dtype=jnp.int32)
    counts = jnp.minimum(counts, ceiling[block_row // panel_blocks])
    fullest = jax.random.randint(third_key, (), 0, BLOCKS)
    counts = counts.at[fullest].set(SLOTS)
    return counts.astype(jnp.int32)


def with_spikes(entries, rng, source, target, blocks, factor):
    owner, partner = [(jnp.arange(entries.shape[position]) // (entries.shape[position] // blocks)).reshape([-1 if axis == position else 1 for axis in range(entries.ndim)]) for position in (source, target)]
    chosen = jax.random.permutation(rng, blocks)[partner]
    strong = (owner == chosen) | (owner == (partner + blocks // 2) % blocks)
    return jnp.where(strong, factor * entries, entries)


def block_scale(rng, dims, cuts, smallest, top_value):
    def one(dim, shards_of):
        heights = jax.random.uniform(jax.random.fold_in(jax.random.fold_in(rng, 6), dim), (shards_of,), jnp.float32, smallest / len(cuts), top_value / len(cuts))
        return jnp.repeat(jnp.exp(heights), dims[dim] // shards_of).reshape((-1,) + (1,) * (len(dims) - dim - 1))

    loudness = one(*cuts[0])
    for cut in cuts[1:]:
        loudness = loudness * one(*cut)
    return loudness


def scatter_about(rng, dims, scale, bound, cuts=(), held_as=jnp.bfloat16):
    values = scale * jax.random.normal(rng, dims, jnp.float32)
    if cuts:
        values = values * block_scale(rng, dims, cuts, -0.22, 0.18)
    return jnp.clip(values, -bound, bound).astype(held_as)


def noise_with(key, extent, spread, reach, cuts, heavy, kind=jnp.bfloat16):
    entries = spread * jax.random.normal(key, extent, jnp.float32)
    if cuts:
        entries = entries * block_scale(key, extent, cuts, -0.22, 0.18)
    return jnp.clip(with_spikes(entries, jax.random.fold_in(key, 3), *heavy), -reach, reach).astype(kind)


def setup_inputs(seed: int = 0) -> dict:
    key_of = jax.random.split(jax.random.key(seed), 7)
    feats = scatter_about(key_of[0], (NODES, F), 1.0, 6.0, ((0, 32),))
    weight = scatter_about(key_of[1], (F, F), F ** -0.5, 0.25)
    tile_vals = scatter_about(key_of[2], (BLOCKS, SLOTS, TILE, TILE), (SLOTS * TILE // 2) ** -0.5, 0.25, ((0, 32),))
    tile_cols = draw_tile_cols(jax.random.fold_in(key_of[6], 71), 0)
    tile_count = draw_tile_count(jax.random.fold_in(key_of[6], 71), 0)
    cotangent = noise_with(key_of[5], (NODES, F), 1.0, 6.0, ((0, 32),), (0, 1, 32, 2.75))
    return {"feats": feats, "weight": weight, "tile_vals": tile_vals, "tile_cols": tile_cols, "tile_count": tile_count, "cotangent": cotangent}


def silu_slope(preact):
    sigma = jax.nn.sigmoid(preact)
    return sigma * (1.0 + preact * (1.0 - sigma))

def reference(feats, weight, tile_vals, tile_cols, tile_count, cotangent):
    feat_blocks = feats.reshape(BLOCKS, TILE, F).astype(jnp.float32)
    live_slots = jnp.arange(SLOTS, dtype=jnp.int32)[None, :] < tile_count[:, None]
    summed = jnp.zeros((BLOCKS, TILE, F), jnp.float32)
    for slot_index in range(SLOTS):
        values = jnp.where(live_slots[:, slot_index, None, None], tile_vals[:, slot_index].astype(jnp.float32), jnp.float32(0.0))
        picked = feat_blocks[tile_cols[:, slot_index]]
        summed = summed + jnp.einsum('nij,njf->nif', values, picked)
    aggregate = summed.reshape(NODES, F).astype(jnp.bfloat16)
    preact = jnp.dot(aggregate, weight, preferred_element_type=jnp.float32)
    output = jax.nn.silu(preact).astype(jnp.bfloat16)
    slope = (cotangent.astype(jnp.float32) * silu_slope(preact)).astype(jnp.bfloat16)
    weight_grad = jnp.dot(aggregate.T, slope, preferred_element_type=jnp.float32) * (1.0 / math.sqrt(NODES))
    backward = jnp.dot(slope, weight.T, preferred_element_type=jnp.float32).astype(jnp.bfloat16)
    back_blocks = backward.reshape(BLOCKS, TILE, F).astype(jnp.float32)
    grad_sum = jnp.zeros((BLOCKS, TILE, F), jnp.float32)
    for slot_index in range(SLOTS):
        values = jnp.where(live_slots[:, slot_index, None, None], tile_vals[:, slot_index].astype(jnp.float32), jnp.float32(0.0))
        contrib = jnp.einsum('nji,njf->nif', values, back_blocks)
        grad_sum = grad_sum.at[tile_cols[:, slot_index]].add(contrib)
    feat_grad = grad_sum.reshape(NODES, F).astype(jnp.bfloat16)
    return (output, weight_grad, feat_grad)
```

```python
import functools
import math

import jax
import jax.numpy as jnp
from jax import lax
from jax.experimental import pallas as pl
from jax.experimental.pallas import tpu as pltpu
from jax.sharding import PartitionSpec as P

TILE = 128
SLOTS = 8
REACH = 2
SPAN = 2 * REACH + 1
VMEM_LIMIT = 48 * 1024 * 1024


def passed_along(value, axis, steps):
    count = lax.axis_size(axis)
    pairs = [(source, (source + steps) % count) for source in range(count)]
    return lax.ppermute(value, axis, pairs)


def silu_slope(preact):
    sigma = jax.nn.sigmoid(preact)
    return sigma * (1.0 + preact * (1.0 - sigma))


def window_index(tile_cols, tile_count, center, panel_blocks, cycle_size):
    panel_of = tile_cols // panel_blocks
    offset = (panel_of - center) % cycle_size
    offset = jnp.where(offset > REACH, offset - cycle_size, offset)
    index = (offset + REACH) * panel_blocks + tile_cols % panel_blocks
    slot_ids = jnp.arange(tile_cols.shape[1], dtype=jnp.int32)
    return jnp.where(slot_ids[None, :] < tile_count[:, None], index, -1)


def pair_of_tiles(index_ref, vals_ref, row, step_row, pair):
    first = index_ref[row, 2 * pair]
    second = index_ref[row, 2 * pair + 1]
    left = vals_ref[step_row, 2 * pair]
    right = vals_ref[step_row, 2 * pair + 1]
    right = jnp.where(second >= 0, right, jnp.zeros_like(right))
    return first, second, jnp.concatenate([left, right], axis=1)


def gather_kernel(rows_per_step, index_ref, vals_ref, *refs):
    pieces = refs[:SPAN]
    out_ref, window, total, sems = refs[SPAN:]
    panel_blocks = pieces[0].shape[0]

    @pl.when(pl.program_id(0) == 0)
    def _():
        copies = [
            pltpu.make_async_copy(
                pieces[p], window.at[pl.ds(p * panel_blocks, panel_blocks)], sems.at[p]
            )
            for p in range(SPAN)
        ]
        for copy in copies:
            copy.start()
        for copy in copies:
            copy.wait()

    for step_row in range(rows_per_step):
        row = pl.program_id(0) * rows_per_step + step_row

        def product(pair):
            first, second, lhs = pair_of_tiles(index_ref, vals_ref, row, step_row, pair)
            rhs = jnp.concatenate([window[first], window[jnp.maximum(second, 0)]], axis=0)
            return jnp.dot(lhs, rhs, preferred_element_type=jnp.float32)

        total[step_row] = product(0)
        for pair in range(1, SLOTS // 2):

            @pl.when(index_ref[row, 2 * pair] >= 0)
            def _():
                total[step_row] += product(pair)

        out_ref[step_row] = total[step_row].astype(out_ref.dtype)


def sparse_gather(index, vals, pieces):
    rows, slots = index.shape
    width = pieces[0].shape[-1]
    rows_per_step = 4
    return pl.pallas_call(
        functools.partial(gather_kernel, rows_per_step),
        grid=(rows // rows_per_step,),
        in_specs=[
            pl.BlockSpec(memory_space=pltpu.SMEM),
            pl.BlockSpec((rows_per_step, slots, TILE, TILE), lambda g: (g, 0, 0, 0)),
        ]
        + [pl.BlockSpec(memory_space=pl.ANY)] * SPAN,
        out_specs=pl.BlockSpec((rows_per_step, TILE, width), lambda g: (g, 0, 0)),
        out_shape=jax.ShapeDtypeStruct((rows, TILE, width), jnp.bfloat16),
        scratch_shapes=[
            pltpu.VMEM((SPAN * pieces[0].shape[0], TILE, width), jnp.bfloat16),
            pltpu.VMEM((rows_per_step, TILE, width), jnp.float32),
            pltpu.SemaphoreType.DMA((SPAN,)),
        ],
        compiler_params=pltpu.CompilerParams(vmem_limit_bytes=VMEM_LIMIT),
        cost_estimate=pl.CostEstimate(
            flops=rows * slots * TILE * TILE * width * 2,
            bytes_accessed=rows * slots * TILE * TILE * 2 + (SPAN + 1) * rows * TILE * width * 2,
            transcendentals=0,
        ),
    )(index, vals, *pieces)


def scatter_kernel(rows_per_step, index_ref, vals_ref, back_ref, *refs):
    outs = refs[:SPAN]
    total = refs[SPAN]
    panel_blocks = outs[0].shape[0]
    step = pl.program_id(0)

    @pl.when(step == 0)
    def _():
        total[...] = jnp.zeros_like(total)

    for step_row in range(rows_per_step):
        row = step * rows_per_step + step_row
        turned = back_ref[step_row].T
        for pair in range(SLOTS // 2):

            def add():
                first, second, rhs = pair_of_tiles(index_ref, vals_ref, row, step_row, pair)
                part = jnp.dot(turned, rhs, preferred_element_type=jnp.float32)
                total[first] += part[:, :TILE]
                total[jnp.maximum(second, 0)] += part[:, TILE:]

            if pair == 0:
                add()
            else:
                pl.when(index_ref[row, 2 * pair] >= 0)(add)

    @pl.when(step == pl.num_programs(0) - 1)
    def _():
        for p in range(SPAN):
            outs[p][...] = total[pl.ds(p * panel_blocks, panel_blocks)].astype(outs[p].dtype)


def sparse_scatter(index, vals, back):
    rows, slots = index.shape
    width = back.shape[-1]
    rows_per_step = 4
    kinds = [jnp.float32 if p == REACH else jnp.bfloat16 for p in range(SPAN)]
    return pl.pallas_call(
        functools.partial(scatter_kernel, rows_per_step),
        grid=(rows // rows_per_step,),
        in_specs=[
            pl.BlockSpec(memory_space=pltpu.SMEM),
            pl.BlockSpec((rows_per_step, slots, TILE, TILE), lambda g: (g, 0, 0, 0)),
            pl.BlockSpec((rows_per_step, TILE, width), lambda g: (g, 0, 0)),
        ],
        out_specs=[pl.BlockSpec((rows, width, TILE), lambda g: (0, 0, 0))] * SPAN,
        out_shape=[jax.ShapeDtypeStruct((rows, width, TILE), kind) for kind in kinds],
        scratch_shapes=[pltpu.VMEM((SPAN * rows, width, TILE), jnp.float32)],
        compiler_params=pltpu.CompilerParams(vmem_limit_bytes=VMEM_LIMIT),
        cost_estimate=pl.CostEstimate(
            flops=rows * slots * TILE * TILE * width * 2,
            bytes_accessed=rows * slots * TILE * TILE * 2 + (SPAN + 2) * rows * TILE * width * 2,
            transcendentals=0,
        ),
    )(index, vals, back)


def local(feats, weight, tile_vals, tile_cols, tile_count, cotangent):
    node_rows, feat_width = feats.shape
    cycle_size = lax.axis_size("blk")
    group_size = lax.axis_size("repl")
    panel_size = node_rows * group_size
    panel_blocks = panel_size // TILE
    block_rows = node_rows // TILE
    width = feat_width // group_size
    center = lax.axis_index("blk")

    own_index = window_index(tile_cols, tile_count, center, panel_blocks, cycle_size)
    index = lax.all_gather(own_index, "repl", axis=0, tiled=True)
    vals = lax.all_gather(tile_vals, "repl", axis=0, tiled=True)

    own_panel = lax.all_to_all(feats, "repl", split_axis=1, concat_axis=0, tiled=True)
    own_panel = own_panel.reshape(panel_blocks, TILE, width)
    pieces = [
        own_panel if offset == 0 else passed_along(own_panel, "blk", -offset)
        for offset in range(-REACH, REACH + 1)
    ]
    columns = sparse_gather(index, vals, pieces).reshape(panel_size, width)
    aggregate = lax.all_to_all(columns, "repl", split_axis=0, concat_axis=1, tiled=True)

    preact = jnp.dot(aggregate, weight, preferred_element_type=jnp.float32)
    output = jax.nn.silu(preact).astype(jnp.bfloat16)
    slope = (cotangent.astype(jnp.float32) * silu_slope(preact)).astype(jnp.bfloat16)
    backward = jnp.einsum("nf,gf->ng", slope, weight, preferred_element_type=jnp.float32).astype(
        jnp.bfloat16
    )
    nodes_total = panel_size * cycle_size
    weight_term = jnp.einsum("nf,ng->fg", aggregate, slope, preferred_element_type=jnp.float32)
    weight_grad = lax.psum(weight_term.astype(jnp.bfloat16), ("blk", "repl")).astype(
        jnp.float32
    ) * (1.0 / math.sqrt(nodes_total))

    back = lax.all_to_all(backward, "repl", split_axis=1, concat_axis=0, tiled=True)
    shares = sparse_scatter(index, vals, back.reshape(panel_blocks, TILE, width))
    total = shares[REACH]
    for offset in range(-REACH, REACH + 1):
        if offset != 0:
            total = total + passed_along(shares[offset + REACH], "blk", offset).astype(jnp.float32)
    owned = lax.all_to_all(
        total.astype(jnp.bfloat16).reshape(group_size, block_rows, width, TILE),
        "repl",
        split_axis=0,
        concat_axis=0,
        tiled=True,
    )
    grad_rows = jnp.transpose(owned, (1, 3, 0, 2)).reshape(node_rows, feat_width)
    return (output, weight_grad, grad_rows)


def solution(mesh):
    in_specs = (
        P(("blk", "repl"), None),
        P(),
        P(("blk", "repl"), None, None, None),
        P(("blk", "repl"), None),
        P(("blk", "repl")),
        P(("blk", "repl"), None),
    )
    out_specs = (P(("blk", "repl"), None), P(), P(("blk", "repl"), None))
    return jax.shard_map(local, mesh=mesh, in_specs=in_specs, out_specs=out_specs, check_vma=False)
```

```python
import functools
import math

import jax
import jax.numpy as jnp
from jax import lax
from jax.experimental import pallas as pl
from jax.experimental.pallas import tpu as pltpu
from jax.sharding import PartitionSpec as P

TILE = 128
REACH = 2
SPAN = 2 * REACH + 1
VMEM_LIMIT = 48 * 1024 * 1024
PARAMS = pltpu.CompilerParams(vmem_limit_bytes=VMEM_LIMIT)
BF16 = jnp.bfloat16
F32 = jnp.float32


def passed_along(value, axis, steps):
    count = lax.axis_size(axis)
    pairs = [(source, (source + steps) % count) for source in range(count)]
    return lax.ppermute(value, axis, pairs)


def swapped(value, axis, mask):
    count = lax.axis_size(axis)
    return lax.ppermute(value, axis, [(source, source ^ mask) for source in range(count)])


def spec_any():
    return pl.BlockSpec(memory_space=pl.ANY)


def spec_smem():
    return pl.BlockSpec(memory_space=pltpu.SMEM)


def cost(flops, bytes_accessed):
    return pl.CostEstimate(flops=flops, bytes_accessed=bytes_accessed, transcendentals=0)


def split_kernel(rank_ref, *refs):
    count = len(refs) // 2
    for d in range(count):
        refs[count + d][...] = refs[d][...]


def split_columns(rank, feats, group):
    rows, columns = feats.shape
    width = columns // group

    def column_of(d):
        return lambda g, rank_ref: (0, rank_ref[0] ^ d)

    return pl.pallas_call(
        split_kernel,
        grid_spec=pltpu.PrefetchScalarGridSpec(
            num_scalar_prefetch=1,
            grid=(1,),
            in_specs=[pl.BlockSpec((rows, width), column_of(d)) for d in range(group)],
            out_specs=[pl.BlockSpec((rows, width), lambda g, rank_ref: (0, 0))] * group,
        ),
        out_shape=[jax.ShapeDtypeStruct((rows, width), feats.dtype)] * group,
        compiler_params=PARAMS,
        cost_estimate=cost(0, 2 * rows * columns * 2),
    )(rank, *([feats] * group))


def gather_kernel(parts, base, index_ref, *refs):
    count = len(base)
    vals = refs[:count]
    pieces = refs[count : count + parts * SPAN]
    outs = refs[count + parts * SPAN : 2 * count + parts * SPAN]
    window, sems = refs[2 * count + parts * SPAN :]
    size = pieces[0].shape[0]
    step = pl.program_id(0)
    slots = vals[0].shape[1]

    @pl.when(step == 0)
    def _():
        copies = [
            pltpu.make_async_copy(pieces[n], window.at[pl.ds(n * size, size)], sems.at[n])
            for n in range(parts * SPAN)
        ]
        for copy in copies:
            copy.start()
        window[parts * SPAN * size] = jnp.zeros(window.shape[1:], window.dtype)
        for copy in copies:
            copy.wait()

    for m in range(count):
        row = base[m] + step
        lhs = jnp.concatenate([vals[m][0, s] for s in range(slots)], axis=1)
        rhs = jnp.concatenate([window[index_ref[row, s]] for s in range(slots)], axis=0)
        outs[m][0] = jnp.dot(lhs, rhs, preferred_element_type=F32).astype(BF16)


def sparse_gather(index, members, vals, pieces, parts):
    block_rows, slots = vals[0].shape[:2]
    size, _, width = pieces[0].shape
    count = len(members)
    body = functools.partial(gather_kernel, parts, [m * block_rows for m in members])
    return pl.pallas_call(
        body,
        grid=(block_rows,),
        in_specs=[spec_smem()]
        + [pl.BlockSpec((1, slots, TILE, TILE), lambda g: (g, 0, 0, 0))] * count
        + [spec_any()] * (parts * SPAN),
        out_specs=[pl.BlockSpec((1, TILE, width), lambda g: (g, 0, 0))] * count,
        out_shape=[jax.ShapeDtypeStruct((block_rows, TILE, width), BF16)] * count,
        scratch_shapes=[
            pltpu.VMEM((SPAN * parts * size + 1, TILE, width), BF16),
            pltpu.SemaphoreType.DMA((SPAN * parts,)),
        ],
        compiler_params=PARAMS,
        cost_estimate=cost(
            count * block_rows * slots * TILE * TILE * width * 2,
            count * block_rows * slots * TILE * TILE * 2 + SPAN * parts * size * TILE * width * 2,
        ),
    )(index, *vals, *pieces)


def dense_kernel(group, rank_ref, *refs):
    parts = refs[:group]
    weights = refs[group : 2 * group]
    turned = refs[2 * group : 3 * group]
    cotangent_ref = refs[3 * group]
    output_ref, slope_ref = refs[3 * group + 1 : 3 * group + 3]
    backs = refs[3 * group + 3 :]
    blocks, tile, width = parts[0].shape
    rows = blocks * tile
    aggregate = jnp.concatenate([p[...].reshape(rows, width) for p in parts], axis=1)
    weight = jnp.concatenate([w[...] for w in weights], axis=0)
    preact = jnp.dot(aggregate, weight, preferred_element_type=F32)
    sigma = jax.nn.sigmoid(preact)
    output_ref[...] = (preact * sigma).astype(BF16)
    slope = sigma * (1.0 + preact * (1.0 - sigma))
    slope = (cotangent_ref[...].astype(F32) * slope).astype(BF16)
    slope_ref[...] = slope
    turned_weight = jnp.concatenate([t[...] for t in turned], axis=1)
    backward = jnp.dot(slope, turned_weight, preferred_element_type=F32).astype(BF16)
    for d in range(group):
        backs[d][...] = backward[:, d * width : (d + 1) * width].reshape(blocks, tile, width)


def dense(rank, parts, weight, turned, cotangent):
    group = len(parts)
    block_rows, _, width = parts[0].shape
    node_rows, feat_out = cotangent.shape
    feat_in = weight.shape[0]
    steps = 2
    blocks = block_rows // steps
    rows = node_rows // steps

    def weight_of(d):
        return lambda g, rank_ref: (rank_ref[0] ^ d, 0)

    def turned_of(d):
        return lambda g, rank_ref: (0, rank_ref[0] ^ d)

    part_spec = pl.BlockSpec((blocks, TILE, width), lambda g, rank_ref: (g, 0, 0))
    row_spec = pl.BlockSpec((rows, feat_out), lambda g, rank_ref: (g, 0))
    return pl.pallas_call(
        functools.partial(dense_kernel, group),
        grid_spec=pltpu.PrefetchScalarGridSpec(
            num_scalar_prefetch=1,
            grid=(steps,),
            in_specs=[part_spec] * group
            + [pl.BlockSpec((width, feat_out), weight_of(d)) for d in range(group)]
            + [pl.BlockSpec((feat_out, width), turned_of(d)) for d in range(group)]
            + [row_spec],
            out_specs=[row_spec, row_spec] + [part_spec] * group,
        ),
        out_shape=[jax.ShapeDtypeStruct((node_rows, feat_out), BF16)] * 2
        + [jax.ShapeDtypeStruct((block_rows, TILE, width), BF16)] * group,
        compiler_params=PARAMS,
        cost_estimate=cost(
            4 * node_rows * feat_in * feat_out,
            2 * (5 * node_rows * feat_out + 2 * feat_in * feat_out),
        ),
    )(rank, *parts, *([weight] * group), *([turned] * group), cotangent)


def term_kernel(group, *refs):
    slope = refs[group][...]
    for d in range(group):
        part = refs[d][...].reshape(slope.shape[0], -1)
        term = lax.dot_general(part, slope, (((0,), (0,)), ((), ())), preferred_element_type=F32)
        refs[group + 1 + d][...] = term.astype(BF16)


def weight_terms(parts, slope):
    group = len(parts)
    width = parts[0].shape[-1]
    node_rows, feat_out = slope.shape
    return pl.pallas_call(
        functools.partial(term_kernel, group),
        out_shape=[jax.ShapeDtypeStruct((width, feat_out), BF16)] * group,
        compiler_params=PARAMS,
        cost_estimate=cost(
            2 * node_rows * width * group * feat_out, 2 * 3 * node_rows * feat_out
        ),
    )(*parts, slope)


def scatter_kernel(parts, index_ref, *refs):
    group = (len(refs) - 1 - parts * SPAN) // 2
    vals = refs[:group]
    backs = refs[group : 2 * group]
    outs = refs[2 * group : 2 * group + parts * SPAN]
    total = refs[-1]
    size = outs[0].shape[0]
    step = pl.program_id(0)
    slots = vals[0].shape[1]

    @pl.when(step == 0)
    def _():
        total[...] = jnp.zeros_like(total)

    for m in range(group):
        row = m * pl.num_programs(0) + step
        turned = backs[m][0].T
        for s in range(0, slots, 2):
            rhs = jnp.concatenate([vals[m][0, s], vals[m][0, s + 1]], axis=1)
            part = jnp.dot(turned, rhs, preferred_element_type=F32)
            total[index_ref[row, s]] += part[:, :TILE]
            total[index_ref[row, s + 1]] += part[:, TILE:]

    @pl.when(step == pl.num_programs(0) - 1)
    def _():
        for n in range(parts * SPAN):
            outs[n][...] = total[pl.ds(n * size, size)].astype(outs[n].dtype)


def sparse_scatter(index, vals, backs, parts):
    group = len(vals)
    block_rows, slots = vals[0].shape[:2]
    width = backs[0].shape[-1]
    size = group * block_rows // parts
    kinds = [F32 if n // parts == REACH else BF16 for n in range(parts * SPAN)]
    return pl.pallas_call(
        functools.partial(scatter_kernel, parts),
        grid=(block_rows,),
        in_specs=[spec_smem()]
        + [pl.BlockSpec((1, slots, TILE, TILE), lambda g: (g, 0, 0, 0))] * group
        + [pl.BlockSpec((1, TILE, width), lambda g: (g, 0, 0))] * group,
        out_specs=[pl.BlockSpec((size, width, TILE), lambda g: (0, 0, 0))] * (parts * SPAN),
        out_shape=[jax.ShapeDtypeStruct((size, width, TILE), kind) for kind in kinds],
        scratch_shapes=[pltpu.VMEM((SPAN * parts * size + 1, width, TILE), F32)],
        compiler_params=PARAMS,
        cost_estimate=cost(
            group * block_rows * slots * TILE * TILE * width * 2,
            group * block_rows * slots * TILE * TILE * 2 + 6 * parts * size * TILE * width * 2,
        ),
    )(index, *vals, *backs)


def sum_kernel(own_ref, *refs):
    outs = refs[SPAN - 1 :]
    size = outs[0].shape[0]
    for n in range(len(outs)):
        rows = pl.ds(n * size, size)
        total = own_ref[rows]
        for ref in refs[: SPAN - 1]:
            total += ref[rows].astype(F32)
        outs[n][...] = total.astype(BF16)


def summed(own, arrived, count):
    size, width, tile = own.shape
    return pl.pallas_call(
        sum_kernel,
        out_shape=[jax.ShapeDtypeStruct((size // count, width, tile), BF16)] * count,
        compiler_params=PARAMS,
        cost_estimate=cost(0, size * width * tile * 14),
    )(own, *arrived)


def place_kernel(rank_ref, *refs):
    out_ref = refs[-1]
    for d, ref in enumerate(refs[:-1]):
        blocks, width, tile = ref.shape
        start = pl.multiple_of((rank_ref[0] ^ d) * width, width)
        for b in range(blocks):
            out_ref[pl.ds(b * tile, tile), pl.ds(start, width)] = ref[b].T


def placed(rank, parts):
    blocks, width, tile = parts[0].shape
    shape = (blocks * tile, width * len(parts))
    return pl.pallas_call(
        place_kernel,
        in_specs=[spec_smem()] + [pl.BlockSpec(memory_space=pltpu.VMEM)] * len(parts),
        out_shape=jax.ShapeDtypeStruct(shape, BF16),
        compiler_params=PARAMS,
        cost_estimate=cost(0, 2 * 2 * shape[0] * shape[1]),
    )(rank, *parts)


def local(feats, weight, tile_vals, tile_cols, tile_count, cotangent):
    node_rows, feat_width = feats.shape
    cycle = lax.axis_size("blk")
    group = lax.axis_size("repl")
    assert group & (group - 1) == 0 and cycle & (cycle - 1) == 0
    block_rows = node_rows // TILE
    panel_blocks = block_rows * group
    width = feat_width // group
    parts = 2
    member = group // parts
    center = lax.axis_index("blk")
    rank = lax.axis_index("repl")
    rank_array = jnp.reshape(rank, (1,)).astype(jnp.int32)

    sent = split_columns(rank_array, feats, group)
    mine = [sent[0]] + [swapped(sent[d], "repl", d) for d in range(1, group)]
    halves = [
        jnp.concatenate(mine[h * member : (h + 1) * member], axis=0).reshape(
            member * block_rows, TILE, width
        )
        for h in range(parts)
    ]

    offset = (tile_cols // panel_blocks - center) % cycle
    offset = jnp.where(offset > REACH, offset - cycle, offset)
    slot_ids = jnp.arange(tile_cols.shape[1], dtype=jnp.int32)
    own_index = jnp.where(
        slot_ids[None, :] < tile_count[:, None],
        (offset + REACH) * panel_blocks + tile_cols % panel_blocks,
        SPAN * panel_blocks,
    )
    index = jnp.concatenate(
        [own_index] + [swapped(own_index, "repl", d) for d in range(1, group)], axis=0
    )
    index = jnp.where(index < SPAN * panel_blocks, index ^ (rank * block_rows), index)
    vals = [tile_vals]
    mask = group // 2
    held = {0: tile_vals}
    while mask:
        for d in sorted(held):
            held[d | mask] = swapped(held[d], "repl", mask)
        mask //= 2
    vals = [held[d] for d in range(group)]

    offsets = range(-REACH, REACH + 1)
    window = {}
    for h in range(parts):
        for o in offsets:
            window[o, h] = halves[h] if o == 0 else passed_along(halves[h], "blk", -o)
    pieces = [window[o, h] for o in offsets for h in range(parts)]

    columns = [None] * group
    for h in reversed(range(parts)):
        members = list(range(h * member, (h + 1) * member))
        made = sparse_gather(index, members, [vals[d] for d in members], pieces, parts)
        for d, value in zip(members, made):
            columns[d] = value
    aggregate = [columns[0]] + [swapped(columns[d], "repl", d) for d in range(1, group)]

    made = dense(rank_array, aggregate, weight, weight.T, cotangent)
    output, slope, backs = made[0], made[1], made[2:]
    backs = [backs[0]] + [swapped(backs[d], "repl", d) for d in range(1, group)]

    terms = weight_terms(aggregate, slope)
    chunk = terms[0].astype(F32)
    for d in range(1, group):
        chunk = chunk + swapped(terms[d], "repl", d).astype(F32)
    mask = 1
    while mask < cycle:
        rounded = lax.optimization_barrier(chunk.astype(BF16))
        chunk = rounded.astype(F32) + swapped(rounded, "blk", mask).astype(F32)
        mask *= 2
    chunk = chunk.astype(BF16)
    chunks = [chunk] + [swapped(chunk, "repl", d) for d in range(1, group)]
    scale = 1.0 / math.sqrt(node_rows * group * cycle)
    weight_grad = jnp.concatenate(chunks, axis=0).astype(F32) * scale
    weight_grad = weight_grad.reshape(group, width, -1)[jnp.arange(group) ^ rank]
    weight_grad = weight_grad.reshape(feat_width, -1)

    shares = sparse_scatter(index, vals, backs, parts)
    owned = [None] * group
    for h in reversed(range(parts)):
        arrived = [
            passed_along(shares[(o + REACH) * parts + h], "blk", o) for o in offsets if o != 0
        ]
        made = summed(shares[REACH * parts + h], arrived, member)
        for n, value in enumerate(made):
            d = h * member + n
            owned[d] = value if d == 0 else swapped(value, "repl", d)
    grad_rows = placed(rank_array, owned)
    return (output, weight_grad, grad_rows)


def solution(mesh):
    in_specs = (
        P(("blk", "repl"), None),
        P(),
        P(("blk", "repl"), None, None, None),
        P(("blk", "repl"), None),
        P(("blk", "repl")),
        P(("blk", "repl"), None),
    )
    out_specs = (P(("blk", "repl"), None), P(), P(("blk", "repl"), None))
    return jax.shard_map(local, mesh=mesh, in_specs=in_specs, out_specs=out_specs, check_vma=False)
```

```python
import functools
import math

import jax
import jax.numpy as jnp
from jax import lax
from jax.experimental import pallas as pl
from jax.experimental.pallas import tpu as pltpu
from jax.sharding import PartitionSpec as P

TILE = 128
REACH = 2
SPAN = 2 * REACH + 1
VMEM_LIMIT = 32 * 1024 * 1024
PARAMS = pltpu.CompilerParams(vmem_limit_bytes=VMEM_LIMIT)
EXTRA = 16
BF16 = jnp.bfloat16
F32 = jnp.float32


def mirrored(value, steps):
    count = lax.axis_size("blk")
    pairs = [(k, (k + steps * (1 - 2 * (k & 1))) % count) for k in range(count)]
    return lax.ppermute(value, "blk", pairs)


def after(value, *others):
    return lax.optimization_barrier((value, *others))[0]


def swapped(value, axis, mask):
    count = lax.axis_size(axis)
    return lax.ppermute(value, axis, [(source, source ^ mask) for source in range(count)])


def spec_smem():
    return pl.BlockSpec(memory_space=pltpu.SMEM)


def spec_vmem():
    return pl.BlockSpec(memory_space=pltpu.VMEM)


def cost(flops, bytes_accessed):
    return pl.CostEstimate(flops=flops, bytes_accessed=bytes_accessed, transcendentals=0)


def split_kernel(panel_blocks, cycle, cols_ref, count_ref, feats_ref, *refs):
    *outs, place_ref = refs
    rows, width = feats_ref.shape[0], outs[0].shape[1]
    block_rows, slots = cols_ref.shape
    rank = lax.axis_index("repl")
    center = lax.axis_index("blk")
    sign = 1 - 2 * (center & 1)
    cols = cols_ref[...]
    offset = (cols // panel_blocks - center) & (cycle - 1)
    offset = jnp.where(offset > REACH, offset - cycle, offset) * sign
    place = (offset + REACH) * panel_blocks + (cols & (panel_blocks - 1))
    row = lax.broadcasted_iota(jnp.int32, cols.shape, 0)
    slot = lax.broadcasted_iota(jnp.int32, cols.shape, 1)
    live = jnp.zeros(cols.shape, jnp.int32)
    for r in range(block_rows):
        live = jnp.where(row == r, count_ref[r], live)
    place = jnp.where(slot < live, place, SPAN * panel_blocks)
    place_ref[...] = jnp.zeros_like(place_ref)
    place_ref[pl.ds(0, block_rows), pl.ds(0, slots)] = place.astype(F32)
    for d, out_ref in enumerate(outs):
        start = pl.multiple_of((rank ^ d) * width, width)
        out_ref[pl.ds(0, rows), :] = feats_ref[:, pl.ds(start, width)]
        out_ref[pl.ds(rows, EXTRA), :] = place_ref[...].astype(BF16)


def split_columns(feats, tile_cols, tile_count, panel_blocks, cycle, group):
    rows, columns = feats.shape
    width = columns // group
    return pl.pallas_call(
        functools.partial(split_kernel, panel_blocks, cycle),
        in_specs=[spec_vmem(), spec_smem(), spec_vmem()],
        out_shape=[jax.ShapeDtypeStruct((rows + EXTRA, width), feats.dtype)] * group,
        scratch_shapes=[pltpu.VMEM((EXTRA, width), F32)],
        compiler_params=PARAMS,
        cost_estimate=cost(0, 2 * rows * columns * 2),
    )(tile_cols, tile_count, feats)


def join_kernel(block_rows, *refs):
    *pieces, panel_ref, index_ref = refs
    group = len(pieces)
    rows = panel_ref.shape[0] // group
    rank = lax.axis_index("repl")
    spare = SPAN * group * block_rows
    for d, piece in enumerate(pieces):
        panel_ref[pl.ds(d * rows, rows), :] = piece[pl.ds(0, rows), :]
        place = piece[pl.ds(rows, EXTRA), :].astype(F32).astype(jnp.int32)[:block_rows]
        place = jnp.where(place < spare, place ^ (rank * block_rows), place)
        index_ref[pl.ds(d * block_rows, block_rows), :] = place


def joined_panel(pieces, block_rows):
    rows, width = pieces[0].shape
    group = len(pieces)
    return pl.pallas_call(
        functools.partial(join_kernel, block_rows),
        out_shape=[
            jax.ShapeDtypeStruct((group * (rows - EXTRA), width), BF16),
            jax.ShapeDtypeStruct((group * block_rows, width), jnp.int32),
        ],
        compiler_params=PARAMS,
        cost_estimate=cost(0, 4 * group * rows * width),
    )(*pieces)


def gather_kernel(group, index_ref, *refs):
    window, sems = refs[-2:]
    outs = refs[-2 - group : -2]
    pieces = refs[-2 - group - SPAN : -2 - group]
    vals = refs[: -2 - group - SPAN]
    size = pieces[0].shape[0]
    copies = [
        pltpu.make_async_copy(pieces[n], window.at[pl.ds(n * size, size)], sems.at[n])
        for n in range(SPAN)
    ]
    for copy in copies:
        copy.start()
    window[SPAN * size] = jnp.zeros(window.shape[1:], window.dtype)
    for copy in copies:
        copy.wait()
    block_rows = outs[0].shape[0]
    part = vals[-1].shape[0]

    @pl.loop(0, part)
    def _(i):
        row = 0
        for val in vals:
            for b in range(0, val.shape[0], part):
                slots = range(val.shape[1])
                lhs = jnp.concatenate([val[b + i, s] for s in slots], axis=1)
                rhs = jnp.concatenate([window[index_ref[row + i, s]] for s in slots], axis=0)
                made = jnp.dot(lhs, rhs, preferred_element_type=F32).astype(BF16)
                outs[row // block_rows][row % block_rows + i] = made
                row += part


def sparse_gather(index, vals, pieces, group):
    rows = sum(val.shape[0] for val in vals)
    slots = vals[0].shape[1]
    size, _, width = pieces[0].shape
    return pl.pallas_call(
        functools.partial(gather_kernel, group),
        in_specs=[spec_smem()]
        + [spec_vmem()] * len(vals)
        + [pl.BlockSpec(memory_space=pltpu.HBM)] * SPAN,
        out_shape=[jax.ShapeDtypeStruct((rows // group, TILE, width), BF16)] * group,
        scratch_shapes=[
            pltpu.VMEM((SPAN * size + 1, TILE, width), BF16),
            pltpu.SemaphoreType.DMA((SPAN,)),
        ],
        compiler_params=PARAMS,
        cost_estimate=cost(
            rows * slots * TILE * TILE * width * 2,
            rows * slots * TILE * TILE * 2 + SPAN * size * TILE * width * 2,
        ),
    )(index, *vals, *pieces)


def dense_kernel(group, rank_ref, *refs):
    parts = refs[:group]
    weights = refs[group : 2 * group]
    turned = refs[2 * group : 3 * group]
    cotangent_ref = refs[3 * group]
    output_ref, slope_ref = refs[3 * group + 1 : 3 * group + 3]
    backs = refs[3 * group + 3 :]
    blocks, tile, width = parts[0].shape
    rows = blocks * tile
    aggregate = jnp.concatenate([p[...].reshape(rows, width) for p in parts], axis=1)
    weight = jnp.concatenate([w[...] for w in weights], axis=0)
    preact = jnp.dot(aggregate, weight, preferred_element_type=F32)
    sigma = jax.nn.sigmoid(preact)
    output_ref[...] = (preact * sigma).astype(BF16)
    slope = sigma * (1.0 + preact * (1.0 - sigma))
    slope = (cotangent_ref[...].astype(F32) * slope).astype(BF16)
    slope_ref[...] = slope
    turned_weight = jnp.concatenate([t[...] for t in turned], axis=1)
    backward = jnp.dot(slope, turned_weight, preferred_element_type=F32).astype(BF16)
    for d in range(group):
        backs[d][...] = backward[:, d * width : (d + 1) * width].reshape(blocks, tile, width)


def dense(where, parts, weight, turned, cotangent):
    group = len(parts)
    block_rows, _, width = parts[0].shape
    node_rows, feat_out = cotangent.shape
    feat_in = weight.shape[0]
    steps = 2
    blocks = block_rows // steps
    rows = node_rows // steps

    def weight_of(d):
        return lambda g, rank_ref: (rank_ref[0] ^ d, 0)

    def turned_of(d):
        return lambda g, rank_ref: (0, rank_ref[0] ^ d)

    part_spec = pl.BlockSpec((blocks, TILE, width), lambda g, rank_ref: (g, 0, 0))
    row_spec = pl.BlockSpec((rows, feat_out), lambda g, rank_ref: (g, 0))
    return pl.pallas_call(
        functools.partial(dense_kernel, group),
        grid_spec=pltpu.PrefetchScalarGridSpec(
            num_scalar_prefetch=1,
            grid=(steps,),
            in_specs=[part_spec] * group
            + [pl.BlockSpec((width, feat_out), weight_of(d)) for d in range(group)]
            + [pl.BlockSpec((feat_out, width), turned_of(d)) for d in range(group)]
            + [row_spec],
            out_specs=[row_spec, row_spec] + [part_spec] * group,
        ),
        out_shape=[jax.ShapeDtypeStruct((node_rows, feat_out), BF16)] * 2
        + [jax.ShapeDtypeStruct((block_rows, TILE, width), BF16)] * group,
        compiler_params=PARAMS,
        cost_estimate=cost(
            4 * node_rows * feat_in * feat_out,
            2 * (5 * node_rows * feat_out + 2 * feat_in * feat_out),
        ),
    )(where, *parts, *([weight] * group), *([turned] * group), cotangent)


def term_kernel(group, *refs):
    slope = refs[group][...]
    for d in range(group):
        part = refs[d][...].reshape(slope.shape[0], -1)
        term = lax.dot_general(part, slope, (((0,), (0,)), ((), ())), preferred_element_type=F32)
        refs[group + 1 + d][...] = term.astype(BF16)


def weight_terms(parts, slope):
    group = len(parts)
    width = parts[0].shape[-1]
    node_rows, feat_out = slope.shape
    return pl.pallas_call(
        functools.partial(term_kernel, group),
        out_shape=[jax.ShapeDtypeStruct((width, feat_out), BF16)] * group,
        compiler_params=PARAMS,
        cost_estimate=cost(
            2 * node_rows * width * group * feat_out, 2 * 3 * node_rows * feat_out
        ),
    )(*parts, slope)


def scatter_kernel(group, index_ref, *refs):
    total = refs[-1]
    outs = refs[-1 - SPAN : -1]
    backs = refs[-1 - SPAN - group : -1 - SPAN]
    vals = refs[: -1 - SPAN - group]
    size = outs[0].shape[0]
    block_rows = backs[0].shape[0]
    part = vals[-1].shape[0]
    total[...] = jnp.zeros_like(total)

    @pl.loop(0, part)
    def _(i):
        row = 0
        for val in vals:
            for b in range(0, val.shape[0], part):
                turned = backs[row // block_rows][row % block_rows + i].T
                for s in range(0, val.shape[1], 2):
                    rhs = jnp.concatenate([val[b + i, s], val[b + i, s + 1]], axis=1)
                    made = jnp.dot(turned, rhs, preferred_element_type=F32)
                    total[index_ref[row + i, s]] += made[:, :TILE]
                    total[index_ref[row + i, s + 1]] += made[:, TILE:]
                row += part

    for n in range(SPAN):
        outs[n][...] = total[pl.ds(n * size, size)].astype(BF16)


def sparse_scatter(index, vals, backs):
    group = len(backs)
    rows = sum(val.shape[0] for val in vals)
    slots = vals[0].shape[1]
    width = backs[0].shape[-1]
    return pl.pallas_call(
        functools.partial(scatter_kernel, group),
        in_specs=[spec_smem()] + [spec_vmem()] * (len(vals) + group),
        out_shape=[jax.ShapeDtypeStruct((rows, width, TILE), BF16)] * SPAN,
        scratch_shapes=[pltpu.VMEM((SPAN * rows + 1, width, TILE), F32)],
        compiler_params=PARAMS,
        cost_estimate=cost(
            rows * slots * TILE * TILE * width * 2,
            rows * slots * TILE * TILE * 2 + 6 * rows * TILE * width * 2,
        ),
    )(index, *vals, *backs)


def sum_kernel(count, *refs):
    outs = refs[count:]
    size = outs[0].shape[0]
    for n in range(len(outs)):
        rows = pl.ds(n * size, size)
        total = refs[0][rows].astype(F32)
        for ref in refs[1:count]:
            total += ref[rows].astype(F32)
        outs[n][...] = total.astype(BF16)


def summed(terms, count):
    size, width, tile = terms[0].shape
    return pl.pallas_call(
        functools.partial(sum_kernel, len(terms)),
        out_shape=[jax.ShapeDtypeStruct((size // count, width, tile), BF16)] * count,
        compiler_params=PARAMS,
        cost_estimate=cost(0, size * width * tile * 2 * (len(terms) + 1)),
    )(*terms)


def place_kernel(rank_ref, *refs):
    out_ref = refs[-1]
    for d, ref in enumerate(refs[:-1]):
        blocks, width, tile = ref.shape
        start = pl.multiple_of((rank_ref[0] ^ d) * width, width)
        for b in range(blocks):
            out_ref[pl.ds(b * tile, tile), pl.ds(start, width)] = ref[b].T


def placed(rank, parts):
    blocks, width, tile = parts[0].shape
    shape = (blocks * tile, width * len(parts))
    return pl.pallas_call(
        place_kernel,
        in_specs=[spec_smem()] + [spec_vmem()] * len(parts),
        out_shape=jax.ShapeDtypeStruct(shape, BF16),
        compiler_params=PARAMS,
        cost_estimate=cost(0, 2 * 2 * shape[0] * shape[1]),
    )(rank, *parts)


def rows_kernel(scale, rank_ref, *refs):
    out_ref = refs[-1]
    for d, ref in enumerate(refs[:-1]):
        size = ref.shape[0]
        start = pl.multiple_of((rank_ref[0] ^ d) * size, size)
        out_ref[pl.ds(start, size), :] = ref[...].astype(F32) * scale


def rows_placed(rank, parts, scale):
    size, columns = parts[0].shape
    return pl.pallas_call(
        functools.partial(rows_kernel, scale),
        in_specs=[spec_smem()] + [spec_vmem()] * len(parts),
        out_shape=jax.ShapeDtypeStruct((size * len(parts), columns), F32),
        compiler_params=PARAMS,
        cost_estimate=cost(0, 6 * size * len(parts) * columns),
    )(rank, *parts)


def local(feats, weight, tile_vals, tile_cols, tile_count, cotangent):
    node_rows = feats.shape[0]
    cycle = lax.axis_size("blk")
    group = lax.axis_size("repl")
    assert group & (group - 1) == 0 and cycle & (cycle - 1) == 0
    block_rows = node_rows // TILE
    panel_blocks = block_rows * group
    where = jnp.reshape(lax.axis_index("repl"), (1,)).astype(jnp.int32)

    sent = split_columns(feats, tile_cols, tile_count, panel_blocks, cycle, group)
    mine = [sent[0]] + [swapped(sent[d], "repl", d) for d in range(1, group)]
    panel, index = joined_panel(mine, block_rows)
    panel = panel.reshape(panel_blocks, TILE, -1)

    ahead = mirrored(panel, -2)
    beside = mirrored(panel, 1)
    half = block_rows // 2
    far_side = group // 2
    first, second = tile_vals[:half], tile_vals[half:]
    crossed_first = swapped(after(first, panel), "repl", far_side)
    near_vals = [tile_vals] + [
        swapped(after(tile_vals, panel), "repl", d) for d in range(1, far_side)
    ]
    behind = mirrored(after(panel, ahead), 2)
    relayed = mirrored(after(ahead, beside), 1)
    crossed_second = swapped(after(second, ahead, beside), "repl", far_side)
    crossed = [crossed_first, crossed_second]
    passed = [after(crossed_first, ahead, beside), crossed_second]
    far_vals = [crossed] + [
        [swapped(part, "repl", d) for part in passed] for d in range(1, far_side)
    ]
    vals = near_vals + [part for parts in far_vals for part in parts]
    columns = sparse_gather(index, vals, [behind, relayed, panel, beside, ahead], group)
    aggregate = [columns[0]] + [swapped(columns[d], "repl", d) for d in range(1, group)]

    made = dense(where, aggregate, weight, weight.T, cotangent)
    output, slope, backs = made[0], made[1], made[2:]
    backs = [backs[0]] + [swapped(backs[d], "repl", d) for d in range(1, group)]

    far, relay, own, near, joined = sparse_scatter(index, vals, backs)
    relay_in = mirrored(relay, 1)
    far_in = mirrored(far, -2)
    joined_in = mirrored(after(summed([joined, relay_in], 1)[0], far_in), 2)
    near_in = mirrored(after(near, relay_in), 1)

    terms = weight_terms(aggregate, after(slope, backs[1]))
    chunk = after(terms[0], own).astype(F32)
    for d in range(1, group):
        chunk = chunk + swapped(terms[d], "repl", d).astype(F32)
    mask = 1
    while mask < cycle:
        rounded = lax.optimization_barrier(chunk.astype(BF16))
        chunk = rounded.astype(F32) + swapped(rounded, "blk", mask).astype(F32)
        mask *= 2
    chunk = chunk.astype(BF16)
    chunks = [chunk] + [swapped(chunk, "repl", d) for d in range(1, group)]
    scale = 1.0 / math.sqrt(node_rows * group * cycle)
    weight_grad = rows_placed(where, chunks, scale)

    owned = summed([own, far_in, near_in, joined_in], group)
    owned = [owned[0]] + [swapped(owned[d], "repl", d) for d in range(1, group)]
    grad_rows = placed(where, owned)
    return (output, weight_grad, grad_rows)


def solution(mesh):
    in_specs = (
        P(("blk", "repl"), None),
        P(),
        P(("blk", "repl"), None, None, None),
        P(("blk", "repl"), None),
        P(("blk", "repl")),
        P(("blk", "repl"), None),
    )
    out_specs = (P(("blk", "repl"), None), P(), P(("blk", "repl"), None))
    return jax.shard_map(local, mesh=mesh, in_specs=in_specs, out_specs=out_specs, check_vma=False)
```

```python
import functools
import math

import jax
import jax.numpy as jnp
from jax import lax
from jax.experimental import pallas as pl
from jax.experimental.pallas import tpu as pltpu
from jax.sharding import PartitionSpec as P

TILE = 128
REACH = 2
SPAN = 2 * REACH + 1
VMEM_LIMIT = 32 * 1024 * 1024
PARAMS = pltpu.CompilerParams(vmem_limit_bytes=VMEM_LIMIT)
EXTRA = 16
BF16 = jnp.bfloat16
F32 = jnp.float32


def mirrored(value, steps):
    count = lax.axis_size("blk")
    pairs = [(k, (k + steps * (1 - 2 * (k & 1))) % count) for k in range(count)]
    return lax.ppermute(value, "blk", pairs)


def after(value, *others):
    return lax.optimization_barrier((value, *others))[0]


def swapped(value, axis, mask):
    count = lax.axis_size(axis)
    return lax.ppermute(value, axis, [(source, source ^ mask) for source in range(count)])


def spec_smem():
    return pl.BlockSpec(memory_space=pltpu.SMEM)


def spec_vmem():
    return pl.BlockSpec(memory_space=pltpu.VMEM)


def spec_hbm():
    return pl.BlockSpec(memory_space=pltpu.HBM)


def cost(flops, bytes_accessed):
    return pl.CostEstimate(flops=flops, bytes_accessed=bytes_accessed, transcendentals=0)


def split_kernel(panel_blocks, cycle, cols_hbm, count_hbm, feats_hbm, *refs):
    cols_ref, count_ref, place_ref, sems = refs[-4:]
    outs = refs[:-4]
    group = len(outs)
    rows, width = feats_hbm.shape[0], outs[0].shape[1]
    block_rows, slots = cols_ref.shape
    rank = lax.axis_index("repl")
    center = lax.axis_index("blk")
    small = [
        pltpu.make_async_copy(cols_hbm, cols_ref, sems.at[group]),
        pltpu.make_async_copy(count_hbm, count_ref, sems.at[group + 1]),
    ]
    large = []
    for d, out_ref in enumerate(outs):
        start = pl.multiple_of((rank ^ d) * width, width)
        large.append(
            pltpu.make_async_copy(
                feats_hbm.at[:, pl.ds(start, width)], out_ref.at[pl.ds(0, rows)], sems.at[d]
            )
        )
    for copy in small + large:
        copy.start()
    for copy in small:
        copy.wait()
    sign = 1 - 2 * (center & 1)
    cols = cols_ref[...]
    offset = (cols // panel_blocks - center) & (cycle - 1)
    offset = jnp.where(offset > REACH, offset - cycle, offset) * sign
    place = (offset + REACH) * panel_blocks + (cols & (panel_blocks - 1))
    row = lax.broadcasted_iota(jnp.int32, cols.shape, 0)
    slot = lax.broadcasted_iota(jnp.int32, cols.shape, 1)
    live = jnp.zeros(cols.shape, jnp.int32)
    for r in range(block_rows):
        live = jnp.where(row == r, count_ref[r], live)
    place = jnp.where(slot < live, place, SPAN * panel_blocks)
    place_ref[...] = jnp.zeros_like(place_ref)
    place_ref[pl.ds(0, block_rows), pl.ds(0, slots)] = place.astype(F32)
    for out_ref in outs:
        out_ref[pl.ds(rows, EXTRA), :] = place_ref[...].astype(BF16)
    for copy in large:
        copy.wait()


def split_columns(feats, tile_cols, tile_count, panel_blocks, cycle, group):
    rows, columns = feats.shape
    width = columns // group
    return pl.pallas_call(
        functools.partial(split_kernel, panel_blocks, cycle),
        in_specs=[spec_hbm()] * 3,
        out_shape=[jax.ShapeDtypeStruct((rows + EXTRA, width), feats.dtype)] * group,
        scratch_shapes=[
            pltpu.VMEM(tile_cols.shape, jnp.int32),
            pltpu.SMEM(tile_count.shape, jnp.int32),
            pltpu.VMEM((EXTRA, width), F32),
            pltpu.SemaphoreType.DMA((group + 2,)),
        ],
        compiler_params=PARAMS,
        cost_estimate=cost(0, 2 * rows * columns * 2),
    )(tile_cols, tile_count, feats)


def join_kernel(block_rows, *refs):
    *pieces, panel_ref, index_ref = refs
    group = len(pieces)
    rows = panel_ref.shape[0] // group
    rank = lax.axis_index("repl")
    spare = SPAN * group * block_rows
    for d, piece in enumerate(pieces):
        panel_ref[pl.ds(d * rows, rows), :] = piece[pl.ds(0, rows), :]
        place = piece[pl.ds(rows, EXTRA), :].astype(F32).astype(jnp.int32)[:block_rows]
        place = jnp.where(place < spare, place ^ (rank * block_rows), place)
        index_ref[pl.ds(d * block_rows, block_rows), :] = place


def joined_panel(pieces, block_rows):
    rows, width = pieces[0].shape
    group = len(pieces)
    return pl.pallas_call(
        functools.partial(join_kernel, block_rows),
        out_shape=[
            jax.ShapeDtypeStruct((group * (rows - EXTRA), width), BF16),
            jax.ShapeDtypeStruct((group * block_rows, width), jnp.int32),
        ],
        compiler_params=PARAMS,
        cost_estimate=cost(0, 4 * group * rows * width),
    )(*pieces)


def gather_kernel(group, index_ref, *refs):
    window, sems = refs[-2:]
    outs = refs[-2 - group : -2]
    pieces = refs[-2 - group - SPAN : -2 - group]
    vals = refs[: -2 - group - SPAN]
    size = pieces[0].shape[0]
    copies = [
        pltpu.make_async_copy(pieces[n], window.at[pl.ds(n * size, size)], sems.at[n])
        for n in range(SPAN)
    ]
    for copy in copies:
        copy.start()
    window[SPAN * size] = jnp.zeros(window.shape[1:], window.dtype)
    for copy in copies:
        copy.wait()
    block_rows = outs[0].shape[0]
    part = vals[-1].shape[0]

    @pl.loop(0, part)
    def _(i):
        row = 0
        for val in vals:
            for b in range(0, val.shape[0], part):
                slots = range(val.shape[1])
                lhs = jnp.concatenate([val[b + i, s] for s in slots], axis=1)
                rhs = jnp.concatenate([window[index_ref[row + i, s]] for s in slots], axis=0)
                made = jnp.dot(lhs, rhs, preferred_element_type=F32).astype(BF16)
                outs[row // block_rows][row % block_rows + i] = made
                row += part


def sparse_gather(index, vals, pieces, group):
    rows = sum(val.shape[0] for val in vals)
    slots = vals[0].shape[1]
    size, _, width = pieces[0].shape
    return pl.pallas_call(
        functools.partial(gather_kernel, group),
        in_specs=[spec_smem()]
        + [spec_vmem()] * len(vals)
        + [spec_hbm()] * SPAN,
        out_shape=[jax.ShapeDtypeStruct((rows // group, TILE, width), BF16)] * group,
        scratch_shapes=[
            pltpu.VMEM((SPAN * size + 1, TILE, width), BF16),
            pltpu.SemaphoreType.DMA((SPAN,)),
        ],
        compiler_params=PARAMS,
        cost_estimate=cost(
            rows * slots * TILE * TILE * width * 2,
            rows * slots * TILE * TILE * 2 + SPAN * size * TILE * width * 2,
        ),
    )(index, *vals, *pieces)


def prepare_kernel(group, weight_ref, rows_ref, turned_ref):
    width = weight_ref.shape[0] // group
    rank = lax.axis_index("repl")
    for d in range(group):
        start = pl.multiple_of((rank ^ d) * width, width)
        chunk = weight_ref[pl.ds(start, width), :]
        rows_ref[pl.ds(d * width, width), :] = chunk
        turned_ref[:, pl.ds(d * width, width)] = chunk.T


def prepared(weight, group):
    rows, columns = weight.shape
    return pl.pallas_call(
        functools.partial(prepare_kernel, group),
        in_specs=[spec_vmem()],
        out_shape=[
            jax.ShapeDtypeStruct((rows, columns), BF16),
            jax.ShapeDtypeStruct((columns, rows), BF16),
        ],
        compiler_params=PARAMS,
        cost_estimate=cost(0, 6 * rows * columns),
    )(weight)


def dense_kernel(group, *refs):
    parts = refs[:group]
    weight_ref, turned_ref, cotangent_ref, output_ref, slope_ref = refs[group : group + 5]
    backs = refs[group + 5 :]
    blocks, tile, width = parts[0].shape
    steps = 2
    blocks = blocks // steps
    rows = blocks * tile

    for g in range(steps):
        at = pl.ds(g * rows, rows)
        blocks_at = pl.ds(g * blocks, blocks)
        aggregate = jnp.concatenate([p[blocks_at].reshape(rows, width) for p in parts], axis=1)
        preact = jnp.dot(aggregate, weight_ref[...], preferred_element_type=F32)
        sigma = jax.nn.sigmoid(preact)
        output_ref[at, :] = (preact * sigma).astype(BF16)
        slope = sigma * (1.0 + preact * (1.0 - sigma))
        slope = (cotangent_ref[at, :].astype(F32) * slope).astype(BF16)
        slope_ref[at, :] = slope
        backward = jnp.dot(slope, turned_ref[...], preferred_element_type=F32).astype(BF16)
        for d in range(group):
            piece = backward[:, d * width : (d + 1) * width]
            backs[d][blocks_at] = piece.reshape(blocks, tile, width)


def dense(parts, weight, turned, cotangent):
    group = len(parts)
    node_rows, feat_out = cotangent.shape
    feat_in = weight.shape[0]
    return pl.pallas_call(
        functools.partial(dense_kernel, group),
        in_specs=[spec_vmem()] * (group + 3),
        out_shape=[jax.ShapeDtypeStruct((node_rows, feat_out), BF16)] * 2
        + [jax.ShapeDtypeStruct(parts[0].shape, BF16)] * group,
        compiler_params=PARAMS,
        cost_estimate=cost(
            4 * node_rows * feat_in * feat_out,
            2 * (5 * node_rows * feat_out + 2 * feat_in * feat_out),
        ),
    )(*parts, weight, turned, cotangent)


def term_kernel(group, *refs):
    slope = refs[group][...]
    for d in range(group):
        part = refs[d][...].reshape(slope.shape[0], -1)
        term = lax.dot_general(part, slope, (((0,), (0,)), ((), ())), preferred_element_type=F32)
        refs[group + 1 + d][...] = term.astype(BF16)


def weight_terms(parts, slope):
    group = len(parts)
    width = parts[0].shape[-1]
    node_rows, feat_out = slope.shape
    return pl.pallas_call(
        functools.partial(term_kernel, group),
        out_shape=[jax.ShapeDtypeStruct((width, feat_out), BF16)] * group,
        compiler_params=PARAMS,
        cost_estimate=cost(
            2 * node_rows * width * group * feat_out, 2 * 3 * node_rows * feat_out
        ),
    )(*parts, slope)


def scatter_kernel(group, index_ref, *refs):
    total = refs[-1]
    outs = refs[-1 - SPAN : -1]
    backs = refs[-1 - SPAN - group : -1 - SPAN]
    vals = refs[: -1 - SPAN - group]
    size = outs[0].shape[0]
    block_rows = backs[0].shape[0]
    part = vals[-1].shape[0]
    total[...] = jnp.zeros_like(total)

    @pl.loop(0, part)
    def _(i):
        row = 0
        for val in vals:
            for b in range(0, val.shape[0], part):
                turned = backs[row // block_rows][row % block_rows + i].T
                for s in range(0, val.shape[1], 2):
                    rhs = jnp.concatenate([val[b + i, s], val[b + i, s + 1]], axis=1)
                    made = jnp.dot(turned, rhs, preferred_element_type=F32)
                    total[index_ref[row + i, s]] += made[:, :TILE]
                    total[index_ref[row + i, s + 1]] += made[:, TILE:]
                row += part

    for n in range(SPAN):
        outs[n][...] = total[pl.ds(n * size, size)].astype(BF16)


def sparse_scatter(index, vals, backs):
    group = len(backs)
    rows = sum(val.shape[0] for val in vals)
    slots = vals[0].shape[1]
    width = backs[0].shape[-1]
    return pl.pallas_call(
        functools.partial(scatter_kernel, group),
        in_specs=[spec_smem()] + [spec_vmem()] * (len(vals) + group),
        out_shape=[jax.ShapeDtypeStruct((rows, width, TILE), BF16)] * SPAN,
        scratch_shapes=[pltpu.VMEM((SPAN * rows + 1, width, TILE), F32)],
        compiler_params=PARAMS,
        cost_estimate=cost(
            rows * slots * TILE * TILE * width * 2,
            rows * slots * TILE * TILE * 2 + 6 * rows * TILE * width * 2,
        ),
    )(index, *vals, *backs)


def sum_kernel(bases, size, *refs):
    terms = refs[: len(bases)]
    for n, out_ref in enumerate(refs[len(bases) :]):
        total = jnp.zeros(out_ref.shape, F32)
        for ref, base in zip(terms, bases):
            total += ref[pl.ds(base + n * size, size)].astype(F32)
        out_ref[...] = total.astype(BF16)


def summed(terms, bases, size, count):
    shape = (size, *terms[0].shape[1:])
    return pl.pallas_call(
        functools.partial(sum_kernel, bases, size),
        in_specs=[spec_vmem()] * len(terms),
        out_shape=[jax.ShapeDtypeStruct(shape, BF16)] * count,
        compiler_params=PARAMS,
        cost_estimate=cost(0, count * math.prod(shape) * 2 * (len(terms) + 1)),
    )(*terms)


def place_kernel(rank_ref, *refs):
    out_ref = refs[-1]
    for d, ref in enumerate(refs[:-1]):
        blocks, width, tile = ref.shape
        start = pl.multiple_of((rank_ref[0] ^ d) * width, width)
        for b in range(blocks):
            out_ref[pl.ds(b * tile, tile), pl.ds(start, width)] = ref[b].T


def placed(rank, parts):
    blocks, width, tile = parts[0].shape
    shape = (blocks * tile, width * len(parts))
    return pl.pallas_call(
        place_kernel,
        in_specs=[spec_smem()] + [spec_vmem()] * len(parts),
        out_shape=jax.ShapeDtypeStruct(shape, BF16),
        compiler_params=PARAMS,
        cost_estimate=cost(0, 2 * 2 * shape[0] * shape[1]),
    )(rank, *parts)


def rows_kernel(scale, rank_ref, *refs):
    out_ref = refs[-1]
    for d, ref in enumerate(refs[:-1]):
        size = ref.shape[0]
        start = pl.multiple_of((rank_ref[0] ^ d) * size, size)
        out_ref[pl.ds(start, size), :] = ref[...].astype(F32) * scale


def rows_placed(rank, parts, scale):
    size, columns = parts[0].shape
    return pl.pallas_call(
        functools.partial(rows_kernel, scale),
        in_specs=[spec_smem()] + [spec_vmem()] * len(parts),
        out_shape=jax.ShapeDtypeStruct((size * len(parts), columns), F32),
        compiler_params=PARAMS,
        cost_estimate=cost(0, 6 * size * len(parts) * columns),
    )(rank, *parts)


def local(feats, weight, tile_vals, tile_cols, tile_count, cotangent):
    node_rows = feats.shape[0]
    cycle = lax.axis_size("blk")
    group = lax.axis_size("repl")
    assert group & (group - 1) == 0 and cycle & (cycle - 1) == 0
    block_rows = node_rows // TILE
    panel_blocks = block_rows * group
    where = jnp.reshape(lax.axis_index("repl"), (1,)).astype(jnp.int32)

    sent = split_columns(feats, tile_cols, tile_count, panel_blocks, cycle, group)
    mine = [sent[0]] + [swapped(sent[d], "repl", d) for d in range(1, group)]
    panel, index = joined_panel(mine, block_rows)
    panel = panel.reshape(panel_blocks, TILE, -1)

    ahead = mirrored(panel, -2)
    beside = mirrored(panel, 1)
    half = block_rows // 2
    far_side = group // 2
    first, second = tile_vals[:half], tile_vals[half:]
    crossed_first = swapped(after(first, panel), "repl", far_side)
    near_vals = [tile_vals] + [
        swapped(after(tile_vals, panel), "repl", d) for d in range(1, far_side)
    ]
    behind = mirrored(panel, 2)
    relayed = mirrored(after(ahead, beside), 1)
    crossed_second = swapped(after(second, ahead, beside), "repl", far_side)
    crossed = [crossed_first, crossed_second]
    passed = [after(crossed_first, behind), after(crossed_second, behind)]
    far_vals = [crossed] + [
        [swapped(part, "repl", d) for part in passed] for d in range(1, far_side)
    ]
    vals = near_vals + [part for parts in far_vals for part in parts]
    columns = sparse_gather(index, vals, [behind, relayed, panel, beside, ahead], group)
    aggregate = [columns[0]] + [swapped(columns[d], "repl", d) for d in range(1, group)]

    made = dense(aggregate, *prepared(after(weight, panel), group), cotangent)
    output, slope, backs = made[0], made[1], made[2:]
    backs = [backs[0]] + [swapped(backs[d], "repl", d) for d in range(1, group)]
    terms = weight_terms(aggregate, after(slope, backs[1]))
    arrived = [swapped(terms[d], "repl", d) for d in range(1, group)]

    backs[0] = after(backs[0], terms[0])
    far, relay, own, near, joined = sparse_scatter(index, vals, backs)
    relay_in = mirrored(relay, 1)
    far_in = mirrored(far, -2)
    near_in = mirrored(near, 1)
    member = panel_blocks // 2
    joined = summed([joined, relay_in], [0, 0], member, 2)
    owned = [None] * group
    for h in (1, 0):
        joined_in = mirrored(after(joined[h], far_in), 2)
        base = h * member
        made = summed(
            [own, far_in, near_in, joined_in], [base, base, base, 0], block_rows, group // 2
        )
        for n, value in enumerate(made):
            owned[h * group // 2 + n] = value
    last = after(owned[0], owned[far_side])
    gathered = [last] + [swapped(owned[d], "repl", d) for d in range(1, group)]
    grad_rows = placed(where, gathered)

    chunk = after(terms[0], own).astype(F32)
    for term in arrived:
        chunk = chunk + term.astype(F32)
    masks = [cycle // 2] + [1 << n for n in range(cycle.bit_length() - 2)]
    waits = [joined[1]] + [owned[far_side]] * (len(masks) - 2) + [owned[0]]
    for mask, wait in zip(masks, waits):
        rounded = lax.optimization_barrier(chunk.astype(BF16))
        other = swapped(rounded, "blk", mask)
        chunk = after(rounded, wait).astype(F32) + other.astype(F32)
    chunk = chunk.astype(BF16)
    chunks = [chunk] + [swapped(chunk, "repl", d) for d in range(1, group)]
    weight_grad = rows_placed(where, chunks, 1.0 / math.sqrt(node_rows * group * cycle))
    return (output, weight_grad, grad_rows)


def solution(mesh):
    in_specs = (
        P(("blk", "repl"), None),
        P(),
        P(("blk", "repl"), None, None, None),
        P(("blk", "repl"), None),
        P(("blk", "repl")),
        P(("blk", "repl"), None),
    )
    out_specs = (P(("blk", "repl"), None), P(), P(("blk", "repl"), None))
    return jax.shard_map(local, mesh=mesh, in_specs=in_specs, out_specs=out_specs, check_vma=False)
```

```python
import functools
import math

import jax
import jax.numpy as jnp
from jax import lax
from jax.experimental import pallas as pl
from jax.experimental.pallas import tpu as pltpu
from jax.sharding import PartitionSpec as P

TILE = 128
REACH = 2
SPAN = 2 * REACH + 1
VMEM_LIMIT = 32 * 1024 * 1024
PARAMS = pltpu.CompilerParams(vmem_limit_bytes=VMEM_LIMIT)
FIRST_PARAMS = pltpu.CompilerParams(vmem_limit_bytes=60 * 1024 * 1024)
EXTRA = 16
BF16 = jnp.bfloat16
F32 = jnp.float32


def mirrored(value, steps):
    count = lax.axis_size("blk")
    pairs = [(k, (k + steps * (1 - 2 * (k & 1))) % count) for k in range(count)]
    return lax.ppermute(value, "blk", pairs)


def after(value, *others):
    return lax.optimization_barrier((value, *others))[0]


def swapped(value, axis, mask):
    count = lax.axis_size(axis)
    return lax.ppermute(value, axis, [(source, source ^ mask) for source in range(count)])


def spec_smem():
    return pl.BlockSpec(memory_space=pltpu.SMEM)


def spec_vmem():
    return pl.BlockSpec(memory_space=pltpu.VMEM)


def spec_hbm():
    return pl.BlockSpec(memory_space=pltpu.HBM)


def cost(flops, bytes_accessed):
    return pl.CostEstimate(flops=flops, bytes_accessed=bytes_accessed, transcendentals=0)


def split_kernel(panel_blocks, cycle, cols_hbm, count_hbm, feats_hbm, *refs):
    cols_ref, count_ref, place_ref, sems = refs[-4:]
    outs = refs[:-4]
    group = len(outs)
    rows, width = feats_hbm.shape[0], outs[0].shape[1]
    block_rows, slots = cols_ref.shape
    rank = lax.axis_index("repl")
    center = lax.axis_index("blk")
    small = [
        pltpu.make_async_copy(cols_hbm, cols_ref, sems.at[group]),
        pltpu.make_async_copy(count_hbm, count_ref, sems.at[group + 1]),
    ]
    large = []
    for d, out_ref in enumerate(outs):
        start = pl.multiple_of((rank ^ d) * width, width)
        large.append(
            pltpu.make_async_copy(
                feats_hbm.at[:, pl.ds(start, width)], out_ref.at[pl.ds(0, rows)], sems.at[d]
            )
        )
    for copy in small + large:
        copy.start()
    for copy in small:
        copy.wait()
    sign = 1 - 2 * (center & 1)
    cols = cols_ref[...]
    offset = (cols // panel_blocks - center) & (cycle - 1)
    offset = jnp.where(offset > REACH, offset - cycle, offset) * sign
    place = (offset + REACH) * panel_blocks + (cols & (panel_blocks - 1))
    row = lax.broadcasted_iota(jnp.int32, cols.shape, 0)
    slot = lax.broadcasted_iota(jnp.int32, cols.shape, 1)
    live = jnp.zeros(cols.shape, jnp.int32)
    for r in range(block_rows):
        live = jnp.where(row == r, count_ref[r], live)
    place = jnp.where(slot < live, place, SPAN * panel_blocks)
    place_ref[...] = jnp.zeros_like(place_ref)
    place_ref[pl.ds(0, block_rows), pl.ds(0, slots)] = place.astype(F32)
    for out_ref in outs:
        out_ref[pl.ds(rows, EXTRA), :] = place_ref[...].astype(BF16)
    for copy in large:
        copy.wait()


def split_columns(feats, tile_cols, tile_count, panel_blocks, cycle, group):
    rows, columns = feats.shape
    width = columns // group
    return pl.pallas_call(
        functools.partial(split_kernel, panel_blocks, cycle),
        in_specs=[spec_hbm()] * 3,
        out_shape=[jax.ShapeDtypeStruct((rows + EXTRA, width), feats.dtype)] * group,
        scratch_shapes=[
            pltpu.VMEM(tile_cols.shape, jnp.int32),
            pltpu.SMEM(tile_count.shape, jnp.int32),
            pltpu.VMEM((EXTRA, width), F32),
            pltpu.SemaphoreType.DMA((group + 2,)),
        ],
        compiler_params=FIRST_PARAMS,
        cost_estimate=cost(0, 2 * rows * columns * 2),
    )(tile_cols, tile_count, feats)


def place_rows(piece, rows, block_rows, spare):
    place = piece[pl.ds(rows, EXTRA), :].astype(F32).astype(jnp.int32)[:block_rows]
    return jnp.where(place < spare, place ^ (lax.axis_index("repl") * block_rows), place)


def join_kernel(block_rows, spare, own_hbm, *refs):
    *pieces, panel_ref, index_ref, own_ref, sem = refs
    copy = pltpu.make_async_copy(own_hbm, own_ref, sem)
    copy.start()
    rows = own_ref.shape[0] - EXTRA
    for d, piece in enumerate(pieces, 1):
        panel_ref[pl.ds(d * rows, rows), :] = piece[pl.ds(0, rows), :]
        place = place_rows(piece, rows, block_rows, spare)
        index_ref[pl.ds(d * block_rows, block_rows), :] = place
    copy.wait()
    panel_ref[pl.ds(0, rows), :] = own_ref[pl.ds(0, rows), :]
    index_ref[pl.ds(0, block_rows), :] = place_rows(own_ref, rows, block_rows, spare)


def joined_panel(pieces, block_rows, spare):
    rows, width = pieces[0].shape
    count = len(pieces)
    shape = (count * (rows - EXTRA), width)
    panel, index = pl.pallas_call(
        functools.partial(join_kernel, block_rows, spare),
        in_specs=[spec_hbm()] + [spec_vmem()] * (count - 1),
        out_shape=[
            jax.ShapeDtypeStruct(shape, BF16),
            jax.ShapeDtypeStruct((count * block_rows, width), jnp.int32),
        ],
        scratch_shapes=[pltpu.VMEM((rows, width), BF16), pltpu.SemaphoreType.DMA(())],
        compiler_params=PARAMS,
        cost_estimate=cost(0, 4 * shape[0] * width),
    )(*pieces)
    return panel.reshape(-1, TILE, width), index


def window_kernel(places, *refs):
    pieces = refs[: len(places)]
    window, sems = refs[-2:]
    copies = [
        pltpu.make_async_copy(
            piece, window.at[pl.ds(place * piece.shape[0], piece.shape[0])], sems.at[n]
        )
        for n, (piece, place) in enumerate(zip(pieces, places))
    ]
    for copy in copies:
        copy.start()
    if len(places) > 1:
        window[window.shape[0] - 1] = jnp.zeros(window.shape[1:], window.dtype)
    for copy in copies:
        copy.wait()


def window_with(pieces, places, window=None):
    size, tile, width = pieces[0].shape
    begun = [] if window is None else [window]
    return pl.pallas_call(
        functools.partial(window_kernel, places),
        in_specs=[spec_vmem()] * len(pieces) + [spec_vmem()] * len(begun),
        out_specs=spec_vmem(),
        out_shape=jax.ShapeDtypeStruct((SPAN * size + 1, tile, width), BF16),
        input_output_aliases={len(pieces): 0} if begun else {},
        scratch_shapes=[pltpu.SemaphoreType.DMA((len(pieces),))],
        compiler_params=PARAMS,
        cost_estimate=cost(0, 4 * len(pieces) * size * tile * width),
    )(*pieces, *begun)


def gather_kernel(group, index, window, *refs):
    outs = refs[-group:]
    vals = refs[:-group]
    block_rows = outs[0].shape[0]
    part = vals[-1].shape[0]

    @pl.loop(0, part)
    def _(i):
        row = 0
        for val in vals:
            for b in range(0, val.shape[0], part):
                slots = range(val.shape[1])
                lhs = jnp.concatenate([val[b + i, s] for s in slots], axis=1)
                rhs = jnp.concatenate([window[index[row + i, s]] for s in slots], axis=0)
                made = jnp.dot(lhs, rhs, preferred_element_type=F32).astype(BF16)
                outs[row // block_rows][row % block_rows + i] = made
                row += part


def sparse_gather(index, vals, window, group):
    rows = sum(val.shape[0] for val in vals)
    slots = vals[0].shape[1]
    blocks, _, width = window.shape
    return pl.pallas_call(
        functools.partial(gather_kernel, group),
        in_specs=[spec_smem()] + [spec_vmem()] * (len(vals) + 1),
        out_shape=[jax.ShapeDtypeStruct((rows // group, TILE, width), BF16)] * group,
        compiler_params=PARAMS,
        cost_estimate=cost(
            rows * slots * TILE * TILE * width * 2,
            rows * slots * TILE * TILE * 2 + blocks * TILE * width * 2,
        ),
    )(index, window, *vals)


def prepare_kernel(group, weight_ref, rows_ref, turned_ref):
    width = weight_ref.shape[0] // group
    rank = lax.axis_index("repl")
    for d in range(group):
        start = pl.multiple_of((rank ^ d) * width, width)
        chunk = weight_ref[pl.ds(start, width), :]
        rows_ref[pl.ds(d * width, width), :] = chunk
        turned_ref[:, pl.ds(d * width, width)] = chunk.T


def prepared(weight, group):
    rows, columns = weight.shape
    return pl.pallas_call(
        functools.partial(prepare_kernel, group),
        in_specs=[spec_vmem()],
        out_shape=[
            jax.ShapeDtypeStruct((rows, columns), BF16),
            jax.ShapeDtypeStruct((columns, rows), BF16),
        ],
        compiler_params=PARAMS,
        cost_estimate=cost(0, 6 * rows * columns),
    )(weight)


def dense_kernel(group, *refs):
    parts = refs[:group]
    weight_ref, turned_ref, cotangent_ref, output_ref, slope_ref = refs[group : group + 5]
    backs = refs[group + 5 :]
    blocks, tile, width = parts[0].shape
    steps = 2
    blocks = blocks // steps
    rows = blocks * tile

    for g in range(steps):
        at = pl.ds(g * rows, rows)
        blocks_at = pl.ds(g * blocks, blocks)
        aggregate = jnp.concatenate([p[blocks_at].reshape(rows, width) for p in parts], axis=1)
        preact = jnp.dot(aggregate, weight_ref[...], preferred_element_type=F32)
        sigma = jax.nn.sigmoid(preact)
        output_ref[at, :] = (preact * sigma).astype(BF16)
        slope = sigma * (1.0 + preact * (1.0 - sigma))
        slope = (cotangent_ref[at, :].astype(F32) * slope).astype(BF16)
        slope_ref[at, :] = slope
        backward = jnp.dot(slope, turned_ref[...], preferred_element_type=F32).astype(BF16)
        for d in range(group):
            piece = backward[:, d * width : (d + 1) * width]
            backs[d][blocks_at] = piece.reshape(blocks, tile, width)


def dense(parts, weight, turned, cotangent):
    group = len(parts)
    node_rows, feat_out = cotangent.shape
    feat_in = weight.shape[0]
    return pl.pallas_call(
        functools.partial(dense_kernel, group),
        in_specs=[spec_vmem()] * (group + 3),
        out_shape=[jax.ShapeDtypeStruct((node_rows, feat_out), BF16)] * 2
        + [jax.ShapeDtypeStruct(parts[0].shape, BF16)] * group,
        compiler_params=PARAMS,
        cost_estimate=cost(
            4 * node_rows * feat_in * feat_out,
            2 * (5 * node_rows * feat_out + 2 * feat_in * feat_out),
        ),
    )(*parts, weight, turned, cotangent)


def term_kernel(slope_ref, *refs):
    group = len(refs) // 2
    slope = slope_ref[...]
    for d in range(group):
        part = refs[d][...].reshape(slope.shape[0], -1)
        term = lax.dot_general(part, slope, (((0,), (0,)), ((), ())), preferred_element_type=F32)
        refs[group + d][...] = term.astype(BF16)


def weight_terms(parts, slope):
    group = len(parts)
    width = parts[0].shape[-1]
    node_rows, feat_out = slope.shape
    return pl.pallas_call(
        term_kernel,
        in_specs=[spec_vmem()] * (group + 1),
        out_shape=[jax.ShapeDtypeStruct((width, feat_out), BF16)] * group,
        compiler_params=PARAMS,
        cost_estimate=cost(
            2 * node_rows * width * group * feat_out, 2 * 3 * node_rows * feat_out
        ),
    )(slope, *parts)


def scatter_kernel(group, index, *refs):
    total = refs[-1]
    outs = refs[-1 - SPAN : -1]
    backs = refs[-1 - SPAN - group : -1 - SPAN]
    vals = refs[: -1 - SPAN - group]
    size = outs[0].shape[0]
    block_rows = backs[0].shape[0]
    part = vals[-1].shape[0]
    total[...] = jnp.zeros_like(total)

    @pl.loop(0, part)
    def _(i):
        row = 0
        for val in vals:
            for b in range(0, val.shape[0], part):
                turned = backs[row // block_rows][row % block_rows + i].T
                for s in range(0, val.shape[1], 2):
                    rhs = jnp.concatenate([val[b + i, s], val[b + i, s + 1]], axis=1)
                    made = jnp.dot(turned, rhs, preferred_element_type=F32)
                    total[index[row + i, s]] += made[:, :TILE]
                    total[index[row + i, s + 1]] += made[:, TILE:]
                row += part

    for n in range(SPAN):
        outs[n][...] = total[pl.ds(n * size, size)].astype(BF16)


def sparse_scatter(index, vals, backs):
    group = len(backs)
    rows = sum(val.shape[0] for val in vals)
    slots = vals[0].shape[1]
    width = backs[0].shape[-1]
    return pl.pallas_call(
        functools.partial(scatter_kernel, group),
        in_specs=[spec_smem()] + [spec_vmem()] * (len(vals) + group),
        out_shape=[jax.ShapeDtypeStruct((rows, width, TILE), BF16)] * SPAN,
        scratch_shapes=[pltpu.VMEM((SPAN * rows + 1, width, TILE), F32)],
        compiler_params=PARAMS,
        cost_estimate=cost(
            rows * slots * TILE * TILE * width * 2,
            rows * slots * TILE * TILE * 2 + 6 * rows * TILE * width * 2,
        ),
    )(index, *vals, *backs)


def sum_kernel(bases, size, *refs):
    terms = refs[: len(bases)]
    for n, out_ref in enumerate(refs[len(bases) :]):
        total = jnp.zeros(out_ref.shape, F32)
        for ref, base in zip(terms, bases):
            total += ref[pl.ds(base + n * size, size)].astype(F32)
        out_ref[...] = total.astype(BF16)


def summed(terms, bases, size, count):
    shape = (size, *terms[0].shape[1:])
    return pl.pallas_call(
        functools.partial(sum_kernel, bases, size),
        in_specs=[spec_vmem()] * len(terms),
        out_shape=[jax.ShapeDtypeStruct(shape, BF16)] * count,
        compiler_params=PARAMS,
        cost_estimate=cost(0, count * math.prod(shape) * 2 * (len(terms) + 1)),
    )(*terms)


def place_kernel(rank_ref, *refs):
    out_ref = refs[-1]
    for d, ref in enumerate(refs[:-1]):
        blocks, width, tile = ref.shape
        start = pl.multiple_of((rank_ref[0] ^ d) * width, width)
        for b in range(blocks):
            out_ref[pl.ds(b * tile, tile), pl.ds(start, width)] = ref[b].T


def placed(rank, parts):
    blocks, width, tile = parts[0].shape
    shape = (blocks * tile, width * len(parts))
    return pl.pallas_call(
        place_kernel,
        in_specs=[spec_smem()] + [spec_vmem()] * len(parts),
        out_shape=jax.ShapeDtypeStruct(shape, BF16),
        compiler_params=PARAMS,
        cost_estimate=cost(0, 2 * 2 * shape[0] * shape[1]),
    )(rank, *parts)


def rows_kernel(scale, rank_ref, *refs):
    out_ref = refs[-1]
    for d, ref in enumerate(refs[:-1]):
        size = ref.shape[0]
        start = pl.multiple_of((rank_ref[0] ^ d) * size, size)
        out_ref[pl.ds(start, size), :] = ref[...].astype(F32) * scale


def rows_placed(rank, parts, scale):
    size, columns = parts[0].shape
    return pl.pallas_call(
        functools.partial(rows_kernel, scale),
        in_specs=[spec_smem()] + [spec_vmem()] * len(parts),
        out_shape=jax.ShapeDtypeStruct((size * len(parts), columns), F32),
        compiler_params=PARAMS,
        cost_estimate=cost(0, 6 * size * len(parts) * columns),
    )(rank, *parts)


def local(feats, weight, tile_vals, tile_cols, tile_count, cotangent):
    node_rows = feats.shape[0]
    cycle = lax.axis_size("blk")
    group = lax.axis_size("repl")
    assert group & (group - 1) == 0 and cycle & (cycle - 1) == 0
    block_rows = node_rows // TILE
    panel_blocks = block_rows * group
    spare = SPAN * panel_blocks
    far_side = group // 2
    where = jnp.reshape(lax.axis_index("repl"), (1,)).astype(jnp.int32)

    sent = split_columns(feats, tile_cols, tile_count, panel_blocks, cycle, group)
    mine = [sent[0]] + [swapped(sent[d], "repl", d) for d in range(1, group)]
    panel, index = joined_panel(mine, block_rows, spare)

    ahead = mirrored(panel, -2)
    beside = mirrored(panel, 1)
    behind = mirrored(panel, 2)
    relayed = mirrored(after(ahead, beside), 1)
    window = window_with([behind, panel, beside, ahead], [0, 2, 3, 4])
    window = window_with([relayed], [1], window)

    half = block_rows // 2
    crossed = [
        swapped(after(tile_vals, panel)[:half], "repl", far_side),
        swapped(after(tile_vals, ahead)[half:], "repl", far_side),
    ]
    near = range(1, far_side)
    vals = [tile_vals] + [swapped(after(tile_vals, panel), "repl", d) for d in near]
    vals += crossed + [swapped(part, "repl", d) for d in near for part in crossed]
    columns = sparse_gather(index, vals, window, group)
    aggregate = [columns[0]] + [swapped(columns[d], "repl", d) for d in range(1, group)]

    made = dense(aggregate, *prepared(after(weight, panel), group), cotangent)
    output, slope, backs = made[0], made[1], made[2:]
    backs = [backs[0]] + [swapped(backs[d], "repl", d) for d in range(1, group)]

    terms = weight_terms(aggregate, after(slope, backs[1]))
    arrived = [swapped(terms[d], "repl", d) for d in range(1, group)]
    backs[0] = after(backs[0], terms[0])
    chunk = terms[0].astype(F32)
    for term in arrived:
        chunk = chunk + term.astype(F32)
    rounded = lax.optimization_barrier(chunk.astype(BF16))

    far, relay, own, near, joined = sparse_scatter(index, vals, backs)
    relay_in = mirrored(relay, 1)
    far_in = mirrored(far, -2)
    near_in = mirrored(near, 1)
    (joined,) = summed([joined, relay_in], [0, 0], panel_blocks, 1)
    joined_in = mirrored(after(joined, far_in), 2)
    owned = summed([own, far_in, near_in, joined_in], [0] * 4, block_rows, group)
    gathered = [owned[0]] + [swapped(owned[d], "repl", d) for d in range(1, group)]
    grad_rows = placed(where, gathered)

    masks = [1 << n for n in range(cycle.bit_length() - 1)]
    masks[:2] = masks[1::-1]
    rounded = after(rounded, own)
    waits = {masks[0]: joined, masks[-1]: owned[0]}
    for mask in masks:
        other = swapped(rounded, "blk", mask)
        chunk = after(rounded, waits.get(mask, joined)).astype(F32) + other.astype(F32)
        rounded = lax.optimization_barrier(chunk.astype(BF16))
    chunks = [rounded] + [swapped(rounded, "repl", d) for d in range(1, group)]
    scale = 1.0 / math.sqrt(node_rows * group * cycle)
    weight_grad = rows_placed(where, chunks, scale)
    return (output, weight_grad, grad_rows)


def solution(mesh):
    in_specs = (
        P(("blk", "repl"), None),
        P(),
        P(("blk", "repl"), None, None, None),
        P(("blk", "repl"), None),
        P(("blk", "repl")),
        P(("blk", "repl"), None),
    )
    out_specs = (P(("blk", "repl"), None), P(), P(("blk", "repl"), None))
    return jax.shard_map(local, mesh=mesh, in_specs=in_specs, out_specs=out_specs, check_vma=False)
```

```python
import functools
import math

import jax
import jax.numpy as jnp
from jax import lax
from jax.experimental import pallas as pl
from jax.experimental.pallas import tpu as pltpu
from jax.sharding import PartitionSpec as P

TILE = 128
REACH = 2
SPAN = 2 * REACH + 1
VMEM_LIMIT = 32 * 1024 * 1024
PARAMS = pltpu.CompilerParams(vmem_limit_bytes=VMEM_LIMIT)
FIRST_PARAMS = pltpu.CompilerParams(vmem_limit_bytes=60 * 1024 * 1024)
EXTRA = 16
BF16 = jnp.bfloat16
F32 = jnp.float32


def mirrored(value, steps):
    count = lax.axis_size("blk")
    pairs = [(k, (k + steps * (1 - 2 * (k & 1))) % count) for k in range(count)]
    return lax.ppermute(value, "blk", pairs)


def after(value, *others):
    return lax.optimization_barrier((value, *others))[0]


def swapped(value, axis, mask):
    count = lax.axis_size(axis)
    return lax.ppermute(value, axis, [(source, source ^ mask) for source in range(count)])


def spec_smem():
    return pl.BlockSpec(memory_space=pltpu.SMEM)


def spec_vmem():
    return pl.BlockSpec(memory_space=pltpu.VMEM)


def spec_hbm():
    return pl.BlockSpec(memory_space=pltpu.HBM)


def cost(flops, bytes_accessed):
    return pl.CostEstimate(flops=flops, bytes_accessed=bytes_accessed, transcendentals=0)


def split_kernel(panel_blocks, cycle, cols_hbm, count_hbm, feats_hbm, *refs):
    cols_ref, count_ref, place_ref, sems = refs[-4:]
    outs = refs[:-4]
    group = len(outs)
    rows, width = feats_hbm.shape[0], outs[0].shape[1]
    block_rows, slots = cols_ref.shape
    rank = lax.axis_index("repl")
    center = lax.axis_index("blk")
    small = [
        pltpu.make_async_copy(cols_hbm, cols_ref, sems.at[group]),
        pltpu.make_async_copy(count_hbm, count_ref, sems.at[group + 1]),
    ]
    large = []
    for d, out_ref in enumerate(outs):
        start = pl.multiple_of((rank ^ d) * width, width)
        large.append(
            pltpu.make_async_copy(
                feats_hbm.at[:, pl.ds(start, width)], out_ref.at[pl.ds(0, rows)], sems.at[d]
            )
        )
    for copy in small + large:
        copy.start()
    for copy in small:
        copy.wait()
    sign = 1 - 2 * (center & 1)
    cols = cols_ref[...]
    offset = (cols // panel_blocks - center) & (cycle - 1)
    offset = jnp.where(offset > REACH, offset - cycle, offset) * sign
    place = (offset + REACH) * panel_blocks + (cols & (panel_blocks - 1))
    row = lax.broadcasted_iota(jnp.int32, cols.shape, 0)
    slot = lax.broadcasted_iota(jnp.int32, cols.shape, 1)
    live = jnp.zeros(cols.shape, jnp.int32)
    for r in range(block_rows):
        live = jnp.where(row == r, count_ref[r], live)
    place = jnp.where(slot < live, place, SPAN * panel_blocks)
    place_ref[...] = jnp.zeros_like(place_ref)
    place_ref[pl.ds(0, block_rows), pl.ds(0, slots)] = place.astype(F32)
    for out_ref in outs:
        out_ref[pl.ds(rows, EXTRA), :] = place_ref[...].astype(BF16)
    for copy in large:
        copy.wait()


def split_columns(feats, tile_cols, tile_count, panel_blocks, cycle, group):
    rows, columns = feats.shape
    width = columns // group
    return pl.pallas_call(
        functools.partial(split_kernel, panel_blocks, cycle),
        in_specs=[spec_hbm()] * 3,
        out_shape=[jax.ShapeDtypeStruct((rows + EXTRA, width), feats.dtype)] * group,
        scratch_shapes=[
            pltpu.VMEM(tile_cols.shape, jnp.int32),
            pltpu.SMEM(tile_count.shape, jnp.int32),
            pltpu.VMEM((EXTRA, width), F32),
            pltpu.SemaphoreType.DMA((group + 2,)),
        ],
        compiler_params=FIRST_PARAMS,
        cost_estimate=cost(0, 2 * rows * columns * 2),
    )(tile_cols, tile_count, feats)


def place_rows(piece, rows, block_rows, spare):
    place = piece[pl.ds(rows, EXTRA), :].astype(F32).astype(jnp.int32)[:block_rows]
    return jnp.where(place < spare, place ^ (lax.axis_index("repl") * block_rows), place)


def join_kernel(block_rows, spare, own_hbm, *refs):
    *pieces, panel_ref, index_ref, own_ref, sem = refs
    copy = pltpu.make_async_copy(own_hbm, own_ref, sem)
    copy.start()
    rows = own_ref.shape[0] - EXTRA
    for d, piece in enumerate(pieces, 1):
        panel_ref[pl.ds(d * rows, rows), :] = piece[pl.ds(0, rows), :]
        place = place_rows(piece, rows, block_rows, spare)
        index_ref[pl.ds(d * block_rows, block_rows), :] = place
    copy.wait()
    panel_ref[pl.ds(0, rows), :] = own_ref[pl.ds(0, rows), :]
    index_ref[pl.ds(0, block_rows), :] = place_rows(own_ref, rows, block_rows, spare)


def joined_panel(pieces, block_rows, spare):
    rows, width = pieces[0].shape
    count = len(pieces)
    shape = (count * (rows - EXTRA), width)
    panel, index = pl.pallas_call(
        functools.partial(join_kernel, block_rows, spare),
        in_specs=[spec_hbm()] + [spec_vmem()] * (count - 1),
        out_shape=[
            jax.ShapeDtypeStruct(shape, BF16),
            jax.ShapeDtypeStruct((count * block_rows, width), jnp.int32),
        ],
        scratch_shapes=[pltpu.VMEM((rows, width), BF16), pltpu.SemaphoreType.DMA(())],
        compiler_params=PARAMS,
        cost_estimate=cost(0, 4 * shape[0] * width),
    )(*pieces)
    return panel.reshape(-1, TILE, width), index


def window_kernel(places, *refs):
    pieces = refs[: len(places)]
    window, sems = refs[-2:]
    copies = [
        pltpu.make_async_copy(
            piece, window.at[pl.ds(place * piece.shape[0], piece.shape[0])], sems.at[n]
        )
        for n, (piece, place) in enumerate(zip(pieces, places))
    ]
    for copy in copies:
        copy.start()
    if len(places) > 1:
        window[window.shape[0] - 1] = jnp.zeros(window.shape[1:], window.dtype)
    for copy in copies:
        copy.wait()


def window_with(pieces, places, window=None):
    size, tile, width = pieces[0].shape
    begun = [] if window is None else [window]
    return pl.pallas_call(
        functools.partial(window_kernel, places),
        in_specs=[spec_vmem()] * len(pieces) + [spec_vmem()] * len(begun),
        out_specs=spec_vmem(),
        out_shape=jax.ShapeDtypeStruct((SPAN * size + 1, tile, width), BF16),
        input_output_aliases={len(pieces): 0} if begun else {},
        scratch_shapes=[pltpu.SemaphoreType.DMA((len(pieces),))],
        compiler_params=PARAMS,
        cost_estimate=cost(0, 4 * len(pieces) * size * tile * width),
    )(*pieces, *begun)


def gather_kernel(group, index, window, *refs):
    outs = refs[-group:]
    vals = refs[:-group]
    block_rows = outs[0].shape[0]
    part = vals[-1].shape[0]

    @pl.loop(0, part)
    def _(i):
        row = 0
        for val in vals:
            for b in range(0, val.shape[0], part):
                slots = range(val.shape[1])
                lhs = jnp.concatenate([val[b + i, s] for s in slots], axis=1)
                rhs = jnp.concatenate([window[index[row + i, s]] for s in slots], axis=0)
                made = jnp.dot(lhs, rhs, preferred_element_type=F32).astype(BF16)
                outs[row // block_rows][row % block_rows + i] = made
                row += part


def sparse_gather(index, vals, window, group):
    rows = sum(val.shape[0] for val in vals)
    slots = vals[0].shape[1]
    blocks, _, width = window.shape
    return pl.pallas_call(
        functools.partial(gather_kernel, group),
        in_specs=[spec_smem()] + [spec_vmem()] * (len(vals) + 1),
        out_shape=[jax.ShapeDtypeStruct((rows // group, TILE, width), BF16)] * group,
        compiler_params=PARAMS,
        cost_estimate=cost(
            rows * slots * TILE * TILE * width * 2,
            rows * slots * TILE * TILE * 2 + blocks * TILE * width * 2,
        ),
    )(index, window, *vals)


def prepare_kernel(group, weight_ref, rows_ref, turned_ref):
    width = weight_ref.shape[0] // group
    rank = lax.axis_index("repl")
    for d in range(group):
        start = pl.multiple_of((rank ^ d) * width, width)
        chunk = weight_ref[pl.ds(start, width), :]
        rows_ref[pl.ds(d * width, width), :] = chunk
        turned_ref[:, pl.ds(d * width, width)] = chunk.T


def prepared(weight, group):
    rows, columns = weight.shape
    return pl.pallas_call(
        functools.partial(prepare_kernel, group),
        in_specs=[spec_vmem()],
        out_shape=[
            jax.ShapeDtypeStruct((rows, columns), BF16),
            jax.ShapeDtypeStruct((columns, rows), BF16),
        ],
        compiler_params=PARAMS,
        cost_estimate=cost(0, 6 * rows * columns),
    )(weight)


def dense_kernel(group, *refs):
    parts = refs[:group]
    weight_ref, turned_ref, cotangent_ref, output_ref, slope_ref = refs[group : group + 5]
    backs = refs[group + 5 :]
    blocks, tile, width = parts[0].shape
    steps = 2
    blocks = blocks // steps
    rows = blocks * tile

    for g in range(steps):
        at = pl.ds(g * rows, rows)
        blocks_at = pl.ds(g * blocks, blocks)
        aggregate = jnp.concatenate([p[blocks_at].reshape(rows, width) for p in parts], axis=1)
        preact = jnp.dot(aggregate, weight_ref[...], preferred_element_type=F32)
        sigma = jax.nn.sigmoid(preact)
        output_ref[at, :] = (preact * sigma).astype(BF16)
        slope = sigma * (1.0 + preact * (1.0 - sigma))
        slope = (cotangent_ref[at, :].astype(F32) * slope).astype(BF16)
        slope_ref[at, :] = slope
        backward = jnp.dot(slope, turned_ref[...], preferred_element_type=F32).astype(BF16)
        for d in range(group):
            piece = backward[:, d * width : (d + 1) * width]
            backs[d][blocks_at] = piece.reshape(blocks, tile, width)


def dense(parts, weight, turned, cotangent):
    group = len(parts)
    node_rows, feat_out = cotangent.shape
    feat_in = weight.shape[0]
    return pl.pallas_call(
        functools.partial(dense_kernel, group),
        in_specs=[spec_vmem()] * (group + 3),
        out_shape=[jax.ShapeDtypeStruct((node_rows, feat_out), BF16)] * 2
        + [jax.ShapeDtypeStruct(parts[0].shape, BF16)] * group,
        compiler_params=PARAMS,
        cost_estimate=cost(
            4 * node_rows * feat_in * feat_out,
            2 * (5 * node_rows * feat_out + 2 * feat_in * feat_out),
        ),
    )(*parts, weight, turned, cotangent)


def term_kernel(slope_ref, *refs):
    group = len(refs) // 2
    slope = slope_ref[...]
    for d in range(group):
        part = refs[d][...].reshape(slope.shape[0], -1)
        term = lax.dot_general(part, slope, (((0,), (0,)), ((), ())), preferred_element_type=F32)
        refs[group + d][...] = term.astype(BF16)


def weight_terms(parts, slope):
    group = len(parts)
    width = parts[0].shape[-1]
    node_rows, feat_out = slope.shape
    return pl.pallas_call(
        term_kernel,
        in_specs=[spec_vmem()] * (group + 1),
        out_shape=[jax.ShapeDtypeStruct((width, feat_out), BF16)] * group,
        compiler_params=PARAMS,
        cost_estimate=cost(
            2 * node_rows * width * group * feat_out, 2 * 3 * node_rows * feat_out
        ),
    )(slope, *parts)


def scatter_kernel(group, index, *refs):
    total = refs[-1]
    outs = refs[-1 - SPAN : -1]
    backs = refs[-1 - SPAN - group : -1 - SPAN]
    vals = refs[: -1 - SPAN - group]
    size = outs[0].shape[0]
    block_rows = backs[0].shape[0]
    part = vals[-1].shape[0]
    total[...] = jnp.zeros_like(total)

    @pl.loop(0, part)
    def _(i):
        row = 0
        for val in vals:
            for b in range(0, val.shape[0], part):
                turned = backs[row // block_rows][row % block_rows + i].T
                for s in range(0, val.shape[1], 2):
                    rhs = jnp.concatenate([val[b + i, s], val[b + i, s + 1]], axis=1)
                    made = jnp.dot(turned, rhs, preferred_element_type=F32)
                    total[index[row + i, s]] += made[:, :TILE]
                    total[index[row + i, s + 1]] += made[:, TILE:]
                row += part

    for n in range(SPAN):
        outs[n][...] = total[pl.ds(n * size, size)].astype(BF16)


def sparse_scatter(index, vals, backs):
    group = len(backs)
    rows = sum(val.shape[0] for val in vals)
    slots = vals[0].shape[1]
    width = backs[0].shape[-1]
    return pl.pallas_call(
        functools.partial(scatter_kernel, group),
        in_specs=[spec_smem()] + [spec_vmem()] * (len(vals) + group),
        out_shape=[jax.ShapeDtypeStruct((rows, width, TILE), BF16)] * SPAN,
        scratch_shapes=[pltpu.VMEM((SPAN * rows + 1, width, TILE), F32)],
        compiler_params=PARAMS,
        cost_estimate=cost(
            rows * slots * TILE * TILE * width * 2,
            rows * slots * TILE * TILE * 2 + 6 * rows * TILE * width * 2,
        ),
    )(index, *vals, *backs)


def sum_kernel(bases, size, *refs):
    terms = refs[: len(bases)]
    for n, out_ref in enumerate(refs[len(bases) :]):
        total = jnp.zeros(out_ref.shape, F32)
        for ref, base in zip(terms, bases):
            total += ref[pl.ds(base + n * size, size)].astype(F32)
        out_ref[...] = total.astype(BF16)


def summed(terms, bases, size, count):
    shape = (size, *terms[0].shape[1:])
    return pl.pallas_call(
        functools.partial(sum_kernel, bases, size),
        in_specs=[spec_vmem()] * len(terms),
        out_shape=[jax.ShapeDtypeStruct(shape, BF16)] * count,
        compiler_params=PARAMS,
        cost_estimate=cost(0, count * math.prod(shape) * 2 * (len(terms) + 1)),
    )(*terms)


def place_kernel(rank_ref, *refs):
    out_ref = refs[-1]
    for d, ref in enumerate(refs[:-1]):
        blocks, width, tile = ref.shape
        start = pl.multiple_of((rank_ref[0] ^ d) * width, width)
        for b in range(blocks):
            out_ref[pl.ds(b * tile, tile), pl.ds(start, width)] = ref[b].T


def placed(rank, parts):
    blocks, width, tile = parts[0].shape
    shape = (blocks * tile, width * len(parts))
    return pl.pallas_call(
        place_kernel,
        in_specs=[spec_smem()] + [spec_vmem()] * len(parts),
        out_shape=jax.ShapeDtypeStruct(shape, BF16),
        compiler_params=PARAMS,
        cost_estimate=cost(0, 2 * 2 * shape[0] * shape[1]),
    )(rank, *parts)


def rows_kernel(scale, rank_ref, *refs):
    out_ref = refs[-1]
    for d, ref in enumerate(refs[:-1]):
        size = ref.shape[0]
        start = pl.multiple_of((rank_ref[0] ^ d) * size, size)
        out_ref[pl.ds(start, size), :] = ref[...].astype(F32) * scale


def rows_placed(rank, parts, scale):
    size, columns = parts[0].shape
    return pl.pallas_call(
        functools.partial(rows_kernel, scale),
        in_specs=[spec_smem()] + [spec_vmem()] * len(parts),
        out_shape=jax.ShapeDtypeStruct((size * len(parts), columns), F32),
        compiler_params=PARAMS,
        cost_estimate=cost(0, 6 * size * len(parts) * columns),
    )(rank, *parts)


def local(feats, weight, tile_vals, tile_cols, tile_count, cotangent):
    node_rows = feats.shape[0]
    cycle = lax.axis_size("blk")
    group = lax.axis_size("repl")
    assert group & (group - 1) == 0 and cycle & (cycle - 1) == 0
    block_rows = node_rows // TILE
    panel_blocks = block_rows * group
    spare = SPAN * panel_blocks
    far_side = group // 2
    where = jnp.reshape(lax.axis_index("repl"), (1,)).astype(jnp.int32)

    sent = split_columns(feats, tile_cols, tile_count, panel_blocks, cycle, group)
    mine = [sent[0]] + [swapped(sent[d], "repl", d) for d in range(1, group)]
    panel, index = joined_panel(mine, block_rows, spare)

    ahead = mirrored(panel, -2)
    beside = mirrored(panel, 1)
    behind = mirrored(panel, 2)
    relayed = mirrored(after(ahead, beside), 1)
    window = window_with([behind, panel, beside, ahead], [0, 2, 3, 4])
    window = window_with([relayed], [1], window)

    half = block_rows // 2
    ready = after(tile_vals, mine[1])
    own_vals = [ready[:half], ready[half:]]
    crossed = [swapped(after(part, panel), "repl", far_side) for part in own_vals]
    near = range(1, far_side)
    vals = own_vals + [swapped(after(part, panel), "repl", d) for d in near for part in own_vals]
    vals += crossed + [swapped(part, "repl", d) for d in near for part in crossed]
    columns = sparse_gather(index, vals, window, group)
    aggregate = [columns[0]] + [swapped(columns[d], "repl", d) for d in range(1, group)]

    made = dense(aggregate, *prepared(after(weight, panel), group), cotangent)
    output, slope, backs = made[0], made[1], made[2:]
    backs = [backs[0]] + [swapped(backs[d], "repl", d) for d in range(1, group)]

    terms = weight_terms(aggregate, after(slope, backs[1]))
    arrived = [swapped(terms[d], "repl", d) for d in range(1, group)]
    backs[0] = after(backs[0], terms[0])
    chunk = terms[0].astype(F32)
    for term in arrived:
        chunk = chunk + term.astype(F32)
    rounded = lax.optimization_barrier(chunk.astype(BF16))

    far, relay, own, near_share, joined = sparse_scatter(index, vals, backs)
    relay_in = mirrored(relay, 1)
    far_in = mirrored(far, -2)
    near_in = mirrored(near_share, 1)
    (joined,) = summed([joined, relay_in], [0, 0], panel_blocks, 1)

    rounded = after(rounded, own)
    masks = [cycle // 2] + [1 << n for n in range(cycle.bit_length() - 2)]
    wait = None
    for mask in masks:
        other = swapped(rounded, "blk", mask)
        if mask == masks[-1]:
            joined_in = mirrored(after(joined, far_in, wait), 2)
            owned = summed([own, far_in, near_in, joined_in], [0] * 4, block_rows, group)
            gathered = [owned[0]] + [swapped(owned[d], "repl", d) for d in range(1, group)]
            rounded = after(rounded, gathered[1])
        chunk = rounded.astype(F32) + other.astype(F32)
        rounded = lax.optimization_barrier(chunk.astype(BF16))
        wait = rounded if wait is None else wait
    grad_rows = placed(where, gathered)
    chunks = [rounded] + [swapped(rounded, "repl", d) for d in range(1, group)]
    scale = 1.0 / math.sqrt(node_rows * group * cycle)
    weight_grad = rows_placed(where, chunks, scale)
    return (output, weight_grad, grad_rows)


def solution(mesh):
    in_specs = (
        P(("blk", "repl"), None),
        P(),
        P(("blk", "repl"), None, None, None),
        P(("blk", "repl"), None),
        P(("blk", "repl")),
        P(("blk", "repl"), None),
    )
    out_specs = (P(("blk", "repl"), None), P(), P(("blk", "repl"), None))
    return jax.shard_map(local, mesh=mesh, in_specs=in_specs, out_specs=out_specs, check_vma=False)
```

```python
import functools
import math

import jax
import jax.numpy as jnp
from jax import lax
from jax.experimental import pallas as pl
from jax.experimental.pallas import tpu as pltpu
from jax.sharding import PartitionSpec as P

TILE = 128
REACH = 2
SPAN = 2 * REACH + 1
VMEM_LIMIT = 32 * 1024 * 1024
PARAMS = pltpu.CompilerParams(vmem_limit_bytes=VMEM_LIMIT)
FIRST_PARAMS = pltpu.CompilerParams(vmem_limit_bytes=60 * 1024 * 1024)
EXTRA = 16
BF16 = jnp.bfloat16
F32 = jnp.float32


def mirrored(value, steps):
    count = lax.axis_size("blk")
    pairs = [(k, (k + steps * (1 - 2 * (k & 1))) % count) for k in range(count)]
    return lax.ppermute(value, "blk", pairs)


def after(value, *others):
    return lax.optimization_barrier((value, *others))[0]


def swapped(value, axis, mask):
    count = lax.axis_size(axis)
    return lax.ppermute(value, axis, [(source, source ^ mask) for source in range(count)])


def spec_smem():
    return pl.BlockSpec(memory_space=pltpu.SMEM)


def spec_vmem():
    return pl.BlockSpec(memory_space=pltpu.VMEM)


def spec_hbm():
    return pl.BlockSpec(memory_space=pltpu.HBM)


def cost(flops, bytes_accessed):
    return pl.CostEstimate(flops=flops, bytes_accessed=bytes_accessed, transcendentals=0)


def split_kernel(panel_blocks, cycle, cols_hbm, count_hbm, feats_hbm, *refs):
    cols_ref, count_ref, place_ref, sems = refs[-4:]
    outs = refs[:-4]
    group = len(outs)
    rows, width = feats_hbm.shape[0], outs[0].shape[1]
    block_rows, slots = cols_ref.shape
    rank = lax.axis_index("repl")
    center = lax.axis_index("blk")
    small = [
        pltpu.make_async_copy(cols_hbm, cols_ref, sems.at[group]),
        pltpu.make_async_copy(count_hbm, count_ref, sems.at[group + 1]),
    ]
    large = []
    for d, out_ref in enumerate(outs):
        start = pl.multiple_of((rank ^ d) * width, width)
        large.append(
            pltpu.make_async_copy(
                feats_hbm.at[:, pl.ds(start, width)], out_ref.at[pl.ds(0, rows)], sems.at[d]
            )
        )
    for copy in small + large:
        copy.start()
    for copy in small:
        copy.wait()
    sign = 1 - 2 * (center & 1)
    cols = cols_ref[...]
    offset = (cols // panel_blocks - center) & (cycle - 1)
    offset = jnp.where(offset > REACH, offset - cycle, offset) * sign
    place = (offset + REACH) * panel_blocks + (cols & (panel_blocks - 1))
    row = lax.broadcasted_iota(jnp.int32, cols.shape, 0)
    slot = lax.broadcasted_iota(jnp.int32, cols.shape, 1)
    live = jnp.zeros(cols.shape, jnp.int32)
    for r in range(block_rows):
        live = jnp.where(row == r, count_ref[r], live)
    place = jnp.where(slot < live, place, SPAN * panel_blocks)
    place_ref[...] = jnp.zeros_like(place_ref)
    place_ref[pl.ds(0, block_rows), pl.ds(0, slots)] = place.astype(F32)
    for out_ref in outs:
        out_ref[pl.ds(rows, EXTRA), :] = place_ref[...].astype(BF16)
    for copy in large:
        copy.wait()


def split_columns(feats, tile_cols, tile_count, panel_blocks, cycle, group):
    rows, columns = feats.shape
    width = columns // group
    return pl.pallas_call(
        functools.partial(split_kernel, panel_blocks, cycle),
        in_specs=[spec_hbm()] * 3,
        out_shape=[jax.ShapeDtypeStruct((rows + EXTRA, width), feats.dtype)] * group,
        scratch_shapes=[
            pltpu.VMEM(tile_cols.shape, jnp.int32),
            pltpu.SMEM(tile_count.shape, jnp.int32),
            pltpu.VMEM((EXTRA, width), F32),
            pltpu.SemaphoreType.DMA((group + 2,)),
        ],
        compiler_params=FIRST_PARAMS,
        cost_estimate=cost(0, 2 * rows * columns * 2),
    )(tile_cols, tile_count, feats)


def place_rows(piece, rows, block_rows, spare):
    place = piece[pl.ds(rows, EXTRA), :].astype(F32).astype(jnp.int32)[:block_rows]
    return jnp.where(place < spare, place ^ (lax.axis_index("repl") * block_rows), place)


def join_kernel(block_rows, spare, own_hbm, *refs):
    *pieces, panel_ref, index_ref, own_ref, sem = refs
    copy = pltpu.make_async_copy(own_hbm, own_ref, sem)
    copy.start()
    rows = own_ref.shape[0] - EXTRA
    for d, piece in enumerate(pieces, 1):
        panel_ref[pl.ds(d * rows, rows), :] = piece[pl.ds(0, rows), :]
        place = place_rows(piece, rows, block_rows, spare)
        index_ref[pl.ds(d * block_rows, block_rows), :] = place
    copy.wait()
    panel_ref[pl.ds(0, rows), :] = own_ref[pl.ds(0, rows), :]
    index_ref[pl.ds(0, block_rows), :] = place_rows(own_ref, rows, block_rows, spare)


def joined_panel(pieces, block_rows, spare):
    rows, width = pieces[0].shape
    count = len(pieces)
    shape = (count * (rows - EXTRA), width)
    panel, index = pl.pallas_call(
        functools.partial(join_kernel, block_rows, spare),
        in_specs=[spec_hbm()] + [spec_vmem()] * (count - 1),
        out_shape=[
            jax.ShapeDtypeStruct(shape, BF16),
            jax.ShapeDtypeStruct((count * block_rows, width), jnp.int32),
        ],
        scratch_shapes=[pltpu.VMEM((rows, width), BF16), pltpu.SemaphoreType.DMA(())],
        compiler_params=PARAMS,
        cost_estimate=cost(0, 4 * shape[0] * width),
    )(*pieces)
    return panel.reshape(-1, TILE, width), index


def window_kernel(places, *refs):
    pieces = refs[: len(places)]
    window, sems = refs[-2:]
    copies = [
        pltpu.make_async_copy(
            piece, window.at[pl.ds(place * piece.shape[0], piece.shape[0])], sems.at[n]
        )
        for n, (piece, place) in enumerate(zip(pieces, places))
    ]
    for copy in copies:
        copy.start()
    if len(places) > 1:
        window[window.shape[0] - 1] = jnp.zeros(window.shape[1:], window.dtype)
    for copy in copies:
        copy.wait()


def window_with(pieces, places, window=None):
    size, tile, width = pieces[0].shape
    begun = [] if window is None else [window]
    return pl.pallas_call(
        functools.partial(window_kernel, places),
        in_specs=[spec_vmem()] * len(pieces) + [spec_vmem()] * len(begun),
        out_specs=spec_vmem(),
        out_shape=jax.ShapeDtypeStruct((SPAN * size + 1, tile, width), BF16),
        input_output_aliases={len(pieces): 0} if begun else {},
        scratch_shapes=[pltpu.SemaphoreType.DMA((len(pieces),))],
        compiler_params=PARAMS,
        cost_estimate=cost(0, 4 * len(pieces) * size * tile * width),
    )(*pieces, *begun)


def gather_kernel(group, index, window, *refs):
    outs = refs[-group:]
    vals = refs[:-group]
    block_rows = outs[0].shape[0]
    part = vals[-1].shape[0]

    @pl.loop(0, part)
    def _(i):
        row = 0
        for val in vals:
            for b in range(0, val.shape[0], part):
                slots = range(val.shape[1])
                lhs = jnp.concatenate([val[b + i, s] for s in slots], axis=1)
                rhs = jnp.concatenate([window[index[row + i, s]] for s in slots], axis=0)
                made = jnp.dot(lhs, rhs, preferred_element_type=F32).astype(BF16)
                outs[row // block_rows][row % block_rows + i] = made
                row += part


def sparse_gather(index, vals, window, group):
    rows = sum(val.shape[0] for val in vals)
    slots = vals[0].shape[1]
    blocks, _, width = window.shape
    return pl.pallas_call(
        functools.partial(gather_kernel, group),
        in_specs=[spec_smem()] + [spec_vmem()] * (len(vals) + 1),
        out_shape=[jax.ShapeDtypeStruct((rows // group, TILE, width), BF16)] * group,
        compiler_params=PARAMS,
        cost_estimate=cost(
            rows * slots * TILE * TILE * width * 2,
            rows * slots * TILE * TILE * 2 + blocks * TILE * width * 2,
        ),
    )(index, window, *vals)


def prepare_kernel(group, weight_ref, rows_ref, turned_ref):
    width = weight_ref.shape[0] // group
    rank = lax.axis_index("repl")
    for d in range(group):
        start = pl.multiple_of((rank ^ d) * width, width)
        chunk = weight_ref[pl.ds(start, width), :]
        rows_ref[pl.ds(d * width, width), :] = chunk
        turned_ref[:, pl.ds(d * width, width)] = chunk.T


def prepared(weight, group):
    rows, columns = weight.shape
    return pl.pallas_call(
        functools.partial(prepare_kernel, group),
        in_specs=[spec_vmem()],
        out_shape=[
            jax.ShapeDtypeStruct((rows, columns), BF16),
            jax.ShapeDtypeStruct((columns, rows), BF16),
        ],
        compiler_params=PARAMS,
        cost_estimate=cost(0, 6 * rows * columns),
    )(weight)


def dense_kernel(group, *refs):
    parts = refs[:group]
    weight_ref, turned_ref, cotangent_ref, output_ref, slope_ref = refs[group : group + 5]
    backs = refs[group + 5 :]
    blocks, tile, width = parts[0].shape
    steps = 2
    blocks = blocks // steps
    rows = blocks * tile

    for g in range(steps):
        at = pl.ds(g * rows, rows)
        blocks_at = pl.ds(g * blocks, blocks)
        aggregate = jnp.concatenate([p[blocks_at].reshape(rows, width) for p in parts], axis=1)
        preact = jnp.dot(aggregate, weight_ref[...], preferred_element_type=F32)
        sigma = jax.nn.sigmoid(preact)
        output_ref[at, :] = (preact * sigma).astype(BF16)
        slope = sigma * (1.0 + preact * (1.0 - sigma))
        slope = (cotangent_ref[at, :].astype(F32) * slope).astype(BF16)
        slope_ref[at, :] = slope
        backward = jnp.dot(slope, turned_ref[...], preferred_element_type=F32).astype(BF16)
        for d in range(group):
            piece = backward[:, d * width : (d + 1) * width]
            backs[d][blocks_at] = piece.reshape(blocks, tile, width)


def dense(parts, weight, turned, cotangent):
    group = len(parts)
    node_rows, feat_out = cotangent.shape
    feat_in = weight.shape[0]
    return pl.pallas_call(
        functools.partial(dense_kernel, group),
        in_specs=[spec_vmem()] * (group + 3),
        out_shape=[jax.ShapeDtypeStruct((node_rows, feat_out), BF16)] * 2
        + [jax.ShapeDtypeStruct(parts[0].shape, BF16)] * group,
        compiler_params=PARAMS,
        cost_estimate=cost(
            4 * node_rows * feat_in * feat_out,
            2 * (5 * node_rows * feat_out + 2 * feat_in * feat_out),
        ),
    )(*parts, weight, turned, cotangent)


def term_kernel(slope_ref, *refs):
    group = len(refs) // 2
    slope = slope_ref[...]
    for d in range(group):
        part = refs[d][...].reshape(slope.shape[0], -1)
        term = lax.dot_general(part, slope, (((0,), (0,)), ((), ())), preferred_element_type=F32)
        refs[group + d][...] = term.astype(BF16)


def weight_terms(parts, slope):
    group = len(parts)
    width = parts[0].shape[-1]
    node_rows, feat_out = slope.shape
    return pl.pallas_call(
        term_kernel,
        in_specs=[spec_vmem()] * (group + 1),
        out_shape=[jax.ShapeDtypeStruct((width, feat_out), BF16)] * group,
        compiler_params=PARAMS,
        cost_estimate=cost(
            2 * node_rows * width * group * feat_out, 2 * 3 * node_rows * feat_out
        ),
    )(slope, *parts)


def scatter_kernel(group, index, *refs):
    total = refs[-1]
    outs = refs[-1 - SPAN : -1]
    backs = refs[-1 - SPAN - group : -1 - SPAN]
    vals = refs[: -1 - SPAN - group]
    size = outs[0].shape[0]
    block_rows = backs[0].shape[0]
    part = vals[-1].shape[0]
    total[...] = jnp.zeros_like(total)

    @pl.loop(0, part)
    def _(i):
        row = 0
        for val in vals:
            for b in range(0, val.shape[0], part):
                turned = backs[row // block_rows][row % block_rows + i].T
                for s in range(0, val.shape[1], 2):
                    rhs = jnp.concatenate([val[b + i, s], val[b + i, s + 1]], axis=1)
                    made = jnp.dot(turned, rhs, preferred_element_type=F32)
                    total[index[row + i, s]] += made[:, :TILE]
                    total[index[row + i, s + 1]] += made[:, TILE:]
                row += part

    for n in range(SPAN):
        outs[n][...] = total[pl.ds(n * size, size)].astype(BF16)


def sparse_scatter(index, vals, backs):
    group = len(backs)
    rows = sum(val.shape[0] for val in vals)
    slots = vals[0].shape[1]
    width = backs[0].shape[-1]
    return pl.pallas_call(
        functools.partial(scatter_kernel, group),
        in_specs=[spec_smem()] + [spec_vmem()] * (len(vals) + group),
        out_shape=[jax.ShapeDtypeStruct((rows, width, TILE), BF16)] * SPAN,
        scratch_shapes=[pltpu.VMEM((SPAN * rows + 1, width, TILE), F32)],
        compiler_params=PARAMS,
        cost_estimate=cost(
            rows * slots * TILE * TILE * width * 2,
            rows * slots * TILE * TILE * 2 + 6 * rows * TILE * width * 2,
        ),
    )(index, *vals, *backs)


def sum_kernel(bases, size, *refs):
    terms = refs[: len(bases)]
    for n, out_ref in enumerate(refs[len(bases) :]):
        total = jnp.zeros(out_ref.shape, F32)
        for ref, base in zip(terms, bases):
            total += ref[pl.ds(base + n * size, size)].astype(F32)
        out_ref[...] = total.astype(BF16)


def summed(terms, bases, size, count):
    shape = (size, *terms[0].shape[1:])
    return pl.pallas_call(
        functools.partial(sum_kernel, bases, size),
        in_specs=[spec_vmem()] * len(terms),
        out_shape=[jax.ShapeDtypeStruct(shape, BF16)] * count,
        compiler_params=PARAMS,
        cost_estimate=cost(0, count * math.prod(shape) * 2 * (len(terms) + 1)),
    )(*terms)


def place_kernel(rank_ref, *refs):
    out_ref = refs[-1]
    for d, ref in enumerate(refs[:-1]):
        blocks, width, tile = ref.shape
        start = pl.multiple_of((rank_ref[0] ^ d) * width, width)
        for b in range(blocks):
            out_ref[pl.ds(b * tile, tile), pl.ds(start, width)] = ref[b].T


def placed(rank, parts):
    blocks, width, tile = parts[0].shape
    shape = (blocks * tile, width * len(parts))
    return pl.pallas_call(
        place_kernel,
        in_specs=[spec_smem()] + [spec_vmem()] * len(parts),
        out_shape=jax.ShapeDtypeStruct(shape, BF16),
        compiler_params=PARAMS,
        cost_estimate=cost(0, 2 * 2 * shape[0] * shape[1]),
    )(rank, *parts)


def rows_kernel(scale, rank_ref, *refs):
    out_ref = refs[-1]
    for d, ref in enumerate(refs[:-1]):
        size = ref.shape[0]
        start = pl.multiple_of((rank_ref[0] ^ d) * size, size)
        out_ref[pl.ds(start, size), :] = ref[...].astype(F32) * scale


def rows_placed(rank, parts, scale):
    size, columns = parts[0].shape
    return pl.pallas_call(
        functools.partial(rows_kernel, scale),
        in_specs=[spec_smem()] + [spec_vmem()] * len(parts),
        out_shape=jax.ShapeDtypeStruct((size * len(parts), columns), F32),
        compiler_params=PARAMS,
        cost_estimate=cost(0, 6 * size * len(parts) * columns),
    )(rank, *parts)


def local(feats, weight, tile_vals, tile_cols, tile_count, cotangent):
    node_rows = feats.shape[0]
    cycle = lax.axis_size("blk")
    group = lax.axis_size("repl")
    assert group & (group - 1) == 0 and cycle & (cycle - 1) == 0
    block_rows = node_rows // TILE
    panel_blocks = block_rows * group
    spare = SPAN * panel_blocks
    far_side = group // 2
    where = jnp.reshape(lax.axis_index("repl"), (1,)).astype(jnp.int32)

    sent = split_columns(feats, tile_cols, tile_count, panel_blocks, cycle, group)
    mine = [sent[0]] + [swapped(sent[d], "repl", d) for d in range(1, group)]
    panel, index = joined_panel(mine, block_rows, spare)

    ahead = mirrored(panel, -2)
    beside = mirrored(panel, 1)
    behind = mirrored(after(panel, ahead), 2)
    relayed = mirrored(after(ahead, beside), 1)
    window = window_with([behind, panel, beside, ahead], [0, 2, 3, 4])
    window = window_with([relayed], [1], window)

    half = block_rows // 2
    ready = after(tile_vals, mine[1])
    own_vals = [ready[:half], ready[half:]]
    crossed = [swapped(after(part, panel), "repl", far_side) for part in own_vals]
    near = range(1, far_side)
    vals = own_vals + [swapped(after(tile_vals, panel), "repl", d) for d in near]
    vals += crossed + [swapped(part, "repl", d) for d in near for part in crossed]
    columns = sparse_gather(index, vals, window, group)
    aggregate = [columns[0]] + [swapped(columns[d], "repl", d) for d in range(1, group)]

    made = dense(aggregate, *prepared(after(weight, panel), group), cotangent)
    output, slope, backs = made[0], made[1], made[2:]
    backs = [backs[0]] + [swapped(backs[d], "repl", d) for d in range(1, group)]

    terms = weight_terms(aggregate, after(slope, backs[1]))
    arrived = [swapped(terms[d], "repl", d) for d in range(1, group)]
    backs[0] = after(backs[0], terms[0])
    chunk = terms[0].astype(F32)
    for term in arrived:
        chunk = chunk + term.astype(F32)
    rounded = lax.optimization_barrier(chunk.astype(BF16))

    far, relay, own, near_share, joined = sparse_scatter(index, vals, backs)
    relay_in = mirrored(relay, 1)
    far_in = mirrored(far, -2)
    near_in = mirrored(near_share, 1)
    (joined,) = summed([joined, relay_in], [0, 0], panel_blocks, 1)

    rounded = after(rounded, own)
    masks = [1 << n for n in range(cycle.bit_length() - 1)]
    masks[:2] = masks[1::-1]
    wait = None
    for mask in masks:
        other = swapped(rounded, "blk", mask)
        if mask == masks[-1]:
            joined_in = mirrored(after(joined, far_in, wait), 2)
            owned = summed([own, far_in, near_in, joined_in], [0] * 4, block_rows, group)
            gathered = [owned[0]] + [swapped(owned[d], "repl", d) for d in range(1, group)]
            rounded = after(rounded, gathered[1])
        chunk = rounded.astype(F32) + other.astype(F32)
        rounded = lax.optimization_barrier(chunk.astype(BF16))
        wait = rounded if wait is None else wait
    grad_rows = placed(where, gathered)
    chunks = [rounded] + [swapped(rounded, "repl", d) for d in range(1, group)]
    scale = 1.0 / math.sqrt(node_rows * group * cycle)
    weight_grad = rows_placed(where, chunks, scale)
    return (output, weight_grad, grad_rows)


def solution(mesh):
    in_specs = (
        P(("blk", "repl"), None),
        P(),
        P(("blk", "repl"), None, None, None),
        P(("blk", "repl"), None),
        P(("blk", "repl")),
        P(("blk", "repl"), None),
    )
    out_specs = (P(("blk", "repl"), None), P(), P(("blk", "repl"), None))
    return jax.shard_map(local, mesh=mesh, in_specs=in_specs, out_specs=out_specs, check_vma=False)
```

```python
import functools
import math

import jax
import jax.numpy as jnp
from jax import lax
from jax.experimental import pallas as pl
from jax.experimental.pallas import tpu as pltpu
from jax.sharding import PartitionSpec as P

TILE = 128
REACH = 2
SPAN = 2 * REACH + 1
VMEM_LIMIT = 32 * 1024 * 1024
PARAMS = pltpu.CompilerParams(vmem_limit_bytes=VMEM_LIMIT)
FIRST_PARAMS = pltpu.CompilerParams(vmem_limit_bytes=60 * 1024 * 1024)
EXTRA = 16
BF16 = jnp.bfloat16
F32 = jnp.float32


def mirrored(value, steps):
    count = lax.axis_size("blk")
    pairs = [(k, (k + steps * (1 - 2 * (k & 1))) % count) for k in range(count)]
    return lax.ppermute(value, "blk", pairs)


def after(value, *others):
    return lax.optimization_barrier((value, *others))[0]


def swapped(value, axis, mask):
    count = lax.axis_size(axis)
    return lax.ppermute(value, axis, [(source, source ^ mask) for source in range(count)])


def spec_smem():
    return pl.BlockSpec(memory_space=pltpu.SMEM)


def spec_vmem():
    return pl.BlockSpec(memory_space=pltpu.VMEM)


def spec_hbm():
    return pl.BlockSpec(memory_space=pltpu.HBM)


def cost(flops, bytes_accessed):
    return pl.CostEstimate(flops=flops, bytes_accessed=bytes_accessed, transcendentals=0)


def split_kernel(panel_blocks, cycle, cols_hbm, count_hbm, feats_hbm, *refs):
    cols_ref, count_ref, place_ref, sems = refs[-4:]
    outs = refs[:-4]
    group = len(outs)
    rows, width = feats_hbm.shape[0], outs[0].shape[1]
    block_rows, slots = cols_ref.shape
    rank = lax.axis_index("repl")
    center = lax.axis_index("blk")
    small = [
        pltpu.make_async_copy(cols_hbm, cols_ref, sems.at[group]),
        pltpu.make_async_copy(count_hbm, count_ref, sems.at[group + 1]),
    ]
    large = []
    for d, out_ref in enumerate(outs):
        start = pl.multiple_of((rank ^ d) * width, width)
        large.append(
            pltpu.make_async_copy(
                feats_hbm.at[:, pl.ds(start, width)], out_ref.at[pl.ds(0, rows)], sems.at[d]
            )
        )
    for copy in small + large:
        copy.start()
    for copy in small:
        copy.wait()
    sign = 1 - 2 * (center & 1)
    cols = cols_ref[...]
    offset = (cols // panel_blocks - center) & (cycle - 1)
    offset = jnp.where(offset > REACH, offset - cycle, offset) * sign
    place = (offset + REACH) * panel_blocks + (cols & (panel_blocks - 1))
    row = lax.broadcasted_iota(jnp.int32, cols.shape, 0)
    slot = lax.broadcasted_iota(jnp.int32, cols.shape, 1)
    live = jnp.zeros(cols.shape, jnp.int32)
    for r in range(block_rows):
        live = jnp.where(row == r, count_ref[r], live)
    place = jnp.where(slot < live, place, SPAN * panel_blocks)
    place_ref[...] = jnp.zeros_like(place_ref)
    place_ref[pl.ds(0, block_rows), pl.ds(0, slots)] = place.astype(F32)
    for out_ref in outs:
        out_ref[pl.ds(rows, EXTRA), :] = place_ref[...].astype(BF16)
    for copy in large:
        copy.wait()


def split_columns(feats, tile_cols, tile_count, panel_blocks, cycle, group):
    rows, columns = feats.shape
    width = columns // group
    return pl.pallas_call(
        functools.partial(split_kernel, panel_blocks, cycle),
        in_specs=[spec_hbm()] * 3,
        out_shape=[jax.ShapeDtypeStruct((rows + EXTRA, width), feats.dtype)] * group,
        scratch_shapes=[
            pltpu.VMEM(tile_cols.shape, jnp.int32),
            pltpu.SMEM(tile_count.shape, jnp.int32),
            pltpu.VMEM((EXTRA, width), F32),
            pltpu.SemaphoreType.DMA((group + 2,)),
        ],
        compiler_params=FIRST_PARAMS,
        cost_estimate=cost(0, 2 * rows * columns * 2),
    )(tile_cols, tile_count, feats)


def place_rows(piece, rows, block_rows, spare):
    place = piece[pl.ds(rows, EXTRA), :].astype(F32).astype(jnp.int32)[:block_rows]
    return jnp.where(place < spare, place ^ (lax.axis_index("repl") * block_rows), place)


def join_kernel(block_rows, spare, own_hbm, *refs):
    *pieces, panel_ref, index_ref, own_ref, sem = refs
    copy = pltpu.make_async_copy(own_hbm, own_ref, sem)
    copy.start()
    rows = own_ref.shape[0] - EXTRA
    for d, piece in enumerate(pieces, 1):
        panel_ref[pl.ds(d * rows, rows), :] = piece[pl.ds(0, rows), :]
        place = place_rows(piece, rows, block_rows, spare)
        index_ref[pl.ds(d * block_rows, block_rows), :] = place
    copy.wait()
    panel_ref[pl.ds(0, rows), :] = own_ref[pl.ds(0, rows), :]
    index_ref[pl.ds(0, block_rows), :] = place_rows(own_ref, rows, block_rows, spare)


def joined_panel(pieces, block_rows, spare):
    rows, width = pieces[0].shape
    count = len(pieces)
    shape = (count * (rows - EXTRA), width)
    panel, index = pl.pallas_call(
        functools.partial(join_kernel, block_rows, spare),
        in_specs=[spec_hbm()] + [spec_vmem()] * (count - 1),
        out_shape=[
            jax.ShapeDtypeStruct(shape, BF16),
            jax.ShapeDtypeStruct((count * block_rows, width), jnp.int32),
        ],
        scratch_shapes=[pltpu.VMEM((rows, width), BF16), pltpu.SemaphoreType.DMA(())],
        compiler_params=PARAMS,
        cost_estimate=cost(0, 4 * shape[0] * width),
    )(*pieces)
    return panel.reshape(-1, TILE, width), index


def window_kernel(places, *refs):
    pieces = refs[: len(places)]
    window, sems = refs[-2:]
    copies = [
        pltpu.make_async_copy(
            piece, window.at[pl.ds(place * piece.shape[0], piece.shape[0])], sems.at[n]
        )
        for n, (piece, place) in enumerate(zip(pieces, places))
    ]
    for copy in copies:
        copy.start()
    if len(places) > 1:
        window[window.shape[0] - 1] = jnp.zeros(window.shape[1:], window.dtype)
    for copy in copies:
        copy.wait()


def window_with(pieces, places, window=None):
    size, tile, width = pieces[0].shape
    begun = [] if window is None else [window]
    return pl.pallas_call(
        functools.partial(window_kernel, places),
        in_specs=[spec_vmem()] * len(pieces) + [spec_vmem()] * len(begun),
        out_specs=spec_vmem(),
        out_shape=jax.ShapeDtypeStruct((SPAN * size + 1, tile, width), BF16),
        input_output_aliases={len(pieces): 0} if begun else {},
        scratch_shapes=[pltpu.SemaphoreType.DMA((len(pieces),))],
        compiler_params=PARAMS,
        cost_estimate=cost(0, 4 * len(pieces) * size * tile * width),
    )(*pieces, *begun)


def gather_kernel(group, index, window, *refs):
    outs = refs[-group:]
    vals = refs[:-group]
    block_rows = outs[0].shape[0]
    part = vals[-1].shape[0]

    @pl.loop(0, part)
    def _(i):
        row = 0
        for val in vals:
            for b in range(0, val.shape[0], part):
                slots = range(val.shape[1])
                lhs = jnp.concatenate([val[b + i, s] for s in slots], axis=1)
                rhs = jnp.concatenate([window[index[row + i, s]] for s in slots], axis=0)
                made = jnp.dot(lhs, rhs, preferred_element_type=F32).astype(BF16)
                outs[row // block_rows][row % block_rows + i] = made
                row += part


def sparse_gather(index, vals, window, group):
    rows = sum(val.shape[0] for val in vals)
    slots = vals[0].shape[1]
    blocks, _, width = window.shape
    return pl.pallas_call(
        functools.partial(gather_kernel, group),
        in_specs=[spec_smem()] + [spec_vmem()] * (len(vals) + 1),
        out_shape=[jax.ShapeDtypeStruct((rows // group, TILE, width), BF16)] * group,
        compiler_params=PARAMS,
        cost_estimate=cost(
            rows * slots * TILE * TILE * width * 2,
            rows * slots * TILE * TILE * 2 + blocks * TILE * width * 2,
        ),
    )(index, window, *vals)


def prepare_kernel(group, weight_ref, rows_ref, turned_ref):
    width = weight_ref.shape[0] // group
    rank = lax.axis_index("repl")
    for d in range(group):
        start = pl.multiple_of((rank ^ d) * width, width)
        chunk = weight_ref[pl.ds(start, width), :]
        rows_ref[pl.ds(d * width, width), :] = chunk
        turned_ref[:, pl.ds(d * width, width)] = chunk.T


def prepared(weight, group):
    rows, columns = weight.shape
    return pl.pallas_call(
        functools.partial(prepare_kernel, group),
        in_specs=[spec_vmem()],
        out_shape=[
            jax.ShapeDtypeStruct((rows, columns), BF16),
            jax.ShapeDtypeStruct((columns, rows), BF16),
        ],
        compiler_params=PARAMS,
        cost_estimate=cost(0, 6 * rows * columns),
    )(weight)


def dense_kernel(group, *refs):
    parts = refs[:group]
    weight_ref, turned_ref, cotangent_ref, output_ref, slope_ref = refs[group : group + 5]
    backs = refs[group + 5 :]
    blocks, tile, width = parts[0].shape
    steps = 2
    blocks = blocks // steps
    rows = blocks * tile

    for g in range(steps):
        at = pl.ds(g * rows, rows)
        blocks_at = pl.ds(g * blocks, blocks)
        aggregate = jnp.concatenate([p[blocks_at].reshape(rows, width) for p in parts], axis=1)
        preact = jnp.dot(aggregate, weight_ref[...], preferred_element_type=F32)
        sigma = jax.nn.sigmoid(preact)
        output_ref[at, :] = (preact * sigma).astype(BF16)
        slope = sigma * (1.0 + preact * (1.0 - sigma))
        slope = (cotangent_ref[at, :].astype(F32) * slope).astype(BF16)
        slope_ref[at, :] = slope
        backward = jnp.dot(slope, turned_ref[...], preferred_element_type=F32).astype(BF16)
        for d in range(group):
            piece = backward[:, d * width : (d + 1) * width]
            backs[d][blocks_at] = piece.reshape(blocks, tile, width)


def dense(parts, weight, turned, cotangent):
    group = len(parts)
    node_rows, feat_out = cotangent.shape
    feat_in = weight.shape[0]
    return pl.pallas_call(
        functools.partial(dense_kernel, group),
        in_specs=[spec_vmem()] * (group + 3),
        out_shape=[jax.ShapeDtypeStruct((node_rows, feat_out), BF16)] * 2
        + [jax.ShapeDtypeStruct(parts[0].shape, BF16)] * group,
        compiler_params=PARAMS,
        cost_estimate=cost(
            4 * node_rows * feat_in * feat_out,
            2 * (5 * node_rows * feat_out + 2 * feat_in * feat_out),
        ),
    )(*parts, weight, turned, cotangent)


def term_kernel(slope_ref, *refs):
    group = len(refs) // 2
    slope = slope_ref[...]
    for d in range(group):
        part = refs[d][...].reshape(slope.shape[0], -1)
        term = lax.dot_general(part, slope, (((0,), (0,)), ((), ())), preferred_element_type=F32)
        refs[group + d][...] = term.astype(BF16)


def weight_terms(parts, slope):
    group = len(parts)
    width = parts[0].shape[-1]
    node_rows, feat_out = slope.shape
    return pl.pallas_call(
        term_kernel,
        in_specs=[spec_vmem()] * (group + 1),
        out_shape=[jax.ShapeDtypeStruct((width, feat_out), BF16)] * group,
        compiler_params=PARAMS,
        cost_estimate=cost(
            2 * node_rows * width * group * feat_out, 2 * 3 * node_rows * feat_out
        ),
    )(slope, *parts)


def scatter_kernel(group, index, *refs):
    total = refs[-1]
    outs = refs[-1 - SPAN : -1]
    backs = refs[-1 - SPAN - group : -1 - SPAN]
    vals = refs[: -1 - SPAN - group]
    size = outs[0].shape[0]
    block_rows = backs[0].shape[0]
    part = vals[-1].shape[0]
    total[...] = jnp.zeros_like(total)

    @pl.loop(0, part)
    def _(i):
        row = 0
        for val in vals:
            for b in range(0, val.shape[0], part):
                turned = backs[row // block_rows][row % block_rows + i].T
                for s in range(0, val.shape[1], 2):
                    rhs = jnp.concatenate([val[b + i, s], val[b + i, s + 1]], axis=1)
                    made = jnp.dot(turned, rhs, preferred_element_type=F32)
                    total[index[row + i, s]] += made[:, :TILE]
                    total[index[row + i, s + 1]] += made[:, TILE:]
                row += part

    for n in range(SPAN):
        outs[n][...] = total[pl.ds(n * size, size)].astype(BF16)


def sparse_scatter(index, vals, backs):
    group = len(backs)
    rows = sum(val.shape[0] for val in vals)
    slots = vals[0].shape[1]
    width = backs[0].shape[-1]
    return pl.pallas_call(
        functools.partial(scatter_kernel, group),
        in_specs=[spec_smem()] + [spec_vmem()] * (len(vals) + group),
        out_shape=[jax.ShapeDtypeStruct((rows, width, TILE), BF16)] * SPAN,
        scratch_shapes=[pltpu.VMEM((SPAN * rows + 1, width, TILE), F32)],
        compiler_params=PARAMS,
        cost_estimate=cost(
            rows * slots * TILE * TILE * width * 2,
            rows * slots * TILE * TILE * 2 + 6 * rows * TILE * width * 2,
        ),
    )(index, *vals, *backs)


def sum_kernel(bases, size, *refs):
    terms = refs[: len(bases)]
    for n, out_ref in enumerate(refs[len(bases) :]):
        total = jnp.zeros(out_ref.shape, F32)
        for ref, base in zip(terms, bases):
            total += ref[pl.ds(base + n * size, size)].astype(F32)
        out_ref[...] = total.astype(BF16)


def summed(terms, bases, size, count):
    shape = (size, *terms[0].shape[1:])
    return pl.pallas_call(
        functools.partial(sum_kernel, bases, size),
        in_specs=[spec_vmem()] * len(terms),
        out_shape=[jax.ShapeDtypeStruct(shape, BF16)] * count,
        compiler_params=PARAMS,
        cost_estimate=cost(0, count * math.prod(shape) * 2 * (len(terms) + 1)),
    )(*terms)


def place_kernel(rank_ref, *refs):
    out_ref = refs[-1]
    for d, ref in enumerate(refs[:-1]):
        blocks, width, tile = ref.shape
        start = pl.multiple_of((rank_ref[0] ^ d) * width, width)
        for b in range(blocks):
            out_ref[pl.ds(b * tile, tile), pl.ds(start, width)] = ref[b].T


def placed(rank, parts):
    blocks, width, tile = parts[0].shape
    shape = (blocks * tile, width * len(parts))
    return pl.pallas_call(
        place_kernel,
        in_specs=[spec_smem()] + [spec_vmem()] * len(parts),
        out_shape=jax.ShapeDtypeStruct(shape, BF16),
        compiler_params=PARAMS,
        cost_estimate=cost(0, 2 * 2 * shape[0] * shape[1]),
    )(rank, *parts)


def rows_kernel(scale, rank_ref, *refs):
    out_ref = refs[-1]
    for d, ref in enumerate(refs[:-1]):
        size = ref.shape[0]
        start = pl.multiple_of((rank_ref[0] ^ d) * size, size)
        out_ref[pl.ds(start, size), :] = ref[...].astype(F32) * scale


def rows_placed(rank, parts, scale):
    size, columns = parts[0].shape
    return pl.pallas_call(
        functools.partial(rows_kernel, scale),
        in_specs=[spec_smem()] + [spec_vmem()] * len(parts),
        out_shape=jax.ShapeDtypeStruct((size * len(parts), columns), F32),
        compiler_params=PARAMS,
        cost_estimate=cost(0, 6 * size * len(parts) * columns),
    )(rank, *parts)


def local(feats, weight, tile_vals, tile_cols, tile_count, cotangent):
    node_rows = feats.shape[0]
    cycle = lax.axis_size("blk")
    group = lax.axis_size("repl")
    assert group & (group - 1) == 0 and cycle & (cycle - 1) == 0
    block_rows = node_rows // TILE
    panel_blocks = block_rows * group
    spare = SPAN * panel_blocks
    far_side = group // 2
    where = jnp.reshape(lax.axis_index("repl"), (1,)).astype(jnp.int32)

    sent = split_columns(feats, tile_cols, tile_count, panel_blocks, cycle, group)
    mine = [sent[0]] + [swapped(sent[d], "repl", d) for d in range(1, group)]
    panel, index = joined_panel(mine, block_rows, spare)

    ahead = mirrored(panel, -2)
    beside = mirrored(panel, 1)
    behind = mirrored(after(panel, ahead), 2)
    relayed = mirrored(after(ahead, beside), 1)
    window = window_with([behind, panel, beside, ahead], [0, 2, 3, 4])
    window = window_with([relayed], [1], window)

    half = block_rows // 2
    ready = after(tile_vals, mine[far_side])
    own_vals = [ready[:half], ready[half:]]
    crossed = [swapped(part, "repl", far_side) for part in own_vals]
    near = range(1, far_side)
    vals = own_vals + [swapped(after(tile_vals, panel), "repl", d) for d in near]
    vals += crossed + [swapped(part, "repl", d) for d in near for part in crossed]
    columns = sparse_gather(index, vals, window, group)
    aggregate = [columns[0]] + [swapped(columns[d], "repl", d) for d in range(1, group)]

    made = dense(aggregate, *prepared(after(weight, panel), group), cotangent)
    output, slope, backs = made[0], made[1], made[2:]
    backs = [backs[0]] + [swapped(backs[d], "repl", d) for d in range(1, group)]

    terms = weight_terms(aggregate, after(slope, backs[1]))
    arrived = [swapped(terms[d], "repl", d) for d in range(1, group)]
    backs[0] = after(backs[0], terms[0])
    chunk = terms[0].astype(F32)
    for term in arrived:
        chunk = chunk + term.astype(F32)
    rounded = lax.optimization_barrier(chunk.astype(BF16))

    far, relay, own, near_share, joined = sparse_scatter(index, vals, backs)
    relay_in = mirrored(relay, 1)
    far_in = mirrored(far, -2)
    near_in = mirrored(near_share, 1)
    (joined,) = summed([joined, relay_in], [0, 0], panel_blocks, 1)
    joined_in = mirrored(after(joined, far_in), 2)
    owned = summed([own, far_in, near_in, joined_in], [0] * 4, block_rows, group)
    gathered = [owned[0]] + [swapped(owned[d], "repl", d) for d in range(1, group)]
    grad_rows = placed(where, gathered)

    rounded = after(rounded, own)
    masks = [1 << n for n in range(cycle.bit_length() - 1)]
    masks[:2] = masks[1::-1]
    waits = {masks[-1]: owned[0], masks[0]: joined}
    for mask in masks:
        other = swapped(rounded, "blk", mask)
        if mask in waits:
            rounded = after(rounded, waits[mask])
        chunk = rounded.astype(F32) + other.astype(F32)
        rounded = lax.optimization_barrier(chunk.astype(BF16))
    chunks = [rounded] + [swapped(rounded, "repl", d) for d in range(1, group)]
    scale = 1.0 / math.sqrt(node_rows * group * cycle)
    weight_grad = rows_placed(after(where, grad_rows), chunks, scale)
    return (output, weight_grad, grad_rows)


def solution(mesh):
    in_specs = (
        P(("blk", "repl"), None),
        P(),
        P(("blk", "repl"), None, None, None),
        P(("blk", "repl"), None),
        P(("blk", "repl")),
        P(("blk", "repl"), None),
    )
    out_specs = (P(("blk", "repl"), None), P(), P(("blk", "repl"), None))
    return jax.shard_map(local, mesh=mesh, in_specs=in_specs, out_specs=out_specs, check_vma=False)
```

```python
import functools
import math

import jax
import jax.numpy as jnp
from jax import lax
from jax.experimental import pallas as pl
from jax.experimental.pallas import tpu as pltpu
from jax.sharding import PartitionSpec as P

TILE = 128
REACH = 2
SPAN = 2 * REACH + 1
VMEM_LIMIT = 32 * 1024 * 1024
PARAMS = pltpu.CompilerParams(vmem_limit_bytes=VMEM_LIMIT)
FIRST_PARAMS = pltpu.CompilerParams(vmem_limit_bytes=60 * 1024 * 1024)
EXTRA = 16
BF16 = jnp.bfloat16
F32 = jnp.float32


def mirrored(value, steps):
    count = lax.axis_size("blk")
    pairs = [(k, (k + steps * (1 - 2 * (k & 1))) % count) for k in range(count)]
    return lax.ppermute(value, "blk", pairs)


def after(value, *others):
    return lax.optimization_barrier((value, *others))[0]


def swapped(value, axis, mask):
    count = lax.axis_size(axis)
    return lax.ppermute(value, axis, [(source, source ^ mask) for source in range(count)])


def spec_smem():
    return pl.BlockSpec(memory_space=pltpu.SMEM)


def spec_vmem():
    return pl.BlockSpec(memory_space=pltpu.VMEM)


def spec_hbm():
    return pl.BlockSpec(memory_space=pltpu.HBM)


def cost(flops, bytes_accessed):
    return pl.CostEstimate(flops=flops, bytes_accessed=bytes_accessed, transcendentals=0)


def split_kernel(panel_blocks, cycle, cols_hbm, count_hbm, feats_hbm, *refs):
    cols_ref, count_ref, place_ref, sems = refs[-4:]
    outs = refs[:-4]
    group = len(outs)
    rows, width = feats_hbm.shape[0], outs[0].shape[1]
    block_rows, slots = cols_ref.shape
    rank = lax.axis_index("repl")
    center = lax.axis_index("blk")
    small = [
        pltpu.make_async_copy(cols_hbm, cols_ref, sems.at[group]),
        pltpu.make_async_copy(count_hbm, count_ref, sems.at[group + 1]),
    ]
    large = []
    for d, out_ref in enumerate(outs):
        start = pl.multiple_of((rank ^ d) * width, width)
        large.append(
            pltpu.make_async_copy(
                feats_hbm.at[:, pl.ds(start, width)], out_ref.at[pl.ds(0, rows)], sems.at[d]
            )
        )
    for copy in small + large:
        copy.start()
    for copy in small:
        copy.wait()
    sign = 1 - 2 * (center & 1)
    cols = cols_ref[...]
    offset = (cols // panel_blocks - center) & (cycle - 1)
    offset = jnp.where(offset > REACH, offset - cycle, offset) * sign
    place = (offset + REACH) * panel_blocks + (cols & (panel_blocks - 1))
    row = lax.broadcasted_iota(jnp.int32, cols.shape, 0)
    slot = lax.broadcasted_iota(jnp.int32, cols.shape, 1)
    live = jnp.zeros(cols.shape, jnp.int32)
    for r in range(block_rows):
        live = jnp.where(row == r, count_ref[r], live)
    place = jnp.where(slot < live, place, SPAN * panel_blocks)
    place_ref[...] = jnp.zeros_like(place_ref)
    place_ref[pl.ds(0, block_rows), pl.ds(0, slots)] = place.astype(F32)
    for out_ref in outs:
        out_ref[pl.ds(rows, EXTRA), :] = place_ref[...].astype(BF16)
    for copy in large:
        copy.wait()


def split_columns(feats, tile_cols, tile_count, panel_blocks, cycle, group):
    rows, columns = feats.shape
    width = columns // group
    return pl.pallas_call(
        functools.partial(split_kernel, panel_blocks, cycle),
        in_specs=[spec_hbm()] * 3,
        out_shape=[jax.ShapeDtypeStruct((rows + EXTRA, width), feats.dtype)] * group,
        scratch_shapes=[
            pltpu.VMEM(tile_cols.shape, jnp.int32),
            pltpu.SMEM(tile_count.shape, jnp.int32),
            pltpu.VMEM((EXTRA, width), F32),
            pltpu.SemaphoreType.DMA((group + 2,)),
        ],
        compiler_params=FIRST_PARAMS,
        cost_estimate=cost(0, 2 * rows * columns * 2),
    )(tile_cols, tile_count, feats)


def place_rows(piece, rows, block_rows, spare):
    place = piece[pl.ds(rows, EXTRA), :].astype(F32).astype(jnp.int32)[:block_rows]
    return jnp.where(place < spare, place ^ (lax.axis_index("repl") * block_rows), place)


def join_kernel(block_rows, spare, own_hbm, *refs):
    *pieces, panel_ref, index_ref, own_ref, sem = refs
    copy = pltpu.make_async_copy(own_hbm, own_ref, sem)
    copy.start()
    rows = own_ref.shape[0] - EXTRA
    for d, piece in enumerate(pieces, 1):
        panel_ref[pl.ds(d * rows, rows), :] = piece[pl.ds(0, rows), :]
        place = place_rows(piece, rows, block_rows, spare)
        index_ref[pl.ds(d * block_rows, block_rows), :] = place
    copy.wait()
    panel_ref[pl.ds(0, rows), :] = own_ref[pl.ds(0, rows), :]
    index_ref[pl.ds(0, block_rows), :] = place_rows(own_ref, rows, block_rows, spare)


def joined_panel(pieces, block_rows, spare):
    rows, width = pieces[0].shape
    count = len(pieces)
    shape = (count * (rows - EXTRA), width)
    panel, index = pl.pallas_call(
        functools.partial(join_kernel, block_rows, spare),
        in_specs=[spec_hbm()] + [spec_vmem()] * (count - 1),
        out_shape=[
            jax.ShapeDtypeStruct(shape, BF16),
            jax.ShapeDtypeStruct((count * block_rows, width), jnp.int32),
        ],
        scratch_shapes=[pltpu.VMEM((rows, width), BF16), pltpu.SemaphoreType.DMA(())],
        compiler_params=PARAMS,
        cost_estimate=cost(0, 4 * shape[0] * width),
    )(*pieces)
    return panel.reshape(-1, TILE, width), index


def window_kernel(places, *refs):
    pieces = refs[: len(places)]
    window, sems = refs[-2:]
    copies = [
        pltpu.make_async_copy(
            piece, window.at[pl.ds(place * piece.shape[0], piece.shape[0])], sems.at[n]
        )
        for n, (piece, place) in enumerate(zip(pieces, places))
    ]
    for copy in copies:
        copy.start()
    if len(places) > 1:
        window[window.shape[0] - 1] = jnp.zeros(window.shape[1:], window.dtype)
    for copy in copies:
        copy.wait()


def window_with(pieces, places, window=None):
    size, tile, width = pieces[0].shape
    begun = [] if window is None else [window]
    return pl.pallas_call(
        functools.partial(window_kernel, places),
        in_specs=[spec_vmem()] * len(pieces) + [spec_vmem()] * len(begun),
        out_specs=spec_vmem(),
        out_shape=jax.ShapeDtypeStruct((SPAN * size + 1, tile, width), BF16),
        input_output_aliases={len(pieces): 0} if begun else {},
        scratch_shapes=[pltpu.SemaphoreType.DMA((len(pieces),))],
        compiler_params=PARAMS,
        cost_estimate=cost(0, 4 * len(pieces) * size * tile * width),
    )(*pieces, *begun)


def gather_kernel(group, index, window, *refs):
    outs = refs[-group:]
    vals = refs[:-group]
    block_rows = outs[0].shape[0]
    part = vals[-1].shape[0]

    @pl.loop(0, part)
    def _(i):
        row = 0
        for val in vals:
            for b in range(0, val.shape[0], part):
                slots = range(val.shape[1])
                lhs = jnp.concatenate([val[b + i, s] for s in slots], axis=1)
                rhs = jnp.concatenate([window[index[row + i, s]] for s in slots], axis=0)
                made = jnp.dot(lhs, rhs, preferred_element_type=F32).astype(BF16)
                outs[row // block_rows][row % block_rows + i] = made
                row += part


def sparse_gather(index, vals, window, group):
    rows = sum(val.shape[0] for val in vals)
    slots = vals[0].shape[1]
    blocks, _, width = window.shape
    return pl.pallas_call(
        functools.partial(gather_kernel, group),
        in_specs=[spec_smem()] + [spec_vmem()] * (len(vals) + 1),
        out_shape=[jax.ShapeDtypeStruct((rows // group, TILE, width), BF16)] * group,
        compiler_params=PARAMS,
        cost_estimate=cost(
            rows * slots * TILE * TILE * width * 2,
            rows * slots * TILE * TILE * 2 + blocks * TILE * width * 2,
        ),
    )(index, window, *vals)


def prepare_kernel(group, weight_ref, rows_ref, turned_ref):
    width = weight_ref.shape[0] // group
    rank = lax.axis_index("repl")
    for d in range(group):
        start = pl.multiple_of((rank ^ d) * width, width)
        chunk = weight_ref[pl.ds(start, width), :]
        rows_ref[pl.ds(d * width, width), :] = chunk
        turned_ref[:, pl.ds(d * width, width)] = chunk.T


def prepared(weight, group):
    rows, columns = weight.shape
    return pl.pallas_call(
        functools.partial(prepare_kernel, group),
        in_specs=[spec_vmem()],
        out_shape=[
            jax.ShapeDtypeStruct((rows, columns), BF16),
            jax.ShapeDtypeStruct((columns, rows), BF16),
        ],
        compiler_params=PARAMS,
        cost_estimate=cost(0, 6 * rows * columns),
    )(weight)


def dense_kernel(group, *refs):
    parts = refs[:group]
    weight_ref, turned_ref, cotangent_ref, output_ref, slope_ref = refs[group : group + 5]
    backs = refs[group + 5 :]
    blocks, tile, width = parts[0].shape
    steps = 2
    blocks = blocks // steps
    rows = blocks * tile

    for g in range(steps):
        at = pl.ds(g * rows, rows)
        blocks_at = pl.ds(g * blocks, blocks)
        aggregate = jnp.concatenate([p[blocks_at].reshape(rows, width) for p in parts], axis=1)
        preact = jnp.dot(aggregate, weight_ref[...], preferred_element_type=F32)
        sigma = jax.nn.sigmoid(preact)
        output_ref[at, :] = (preact * sigma).astype(BF16)
        slope = sigma * (1.0 + preact * (1.0 - sigma))
        slope = (cotangent_ref[at, :].astype(F32) * slope).astype(BF16)
        slope_ref[at, :] = slope
        backward = jnp.dot(slope, turned_ref[...], preferred_element_type=F32).astype(BF16)
        for d in range(group):
            piece = backward[:, d * width : (d + 1) * width]
            backs[d][blocks_at] = piece.reshape(blocks, tile, width)


def dense(parts, weight, turned, cotangent):
    group = len(parts)
    node_rows, feat_out = cotangent.shape
    feat_in = weight.shape[0]
    return pl.pallas_call(
        functools.partial(dense_kernel, group),
        in_specs=[spec_vmem()] * (group + 3),
        out_shape=[jax.ShapeDtypeStruct((node_rows, feat_out), BF16)] * 2
        + [jax.ShapeDtypeStruct(parts[0].shape, BF16)] * group,
        compiler_params=PARAMS,
        cost_estimate=cost(
            4 * node_rows * feat_in * feat_out,
            2 * (5 * node_rows * feat_out + 2 * feat_in * feat_out),
        ),
    )(*parts, weight, turned, cotangent)


def term_kernel(slope_ref, *refs):
    *parts, kept_ref, given_ref = refs
    slope = slope_ref[...]
    for d, part in enumerate(parts):
        part = part[...].reshape(slope.shape[0], -1)
        term = lax.dot_general(part, slope, (((0,), (0,)), ((), ())), preferred_element_type=F32)
        out_ref = given_ref if d & 1 else kept_ref
        out_ref[pl.ds(d // 2 * term.shape[0], term.shape[0]), :] = term.astype(BF16)


def weight_terms(parts, slope):
    group = len(parts)
    width = parts[0].shape[-1]
    node_rows, feat_out = slope.shape
    return pl.pallas_call(
        term_kernel,
        in_specs=[spec_vmem()] * (group + 1),
        out_shape=[jax.ShapeDtypeStruct((group // 2 * width, feat_out), BF16)] * 2,
        compiler_params=PARAMS,
        cost_estimate=cost(
            2 * node_rows * width * group * feat_out, 2 * 3 * node_rows * feat_out
        ),
    )(slope, *parts)


def halve_kernel(own_first, kept_ref, arrived_ref, keep_ref, give_ref):
    size = keep_ref.shape[0]
    kept = own_first()
    for out_ref, at in ((keep_ref, kept), (give_ref, 1 - kept)):
        rows = pl.ds(pl.multiple_of(at * size, size), size)
        total = kept_ref[rows, :].astype(F32) + arrived_ref[rows, :].astype(F32)
        out_ref[...] = total.astype(BF16)


def halved(kept, arrived, which):
    rows, columns = kept.shape
    return pl.pallas_call(
        functools.partial(halve_kernel, which),
        in_specs=[spec_vmem()] * 2,
        out_shape=[jax.ShapeDtypeStruct((rows // 2, columns), BF16)] * 2,
        compiler_params=PARAMS,
        cost_estimate=cost(0, 6 * rows * columns),
    )(kept, arrived)


def unite_kernel(which, own_ref, other_ref, out_ref):
    size = own_ref.shape[0]
    at = which()
    out_ref[pl.ds(pl.multiple_of(at * size, size), size), :] = own_ref[...]
    out_ref[pl.ds(pl.multiple_of((1 - at) * size, size), size), :] = other_ref[...]


def united(own, other, which):
    rows, columns = own.shape
    return pl.pallas_call(
        functools.partial(unite_kernel, which),
        in_specs=[spec_vmem()] * 2,
        out_shape=jax.ShapeDtypeStruct((2 * rows, columns), BF16),
        compiler_params=PARAMS,
        cost_estimate=cost(0, 8 * rows * columns),
    )(own, other)


def side():
    return lax.axis_index("repl") // (lax.axis_size("repl") // 2)


def parity():
    return lax.axis_index("blk") & 1


def parity_on_side():
    return parity() ^ side()


def scatter_kernel(group, index, *refs):
    total = refs[-1]
    outs = refs[-1 - SPAN : -1]
    backs = refs[-1 - SPAN - group : -1 - SPAN]
    vals = refs[: -1 - SPAN - group]
    size = outs[0].shape[0]
    block_rows = backs[0].shape[0]
    part = vals[-1].shape[0]
    total[...] = jnp.zeros_like(total)

    @pl.loop(0, part)
    def _(i):
        row = 0
        for val in vals:
            for b in range(0, val.shape[0], part):
                turned = backs[row // block_rows][row % block_rows + i].T
                for s in range(0, val.shape[1], 2):
                    rhs = jnp.concatenate([val[b + i, s], val[b + i, s + 1]], axis=1)
                    made = jnp.dot(turned, rhs, preferred_element_type=F32)
                    total[index[row + i, s]] += made[:, :TILE]
                    total[index[row + i, s + 1]] += made[:, TILE:]
                row += part

    for n in range(SPAN):
        outs[n][...] = total[pl.ds(n * size, size)].astype(BF16)


def sparse_scatter(index, vals, backs):
    group = len(backs)
    rows = sum(val.shape[0] for val in vals)
    slots = vals[0].shape[1]
    width = backs[0].shape[-1]
    return pl.pallas_call(
        functools.partial(scatter_kernel, group),
        in_specs=[spec_smem()] + [spec_vmem()] * (len(vals) + group),
        out_shape=[jax.ShapeDtypeStruct((rows, width, TILE), BF16)] * SPAN,
        scratch_shapes=[pltpu.VMEM((SPAN * rows + 1, width, TILE), F32)],
        compiler_params=PARAMS,
        cost_estimate=cost(
            rows * slots * TILE * TILE * width * 2,
            rows * slots * TILE * TILE * 2 + 6 * rows * TILE * width * 2,
        ),
    )(index, *vals, *backs)


def sum_kernel(bases, size, *refs):
    terms = refs[: len(bases)]
    for n, out_ref in enumerate(refs[len(bases) :]):
        total = jnp.zeros(out_ref.shape, F32)
        for ref, base in zip(terms, bases):
            total += ref[pl.ds(base + n * size, size)].astype(F32)
        out_ref[...] = total.astype(BF16)


def summed(terms, bases, size, count):
    shape = (size, *terms[0].shape[1:])
    return pl.pallas_call(
        functools.partial(sum_kernel, bases, size),
        in_specs=[spec_vmem()] * len(terms),
        out_shape=[jax.ShapeDtypeStruct(shape, BF16)] * count,
        compiler_params=PARAMS,
        cost_estimate=cost(0, count * math.prod(shape) * 2 * (len(terms) + 1)),
    )(*terms)


def turn_kernel(*refs):
    count = len(refs) // 2
    for part, out_ref in zip(refs[:count], refs[count:]):
        tile = part.shape[2]
        for b in range(part.shape[0]):
            out_ref[pl.ds(b * tile, tile), :] = part[b].T


def turned(parts):
    blocks, width, tile = parts[0].shape
    return pl.pallas_call(
        turn_kernel,
        in_specs=[spec_vmem()] * len(parts),
        out_shape=[jax.ShapeDtypeStruct((blocks * tile, width), BF16)] * len(parts),
        compiler_params=PARAMS,
        cost_estimate=cost(0, 4 * len(parts) * blocks * tile * width),
    )(*parts)


def place_kernel(*refs):
    *parts, out_ref = refs
    rank = lax.axis_index("repl")
    for d, part in enumerate(parts):
        width = part.shape[1]
        start = pl.multiple_of((rank ^ d) * width, width)
        if len(part.shape) == 2:
            out_ref[:, pl.ds(start, width)] = part[...]
            continue
        tile = part.shape[2]
        for b in range(part.shape[0]):
            out_ref[pl.ds(b * tile, tile), pl.ds(start, width)] = part[b].T


def placed(parts):
    blocks, width, tile = parts[0].shape
    shape = (blocks * tile, width * len(parts))
    return pl.pallas_call(
        place_kernel,
        in_specs=[spec_vmem()] * len(parts),
        out_shape=jax.ShapeDtypeStruct(shape, BF16),
        compiler_params=PARAMS,
        cost_estimate=cost(0, 2 * 2 * shape[0] * shape[1]),
    )(*parts)


def rows_kernel(scale, *refs):
    out_ref = refs[-1]
    size = refs[0].shape[0]
    core = lax.axis_index("repl") & 1
    even = parity()
    for n, ref in enumerate(refs[:-1]):
        start = ((core ^ (n & 1)) + 2 * (even ^ (n // 2))) * size
        out_ref[pl.ds(pl.multiple_of(start, size), size), :] = ref[...].astype(F32) * scale


def rows_placed(parts, scale):
    size, columns = parts[0].shape
    return pl.pallas_call(
        functools.partial(rows_kernel, scale),
        in_specs=[spec_vmem()] * len(parts),
        out_shape=jax.ShapeDtypeStruct((size * len(parts), columns), F32),
        compiler_params=PARAMS,
        cost_estimate=cost(0, 6 * size * len(parts) * columns),
    )(*parts)


def local(feats, weight, tile_vals, tile_cols, tile_count, cotangent):
    node_rows = feats.shape[0]
    cycle = lax.axis_size("blk")
    group = lax.axis_size("repl")
    assert group == 4 and cycle & (cycle - 1) == 0
    block_rows = node_rows // TILE
    panel_blocks = block_rows * group
    spare = SPAN * panel_blocks
    far_side = group // 2

    sent = split_columns(feats, tile_cols, tile_count, panel_blocks, cycle, group)
    mine = [sent[0]] + [swapped(sent[d], "repl", d) for d in range(1, group)]
    panel, index = joined_panel(mine, block_rows, spare)

    ahead = mirrored(panel, -2)
    beside = mirrored(panel, 1)
    behind = mirrored(after(panel, ahead), 2)
    relayed = mirrored(after(ahead, beside), 1)
    window = window_with([behind, panel, beside, ahead], [0, 2, 3, 4])
    window = window_with([relayed], [1], window)

    half = block_rows // 2
    ready = after(tile_vals, mine[far_side])
    own_vals = [ready[:half], ready[half:]]
    crossed = [swapped(part, "repl", far_side) for part in own_vals]
    near = range(1, far_side)
    vals = own_vals + [swapped(after(tile_vals, panel), "repl", d) for d in near]
    vals += crossed + [swapped(part, "repl", d) for d in near for part in crossed]
    columns = sparse_gather(index, vals, window, group)
    aggregate = [columns[0]] + [swapped(columns[d], "repl", d) for d in range(1, group)]

    made = dense(aggregate, *prepared(after(weight, panel), group), cotangent)
    output, slope, backs = made[0], made[1], made[2:]
    backs = [backs[0]] + [swapped(backs[d], "repl", d) for d in range(1, group)]

    kept, given = weight_terms(aggregate, slope)
    arrived = swapped(given, "repl", 1)
    kept, given = halved(after(kept, *backs[1:]), arrived, parity_on_side)
    backs[0] = after(backs[0], given)
    arrived = swapped(given, "blk", 1)

    far, relay, own, near_share, joined = sparse_scatter(index, vals, backs)
    relay_in = mirrored(relay, 1)
    far_in = mirrored(far, -2)
    near_in = mirrored(near_share, 1)
    joined = summed([joined, relay_in], [0, 0], panel_blocks // 2, 2)
    kept, given = halved(after(kept, own), arrived, side)
    chunk = kept.astype(F32) + swapped(given, "repl", far_side).astype(F32)
    rounded = lax.optimization_barrier(chunk.astype(BF16))
    mask = 2
    while mask < cycle:
        chunk = rounded.astype(F32) + swapped(rounded, "blk", mask).astype(F32)
        rounded = lax.optimization_barrier(chunk.astype(BF16))
        if mask == 2:
            joined = [after(part, far_in) for part in joined]
        mask *= 2
    owned = []
    for part in reversed(joined):
        joined_in = mirrored(part, 2)
        base = 0 if owned else part.shape[0]
        terms = [after(own, *owned[:1]), far_in, near_in, joined_in]
        owned = [*summed(terms, [base, base, base, 0], block_rows, far_side), *owned]
    gathered = [owned[0]] + [swapped(owned[d], "repl", d) for d in range(1, group)]
    grad_rows = placed([*gathered[:far_side], *turned(gathered[far_side:])])

    first = united(rounded, swapped(rounded, "repl", far_side), side)
    second = swapped(first, "blk", 1)
    parts = [first, swapped(first, "repl", 1), second, swapped(second, "repl", 1)]
    weight_grad = rows_placed(parts, 1.0 / math.sqrt(node_rows * group * cycle))
    return (output, weight_grad, grad_rows)


def solution(mesh):
    in_specs = (
        P(("blk", "repl"), None),
        P(),
        P(("blk", "repl"), None, None, None),
        P(("blk", "repl"), None),
        P(("blk", "repl")),
        P(("blk", "repl"), None),
    )
    out_specs = (P(("blk", "repl"), None), P(), P(("blk", "repl"), None))
    return jax.shard_map(local, mesh=mesh, in_specs=in_specs, out_specs=out_specs, check_vma=False)
```

```python
import functools
import math

import jax
import jax.numpy as jnp
from jax import lax
from jax.experimental import pallas as pl
from jax.experimental.pallas import tpu as pltpu
from jax.sharding import PartitionSpec as P

TILE = 128
REACH = 2
SPAN = 2 * REACH + 1
VMEM_LIMIT = 32 * 1024 * 1024
PARAMS = pltpu.CompilerParams(vmem_limit_bytes=VMEM_LIMIT)
FIRST_PARAMS = pltpu.CompilerParams(vmem_limit_bytes=60 * 1024 * 1024)
EXTRA = 16
BF16 = jnp.bfloat16
F32 = jnp.float32


def mirrored(value, steps):
    count = lax.axis_size("blk")
    pairs = [(k, (k + steps * (1 - 2 * (k & 1))) % count) for k in range(count)]
    return lax.ppermute(value, "blk", pairs)


def after(value, *others):
    return lax.optimization_barrier((value, *others))[0]


def swapped(value, axis, mask):
    count = lax.axis_size(axis)
    return lax.ppermute(value, axis, [(source, source ^ mask) for source in range(count)])


def spec_smem():
    return pl.BlockSpec(memory_space=pltpu.SMEM)


def spec_vmem():
    return pl.BlockSpec(memory_space=pltpu.VMEM)


def spec_hbm():
    return pl.BlockSpec(memory_space=pltpu.HBM)


def cost(flops, bytes_accessed):
    return pl.CostEstimate(flops=flops, bytes_accessed=bytes_accessed, transcendentals=0)


def split_kernel(panel_blocks, cycle, cols_hbm, count_hbm, feats_hbm, *refs):
    cols_ref, count_ref, place_ref, sems = refs[-4:]
    outs = refs[:-4]
    group = len(outs)
    rows, width = feats_hbm.shape[0], outs[0].shape[1]
    block_rows, slots = cols_ref.shape
    rank = lax.axis_index("repl")
    center = lax.axis_index("blk")
    small = [
        pltpu.make_async_copy(cols_hbm, cols_ref, sems.at[group]),
        pltpu.make_async_copy(count_hbm, count_ref, sems.at[group + 1]),
    ]
    large = []
    for d, out_ref in enumerate(outs):
        start = pl.multiple_of((rank ^ d) * width, width)
        large.append(
            pltpu.make_async_copy(
                feats_hbm.at[:, pl.ds(start, width)], out_ref.at[pl.ds(0, rows)], sems.at[d]
            )
        )
    for copy in small + large:
        copy.start()
    for copy in small:
        copy.wait()
    sign = 1 - 2 * (center & 1)
    cols = cols_ref[...]
    offset = (cols // panel_blocks - center) & (cycle - 1)
    offset = jnp.where(offset > REACH, offset - cycle, offset) * sign
    place = (offset + REACH) * panel_blocks + (cols & (panel_blocks - 1))
    row = lax.broadcasted_iota(jnp.int32, cols.shape, 0)
    slot = lax.broadcasted_iota(jnp.int32, cols.shape, 1)
    live = jnp.zeros(cols.shape, jnp.int32)
    for r in range(block_rows):
        live = jnp.where(row == r, count_ref[r], live)
    place = jnp.where(slot < live, place, SPAN * panel_blocks)
    place_ref[...] = jnp.zeros_like(place_ref)
    place_ref[pl.ds(0, block_rows), pl.ds(0, slots)] = place.astype(F32)
    for out_ref in outs:
        out_ref[pl.ds(rows, EXTRA), :] = place_ref[...].astype(BF16)
    for copy in large:
        copy.wait()


def split_columns(feats, tile_cols, tile_count, panel_blocks, cycle, group):
    rows, columns = feats.shape
    width = columns // group
    return pl.pallas_call(
        functools.partial(split_kernel, panel_blocks, cycle),
        in_specs=[spec_hbm()] * 3,
        out_shape=[jax.ShapeDtypeStruct((rows + EXTRA, width), feats.dtype)] * group,
        scratch_shapes=[
            pltpu.VMEM(tile_cols.shape, jnp.int32),
            pltpu.SMEM(tile_count.shape, jnp.int32),
            pltpu.VMEM((EXTRA, width), F32),
            pltpu.SemaphoreType.DMA((group + 2,)),
        ],
        compiler_params=FIRST_PARAMS,
        cost_estimate=cost(0, 2 * rows * columns * 2),
    )(tile_cols, tile_count, feats)


def place_rows(piece, rows, block_rows, spare):
    place = piece[pl.ds(rows, EXTRA), :].astype(F32).astype(jnp.int32)[:block_rows]
    return jnp.where(place < spare, place ^ (lax.axis_index("repl") * block_rows), place)


def join_kernel(block_rows, spare, own_hbm, *refs):
    *pieces, panel_ref, index_ref, own_ref, sem = refs
    copy = pltpu.make_async_copy(own_hbm, own_ref, sem)
    copy.start()
    rows = own_ref.shape[0] - EXTRA
    for d, piece in enumerate(pieces, 1):
        panel_ref[pl.ds(d * rows, rows), :] = piece[pl.ds(0, rows), :]
        place = place_rows(piece, rows, block_rows, spare)
        index_ref[pl.ds(d * block_rows, block_rows), :] = place
    copy.wait()
    panel_ref[pl.ds(0, rows), :] = own_ref[pl.ds(0, rows), :]
    index_ref[pl.ds(0, block_rows), :] = place_rows(own_ref, rows, block_rows, spare)


def joined_panel(pieces, block_rows, spare):
    rows, width = pieces[0].shape
    count = len(pieces)
    shape = (count * (rows - EXTRA), width)
    panel, index = pl.pallas_call(
        functools.partial(join_kernel, block_rows, spare),
        in_specs=[spec_hbm()] + [spec_vmem()] * (count - 1),
        out_shape=[
            jax.ShapeDtypeStruct(shape, BF16),
            jax.ShapeDtypeStruct((count * block_rows, width), jnp.int32),
        ],
        scratch_shapes=[pltpu.VMEM((rows, width), BF16), pltpu.SemaphoreType.DMA(())],
        compiler_params=PARAMS,
        cost_estimate=cost(0, 4 * shape[0] * width),
    )(*pieces)
    return panel.reshape(-1, TILE, width), index


def window_kernel(places, *refs):
    pieces = refs[: len(places)]
    window, sems = refs[-2:]
    copies = [
        pltpu.make_async_copy(
            piece, window.at[pl.ds(place * piece.shape[0], piece.shape[0])], sems.at[n]
        )
        for n, (piece, place) in enumerate(zip(pieces, places))
    ]
    for copy in copies:
        copy.start()
    if len(places) > 1:
        window[window.shape[0] - 1] = jnp.zeros(window.shape[1:], window.dtype)
    for copy in copies:
        copy.wait()


def window_with(pieces, places, window=None):
    size, tile, width = pieces[0].shape
    begun = [] if window is None else [window]
    return pl.pallas_call(
        functools.partial(window_kernel, places),
        in_specs=[spec_vmem()] * len(pieces) + [spec_vmem()] * len(begun),
        out_specs=spec_vmem(),
        out_shape=jax.ShapeDtypeStruct((SPAN * size + 1, tile, width), BF16),
        input_output_aliases={len(pieces): 0} if begun else {},
        scratch_shapes=[pltpu.SemaphoreType.DMA((len(pieces),))],
        compiler_params=PARAMS,
        cost_estimate=cost(0, 4 * len(pieces) * size * tile * width),
    )(*pieces, *begun)


def gather_kernel(group, index, window, *refs):
    outs = refs[-group:]
    vals = refs[:-group]
    block_rows = outs[0].shape[0]
    part = vals[-1].shape[0]

    @pl.loop(0, part)
    def _(i):
        row = 0
        for val in vals:
            for b in range(0, val.shape[0], part):
                slots = range(val.shape[1])
                lhs = jnp.concatenate([val[b + i, s] for s in slots], axis=1)
                rhs = jnp.concatenate([window[index[row + i, s]] for s in slots], axis=0)
                made = jnp.dot(lhs, rhs, preferred_element_type=F32).astype(BF16)
                outs[row // block_rows][row % block_rows + i] = made
                row += part


def sparse_gather(index, vals, window, group):
    rows = sum(val.shape[0] for val in vals)
    slots = vals[0].shape[1]
    blocks, _, width = window.shape
    return pl.pallas_call(
        functools.partial(gather_kernel, group),
        in_specs=[spec_smem()] + [spec_vmem()] * (len(vals) + 1),
        out_shape=[jax.ShapeDtypeStruct((rows // group, TILE, width), BF16)] * group,
        compiler_params=PARAMS,
        cost_estimate=cost(
            rows * slots * TILE * TILE * width * 2,
            rows * slots * TILE * TILE * 2 + blocks * TILE * width * 2,
        ),
    )(index, window, *vals)


def prepare_kernel(group, weight_ref, rows_ref, turned_ref):
    width = weight_ref.shape[0] // group
    rank = lax.axis_index("repl")
    for d in range(group):
        start = pl.multiple_of((rank ^ d) * width, width)
        chunk = weight_ref[pl.ds(start, width), :]
        rows_ref[pl.ds(d * width, width), :] = chunk
        turned_ref[:, pl.ds(d * width, width)] = chunk.T


def prepared(weight, group):
    rows, columns = weight.shape
    return pl.pallas_call(
        functools.partial(prepare_kernel, group),
        in_specs=[spec_vmem()],
        out_shape=[
            jax.ShapeDtypeStruct((rows, columns), BF16),
            jax.ShapeDtypeStruct((columns, rows), BF16),
        ],
        compiler_params=PARAMS,
        cost_estimate=cost(0, 6 * rows * columns),
    )(weight)


def dense_kernel(group, *refs):
    parts = refs[:group]
    weight_ref, turned_ref, cotangent_ref, output_ref, slope_ref = refs[group : group + 5]
    backs = refs[group + 5 :]
    blocks, tile, width = parts[0].shape
    steps = 2
    blocks = blocks // steps
    rows = blocks * tile

    for g in range(steps):
        at = pl.ds(g * rows, rows)
        blocks_at = pl.ds(g * blocks, blocks)
        aggregate = jnp.concatenate([p[blocks_at].reshape(rows, width) for p in parts], axis=1)
        preact = jnp.dot(aggregate, weight_ref[...], preferred_element_type=F32)
        sigma = jax.nn.sigmoid(preact)
        output_ref[at, :] = (preact * sigma).astype(BF16)
        slope = sigma * (1.0 + preact * (1.0 - sigma))
        slope = (cotangent_ref[at, :].astype(F32) * slope).astype(BF16)
        slope_ref[at, :] = slope
        backward = jnp.dot(slope, turned_ref[...], preferred_element_type=F32).astype(BF16)
        for d in range(group):
            piece = backward[:, d * width : (d + 1) * width]
            backs[d][blocks_at] = piece.reshape(blocks, tile, width)


def dense(parts, weight, turned, cotangent):
    group = len(parts)
    node_rows, feat_out = cotangent.shape
    feat_in = weight.shape[0]
    return pl.pallas_call(
        functools.partial(dense_kernel, group),
        in_specs=[spec_vmem()] * (group + 3),
        out_shape=[jax.ShapeDtypeStruct((node_rows, feat_out), BF16)] * 2
        + [jax.ShapeDtypeStruct(parts[0].shape, BF16)] * group,
        compiler_params=PARAMS,
        cost_estimate=cost(
            4 * node_rows * feat_in * feat_out,
            2 * (5 * node_rows * feat_out + 2 * feat_in * feat_out),
        ),
    )(*parts, weight, turned, cotangent)


def term_kernel(slope_ref, *refs):
    *parts, kept_ref, given_ref = refs
    slope = slope_ref[...]
    for d, part in enumerate(parts):
        part = part[...].reshape(slope.shape[0], -1)
        term = lax.dot_general(part, slope, (((0,), (0,)), ((), ())), preferred_element_type=F32)
        out_ref = given_ref if d & 1 else kept_ref
        out_ref[pl.ds(d // 2 * term.shape[0], term.shape[0]), :] = term.astype(BF16)


def weight_terms(parts, slope):
    group = len(parts)
    width = parts[0].shape[-1]
    node_rows, feat_out = slope.shape
    return pl.pallas_call(
        term_kernel,
        in_specs=[spec_vmem()] * (group + 1),
        out_shape=[jax.ShapeDtypeStruct((group // 2 * width, feat_out), BF16)] * 2,
        compiler_params=PARAMS,
        cost_estimate=cost(
            2 * node_rows * width * group * feat_out, 2 * 3 * node_rows * feat_out
        ),
    )(slope, *parts)


def halve_kernel(own_first, kept_ref, arrived_ref, keep_ref, give_ref):
    size = keep_ref.shape[0]
    kept = own_first()
    for out_ref, at in ((keep_ref, kept), (give_ref, 1 - kept)):
        rows = pl.ds(pl.multiple_of(at * size, size), size)
        total = kept_ref[rows, :].astype(F32) + arrived_ref[rows, :].astype(F32)
        out_ref[...] = total.astype(BF16)


def halved(kept, arrived, which):
    rows, columns = kept.shape
    return pl.pallas_call(
        functools.partial(halve_kernel, which),
        in_specs=[spec_vmem()] * 2,
        out_shape=[jax.ShapeDtypeStruct((rows // 2, columns), BF16)] * 2,
        compiler_params=PARAMS,
        cost_estimate=cost(0, 6 * rows * columns),
    )(kept, arrived)


def side():
    return lax.axis_index("repl") // (lax.axis_size("repl") // 2)


def parity():
    return lax.axis_index("blk") & 1


def parity_on_side():
    return parity() ^ side()


def scatter_kernel(group, index, *refs):
    total = refs[-1]
    outs = refs[-1 - SPAN : -1]
    backs = refs[-1 - SPAN - group : -1 - SPAN]
    vals = refs[: -1 - SPAN - group]
    size = outs[0].shape[0]
    block_rows = backs[0].shape[0]
    part = vals[-1].shape[0]
    total[...] = jnp.zeros_like(total)

    @pl.loop(0, part)
    def _(i):
        row = 0
        for val in vals:
            for b in range(0, val.shape[0], part):
                turned = backs[row // block_rows][row % block_rows + i].T
                for s in range(0, val.shape[1], 2):
                    rhs = jnp.concatenate([val[b + i, s], val[b + i, s + 1]], axis=1)
                    made = jnp.dot(turned, rhs, preferred_element_type=F32)
                    total[index[row + i, s]] += made[:, :TILE]
                    total[index[row + i, s + 1]] += made[:, TILE:]
                row += part

    for n in range(SPAN):
        outs[n][...] = total[pl.ds(n * size, size)].astype(BF16)


def sparse_scatter(index, vals, backs):
    group = len(backs)
    rows = sum(val.shape[0] for val in vals)
    slots = vals[0].shape[1]
    width = backs[0].shape[-1]
    return pl.pallas_call(
        functools.partial(scatter_kernel, group),
        in_specs=[spec_smem()] + [spec_vmem()] * (len(vals) + group),
        out_shape=[jax.ShapeDtypeStruct((rows, width, TILE), BF16)] * SPAN,
        scratch_shapes=[pltpu.VMEM((SPAN * rows + 1, width, TILE), F32)],
        compiler_params=PARAMS,
        cost_estimate=cost(
            rows * slots * TILE * TILE * width * 2,
            rows * slots * TILE * TILE * 2 + 6 * rows * TILE * width * 2,
        ),
    )(index, *vals, *backs)


def sum_kernel(bases, size, *refs):
    terms = refs[: len(bases)]
    for n, out_ref in enumerate(refs[len(bases) :]):
        total = jnp.zeros(out_ref.shape, F32)
        for ref, base in zip(terms, bases):
            total += ref[pl.ds(base + n * size, size)].astype(F32)
        out_ref[...] = total.astype(BF16)


def summed(terms, bases, size, count):
    shape = (size, *terms[0].shape[1:])
    return pl.pallas_call(
        functools.partial(sum_kernel, bases, size),
        in_specs=[spec_vmem()] * len(terms),
        out_shape=[jax.ShapeDtypeStruct(shape, BF16)] * count,
        compiler_params=PARAMS,
        cost_estimate=cost(0, count * math.prod(shape) * 2 * (len(terms) + 1)),
    )(*terms)


def turn_kernel(*refs):
    count = len(refs) // 2
    for part, out_ref in zip(refs[:count], refs[count:]):
        tile = part.shape[2]
        for b in range(part.shape[0]):
            out_ref[pl.ds(b * tile, tile), :] = part[b].T


def turned(parts):
    blocks, width, tile = parts[0].shape
    return pl.pallas_call(
        turn_kernel,
        in_specs=[spec_vmem()] * len(parts),
        out_shape=[jax.ShapeDtypeStruct((blocks * tile, width), BF16)] * len(parts),
        compiler_params=PARAMS,
        cost_estimate=cost(0, 4 * len(parts) * blocks * tile * width),
    )(*parts)


def place_kernel(*refs):
    *parts, out_ref = refs
    rank = lax.axis_index("repl")
    for d, part in enumerate(parts):
        width = part.shape[1]
        start = pl.multiple_of((rank ^ d) * width, width)
        if len(part.shape) == 2:
            out_ref[:, pl.ds(start, width)] = part[...]
            continue
        tile = part.shape[2]
        for b in range(part.shape[0]):
            out_ref[pl.ds(b * tile, tile), pl.ds(start, width)] = part[b].T


def placed(parts):
    blocks, width, tile = parts[0].shape
    shape = (blocks * tile, width * len(parts))
    return pl.pallas_call(
        place_kernel,
        in_specs=[spec_vmem()] * len(parts),
        out_shape=jax.ShapeDtypeStruct(shape, BF16),
        compiler_params=PARAMS,
        cost_estimate=cost(0, 2 * 2 * shape[0] * shape[1]),
    )(*parts)


def rows_kernel(scale, *refs):
    out_ref = refs[-1]
    size = refs[0].shape[0]
    core = lax.axis_index("repl") & 1
    even = parity()
    for n, ref in enumerate(refs[:-1]):
        start = ((core ^ (n & 1)) + 2 * (even ^ (n // 2))) * size
        out_ref[pl.ds(pl.multiple_of(start, size), size), :] = ref[...].astype(F32) * scale


def rows_placed(parts, scale):
    size, columns = parts[0].shape
    return pl.pallas_call(
        functools.partial(rows_kernel, scale),
        in_specs=[spec_vmem()] * len(parts),
        out_shape=jax.ShapeDtypeStruct((size * len(parts), columns), F32),
        compiler_params=PARAMS,
        cost_estimate=cost(0, 6 * size * len(parts) * columns),
    )(*parts)


def local(feats, weight, tile_vals, tile_cols, tile_count, cotangent):
    node_rows = feats.shape[0]
    cycle = lax.axis_size("blk")
    group = lax.axis_size("repl")
    assert group == 4 and cycle & (cycle - 1) == 0
    block_rows = node_rows // TILE
    panel_blocks = block_rows * group
    spare = SPAN * panel_blocks
    far_side = group // 2

    sent = split_columns(feats, tile_cols, tile_count, panel_blocks, cycle, group)
    mine = [sent[0]] + [swapped(sent[d], "repl", d) for d in range(1, group)]
    panel, index = joined_panel(mine, block_rows, spare)

    ahead = mirrored(panel, -2)
    beside = mirrored(panel, 1)
    behind = mirrored(after(panel, ahead), 2)
    relayed = mirrored(after(ahead, beside), 1)
    window = window_with([behind, panel, beside, ahead], [0, 2, 3, 4])
    window = window_with([relayed], [1], window)

    half = block_rows // 2
    ready = after(tile_vals, mine[far_side])
    own_vals = [ready[:half], ready[half:]]
    crossed = [swapped(part, "repl", far_side) for part in own_vals]
    near = range(1, far_side)
    vals = own_vals + [swapped(after(tile_vals, panel), "repl", d) for d in near]
    vals += crossed + [swapped(part, "repl", d) for d in near for part in crossed]
    columns = sparse_gather(index, vals, window, group)
    aggregate = [columns[0]] + [swapped(columns[d], "repl", d) for d in range(1, group)]

    made = dense(aggregate, *prepared(after(weight, panel), group), cotangent)
    output, slope, backs = made[0], made[1], made[2:]
    backs = [backs[0]] + [swapped(backs[d], "repl", d) for d in range(1, group)]

    kept, given = weight_terms(aggregate, slope)
    arrived = swapped(given, "repl", 1)
    kept, given = halved(after(kept, backs[1]), arrived, parity_on_side)
    backs[0] = after(backs[0], given)
    arrived = swapped(given, "blk", 1)

    far, relay, own, near_share, joined = sparse_scatter(index, vals, backs)
    chunk = after(kept, own).astype(F32) + arrived.astype(F32)
    sums = [lax.optimization_barrier(chunk.astype(BF16))]
    mask = cycle // 2
    relay_in = mirrored(relay, 1)
    far_in = mirrored(after(far, sums[0]), -2)
    joined = summed([joined, relay_in], [0, 0], panel_blocks // 2, 2)
    summed_first = joined[0]
    joined = [after(part, far_in) for part in joined]
    while mask > 1:
        other = swapped(sums[-1], "blk", mask)
        if mask == 2:
            near_share = after(near_share, sums[-1])
            sums[-1] = after(sums[-1], summed_first)
        chunk = sums[-1].astype(F32) + other.astype(F32)
        sums.append(lax.optimization_barrier(chunk.astype(BF16)))
        mask //= 2
    near_in = mirrored(near_share, 1)
    owned = []
    for part in reversed(joined):
        joined_in = mirrored(part, 2)
        base = 0 if owned else part.shape[0]
        terms = [after(own, *owned[:1]), far_in, near_in, joined_in]
        owned = [*summed(terms, [base, base, base, 0], block_rows, far_side), *owned]
    gathered = [owned[0]] + [swapped(owned[d], "repl", d) for d in range(1, group)]
    grad_rows = placed([*gathered[:far_side], *turned(gathered[far_side:])])

    chunk = sums[-1].astype(F32) + swapped(sums[-1], "repl", far_side).astype(F32)
    first = chunk.astype(BF16)
    second = after(swapped(first, "blk", 1), owned[far_side])
    parts = [first, swapped(first, "repl", 1), second, swapped(second, "repl", 1)]
    weight_grad = rows_placed(parts, 1.0 / math.sqrt(node_rows * group * cycle))
    return (output, weight_grad, grad_rows)


def solution(mesh):
    in_specs = (
        P(("blk", "repl"), None),
        P(),
        P(("blk", "repl"), None, None, None),
        P(("blk", "repl"), None),
        P(("blk", "repl")),
        P(("blk", "repl"), None),
    )
    out_specs = (P(("blk", "repl"), None), P(), P(("blk", "repl"), None))
    return jax.shard_map(local, mesh=mesh, in_specs=in_specs, out_specs=out_specs, check_vma=False)
```

```python
import functools
import math

import jax
import jax.numpy as jnp
from jax import lax
from jax.experimental import pallas as pl
from jax.experimental.pallas import tpu as pltpu
from jax.sharding import PartitionSpec as P

TILE = 128
REACH = 2
SPAN = 2 * REACH + 1
VMEM_LIMIT = 32 * 1024 * 1024
PARAMS = pltpu.CompilerParams(vmem_limit_bytes=VMEM_LIMIT)
FIRST_PARAMS = pltpu.CompilerParams(vmem_limit_bytes=60 * 1024 * 1024)
EXTRA = 16
BF16 = jnp.bfloat16
F32 = jnp.float32


def mirrored(value, steps):
    count = lax.axis_size("blk")
    pairs = [(k, (k + steps * (1 - 2 * (k & 1))) % count) for k in range(count)]
    return lax.ppermute(value, "blk", pairs)


def after(value, *others):
    return lax.optimization_barrier((value, *others))[0]


def swapped(value, axis, mask):
    count = lax.axis_size(axis)
    return lax.ppermute(value, axis, [(source, source ^ mask) for source in range(count)])


def spec_smem():
    return pl.BlockSpec(memory_space=pltpu.SMEM)


def spec_vmem():
    return pl.BlockSpec(memory_space=pltpu.VMEM)


def spec_hbm():
    return pl.BlockSpec(memory_space=pltpu.HBM)


def cost(flops, bytes_accessed):
    return pl.CostEstimate(flops=flops, bytes_accessed=bytes_accessed, transcendentals=0)


def split_kernel(panel_blocks, cycle, cols_hbm, count_hbm, feats_hbm, *refs):
    cols_ref, count_ref, place_ref, sems = refs[-4:]
    outs = refs[:-4]
    group = len(outs)
    rows, width = feats_hbm.shape[0], outs[0].shape[1]
    block_rows, slots = cols_ref.shape
    rank = lax.axis_index("repl")
    center = lax.axis_index("blk")
    small = [
        pltpu.make_async_copy(cols_hbm, cols_ref, sems.at[group]),
        pltpu.make_async_copy(count_hbm, count_ref, sems.at[group + 1]),
    ]
    large = []
    for d, out_ref in enumerate(outs):
        start = pl.multiple_of((rank ^ d) * width, width)
        large.append(
            pltpu.make_async_copy(
                feats_hbm.at[:, pl.ds(start, width)], out_ref.at[pl.ds(0, rows)], sems.at[d]
            )
        )
    for copy in small + large:
        copy.start()
    for copy in small:
        copy.wait()
    sign = 1 - 2 * (center & 1)
    cols = cols_ref[...]
    offset = (cols // panel_blocks - center) & (cycle - 1)
    offset = jnp.where(offset > REACH, offset - cycle, offset) * sign
    place = (offset + REACH) * panel_blocks + (cols & (panel_blocks - 1))
    row = lax.broadcasted_iota(jnp.int32, cols.shape, 0)
    slot = lax.broadcasted_iota(jnp.int32, cols.shape, 1)
    live = jnp.zeros(cols.shape, jnp.int32)
    for r in range(block_rows):
        live = jnp.where(row == r, count_ref[r], live)
    place = jnp.where(slot < live, place, SPAN * panel_blocks)
    place_ref[...] = jnp.zeros_like(place_ref)
    place_ref[pl.ds(0, block_rows), pl.ds(0, slots)] = place.astype(F32)
    for out_ref in outs:
        out_ref[pl.ds(rows, EXTRA), :] = place_ref[...].astype(BF16)
    for copy in large:
        copy.wait()


def split_columns(feats, tile_cols, tile_count, panel_blocks, cycle, group):
    rows, columns = feats.shape
    width = columns // group
    return pl.pallas_call(
        functools.partial(split_kernel, panel_blocks, cycle),
        in_specs=[spec_hbm()] * 3,
        out_shape=[jax.ShapeDtypeStruct((rows + EXTRA, width), feats.dtype)] * group,
        scratch_shapes=[
            pltpu.VMEM(tile_cols.shape, jnp.int32),
            pltpu.SMEM(tile_count.shape, jnp.int32),
            pltpu.VMEM((EXTRA, width), F32),
            pltpu.SemaphoreType.DMA((group + 2,)),
        ],
        compiler_params=FIRST_PARAMS,
        cost_estimate=cost(0, 2 * rows * columns * 2),
    )(tile_cols, tile_count, feats)


def place_rows(piece, rows, block_rows, spare):
    place = piece[pl.ds(rows, EXTRA), :].astype(F32).astype(jnp.int32)[:block_rows]
    return jnp.where(place < spare, place ^ (lax.axis_index("repl") * block_rows), place)


def join_kernel(block_rows, spare, own_hbm, *refs):
    *pieces, panel_ref, index_ref, own_ref, sem = refs
    copy = pltpu.make_async_copy(own_hbm, own_ref, sem)
    copy.start()
    rows = own_ref.shape[0] - EXTRA
    for d, piece in enumerate(pieces, 1):
        panel_ref[pl.ds(d * rows, rows), :] = piece[pl.ds(0, rows), :]
        place = place_rows(piece, rows, block_rows, spare)
        index_ref[pl.ds(d * block_rows, block_rows), :] = place
    copy.wait()
    panel_ref[pl.ds(0, rows), :] = own_ref[pl.ds(0, rows), :]
    index_ref[pl.ds(0, block_rows), :] = place_rows(own_ref, rows, block_rows, spare)


def joined_panel(pieces, block_rows, spare):
    rows, width = pieces[0].shape
    count = len(pieces)
    shape = (count * (rows - EXTRA), width)
    panel, index = pl.pallas_call(
        functools.partial(join_kernel, block_rows, spare),
        in_specs=[spec_hbm()] + [spec_vmem()] * (count - 1),
        out_shape=[
            jax.ShapeDtypeStruct(shape, BF16),
            jax.ShapeDtypeStruct((count * block_rows, width), jnp.int32),
        ],
        scratch_shapes=[pltpu.VMEM((rows, width), BF16), pltpu.SemaphoreType.DMA(())],
        compiler_params=PARAMS,
        cost_estimate=cost(0, 4 * shape[0] * width),
    )(*pieces)
    return panel.reshape(-1, TILE, width), index


def window_kernel(places, *refs):
    pieces = refs[: len(places)]
    window, sems = refs[-2:]
    copies = [
        pltpu.make_async_copy(
            piece, window.at[pl.ds(place * piece.shape[0], piece.shape[0])], sems.at[n]
        )
        for n, (piece, place) in enumerate(zip(pieces, places))
    ]
    for copy in copies:
        copy.start()
    if len(places) > 1:
        window[window.shape[0] - 1] = jnp.zeros(window.shape[1:], window.dtype)
    for copy in copies:
        copy.wait()


def window_with(pieces, places, window=None):
    size, tile, width = pieces[0].shape
    begun = [] if window is None else [window]
    return pl.pallas_call(
        functools.partial(window_kernel, places),
        in_specs=[spec_vmem()] * len(pieces) + [spec_vmem()] * len(begun),
        out_specs=spec_vmem(),
        out_shape=jax.ShapeDtypeStruct((SPAN * size + 1, tile, width), BF16),
        input_output_aliases={len(pieces): 0} if begun else {},
        scratch_shapes=[pltpu.SemaphoreType.DMA((len(pieces),))],
        compiler_params=PARAMS,
        cost_estimate=cost(0, 4 * len(pieces) * size * tile * width),
    )(*pieces, *begun)


def gather_kernel(group, index, window, *refs):
    outs = refs[-group:]
    vals = refs[:-group]
    block_rows = outs[0].shape[0]
    part = vals[-1].shape[0]

    @pl.loop(0, part)
    def _(i):
        row = 0
        for val in vals:
            for b in range(0, val.shape[0], part):
                slots = range(val.shape[1])
                lhs = jnp.concatenate([val[b + i, s] for s in slots], axis=1)
                rhs = jnp.concatenate([window[index[row + i, s]] for s in slots], axis=0)
                made = jnp.dot(lhs, rhs, preferred_element_type=F32).astype(BF16)
                outs[row // block_rows][row % block_rows + i] = made
                row += part


def sparse_gather(index, vals, window, group):
    rows = sum(val.shape[0] for val in vals)
    slots = vals[0].shape[1]
    blocks, _, width = window.shape
    return pl.pallas_call(
        functools.partial(gather_kernel, group),
        in_specs=[spec_smem()] + [spec_vmem()] * (len(vals) + 1),
        out_shape=[jax.ShapeDtypeStruct((rows // group, TILE, width), BF16)] * group,
        compiler_params=PARAMS,
        cost_estimate=cost(
            rows * slots * TILE * TILE * width * 2,
            rows * slots * TILE * TILE * 2 + blocks * TILE * width * 2,
        ),
    )(index, window, *vals)


def prepare_kernel(group, weight_ref, rows_ref, turned_ref):
    width = weight_ref.shape[0] // group
    rank = lax.axis_index("repl")
    for d in range(group):
        start = pl.multiple_of((rank ^ d) * width, width)
        chunk = weight_ref[pl.ds(start, width), :]
        rows_ref[pl.ds(d * width, width), :] = chunk
        turned_ref[:, pl.ds(d * width, width)] = chunk.T


def prepared(weight, group):
    rows, columns = weight.shape
    return pl.pallas_call(
        functools.partial(prepare_kernel, group),
        in_specs=[spec_vmem()],
        out_shape=[
            jax.ShapeDtypeStruct((rows, columns), BF16),
            jax.ShapeDtypeStruct((columns, rows), BF16),
        ],
        compiler_params=PARAMS,
        cost_estimate=cost(0, 6 * rows * columns),
    )(weight)


def dense_kernel(group, *refs):
    parts = refs[:group]
    weight_ref, turned_ref, cotangent_ref, output_ref, slope_ref = refs[group : group + 5]
    backs = refs[group + 5 :]
    blocks, tile, width = parts[0].shape
    steps = 2
    blocks = blocks // steps
    rows = blocks * tile

    for g in range(steps):
        at = pl.ds(g * rows, rows)
        blocks_at = pl.ds(g * blocks, blocks)
        aggregate = jnp.concatenate([p[blocks_at].reshape(rows, width) for p in parts], axis=1)
        preact = jnp.dot(aggregate, weight_ref[...], preferred_element_type=F32)
        sigma = jax.nn.sigmoid(preact)
        output_ref[at, :] = (preact * sigma).astype(BF16)
        slope = sigma * (1.0 + preact * (1.0 - sigma))
        slope = (cotangent_ref[at, :].astype(F32) * slope).astype(BF16)
        slope_ref[at, :] = slope
        backward = jnp.dot(slope, turned_ref[...], preferred_element_type=F32).astype(BF16)
        for d in range(group):
            piece = backward[:, d * width : (d + 1) * width]
            backs[d][blocks_at] = piece.reshape(blocks, tile, width)


def dense(parts, weight, turned, cotangent):
    group = len(parts)
    node_rows, feat_out = cotangent.shape
    feat_in = weight.shape[0]
    return pl.pallas_call(
        functools.partial(dense_kernel, group),
        in_specs=[spec_vmem()] * (group + 3),
        out_shape=[jax.ShapeDtypeStruct((node_rows, feat_out), BF16)] * 2
        + [jax.ShapeDtypeStruct(parts[0].shape, BF16)] * group,
        compiler_params=PARAMS,
        cost_estimate=cost(
            4 * node_rows * feat_in * feat_out,
            2 * (5 * node_rows * feat_out + 2 * feat_in * feat_out),
        ),
    )(*parts, weight, turned, cotangent)


def term_kernel(slope_ref, *refs):
    *parts, kept_ref, given_ref = refs
    slope = slope_ref[...]
    for d, part in enumerate(parts):
        part = part[...].reshape(slope.shape[0], -1)
        term = lax.dot_general(part, slope, (((0,), (0,)), ((), ())), preferred_element_type=F32)
        out_ref = given_ref if d & 1 else kept_ref
        out_ref[pl.ds(d // 2 * term.shape[0], term.shape[0]), :] = term.astype(BF16)


def weight_terms(parts, slope):
    group = len(parts)
    width = parts[0].shape[-1]
    node_rows, feat_out = slope.shape
    return pl.pallas_call(
        term_kernel,
        in_specs=[spec_vmem()] * (group + 1),
        out_shape=[jax.ShapeDtypeStruct((group // 2 * width, feat_out), BF16)] * 2,
        compiler_params=PARAMS,
        cost_estimate=cost(
            2 * node_rows * width * group * feat_out, 2 * 3 * node_rows * feat_out
        ),
    )(slope, *parts)


def halve_kernel(own_first, kept_ref, arrived_ref, keep_ref, give_ref):
    size = keep_ref.shape[0]
    kept = own_first()
    for out_ref, at in ((keep_ref, kept), (give_ref, 1 - kept)):
        rows = pl.ds(pl.multiple_of(at * size, size), size)
        total = kept_ref[rows, :].astype(F32) + arrived_ref[rows, :].astype(F32)
        out_ref[...] = total.astype(BF16)


def halved(kept, arrived, which):
    rows, columns = kept.shape
    return pl.pallas_call(
        functools.partial(halve_kernel, which),
        in_specs=[spec_vmem()] * 2,
        out_shape=[jax.ShapeDtypeStruct((rows // 2, columns), BF16)] * 2,
        compiler_params=PARAMS,
        cost_estimate=cost(0, 6 * rows * columns),
    )(kept, arrived)


def side():
    return lax.axis_index("repl") // (lax.axis_size("repl") // 2)


def parity():
    return lax.axis_index("blk") & 1


def parity_on_side():
    return parity() ^ side()


def scatter_kernel(group, index, *refs):
    total = refs[-1]
    outs = refs[-1 - SPAN : -1]
    backs = refs[-1 - SPAN - group : -1 - SPAN]
    vals = refs[: -1 - SPAN - group]
    size = outs[0].shape[0]
    block_rows = backs[0].shape[0]
    part = vals[-1].shape[0]
    total[...] = jnp.zeros_like(total)

    @pl.loop(0, part)
    def _(i):
        row = 0
        for val in vals:
            for b in range(0, val.shape[0], part):
                turned = backs[row // block_rows][row % block_rows + i].T
                for s in range(0, val.shape[1], 2):
                    rhs = jnp.concatenate([val[b + i, s], val[b + i, s + 1]], axis=1)
                    made = jnp.dot(turned, rhs, preferred_element_type=F32)
                    total[index[row + i, s]] += made[:, :TILE]
                    total[index[row + i, s + 1]] += made[:, TILE:]
                row += part

    for n in range(SPAN):
        outs[n][...] = total[pl.ds(n * size, size)].astype(BF16)


def sparse_scatter(index, vals, backs):
    group = len(backs)
    rows = sum(val.shape[0] for val in vals)
    slots = vals[0].shape[1]
    width = backs[0].shape[-1]
    return pl.pallas_call(
        functools.partial(scatter_kernel, group),
        in_specs=[spec_smem()] + [spec_vmem()] * (len(vals) + group),
        out_shape=[jax.ShapeDtypeStruct((rows, width, TILE), BF16)] * SPAN,
        scratch_shapes=[pltpu.VMEM((SPAN * rows + 1, width, TILE), F32)],
        compiler_params=PARAMS,
        cost_estimate=cost(
            rows * slots * TILE * TILE * width * 2,
            rows * slots * TILE * TILE * 2 + 6 * rows * TILE * width * 2,
        ),
    )(index, *vals, *backs)


def sum_kernel(bases, size, *refs):
    terms = refs[: len(bases)]
    for n, out_ref in enumerate(refs[len(bases) :]):
        total = jnp.zeros(out_ref.shape, F32)
        for ref, base in zip(terms, bases):
            total += ref[pl.ds(base + n * size, size)].astype(F32)
        out_ref[...] = total.astype(BF16)


def summed(terms, bases, size, count):
    shape = (size, *terms[0].shape[1:])
    return pl.pallas_call(
        functools.partial(sum_kernel, bases, size),
        in_specs=[spec_vmem()] * len(terms),
        out_shape=[jax.ShapeDtypeStruct(shape, BF16)] * count,
        compiler_params=PARAMS,
        cost_estimate=cost(0, count * math.prod(shape) * 2 * (len(terms) + 1)),
    )(*terms)


def turn_kernel(*refs):
    count = len(refs) // 2
    for part, out_ref in zip(refs[:count], refs[count:]):
        tile = part.shape[2]
        for b in range(part.shape[0]):
            out_ref[pl.ds(b * tile, tile), :] = part[b].T


def turned(parts):
    blocks, width, tile = parts[0].shape
    return pl.pallas_call(
        turn_kernel,
        in_specs=[spec_vmem()] * len(parts),
        out_shape=[jax.ShapeDtypeStruct((blocks * tile, width), BF16)] * len(parts),
        compiler_params=PARAMS,
        cost_estimate=cost(0, 4 * len(parts) * blocks * tile * width),
    )(*parts)


def place_kernel(*refs):
    *parts, out_ref = refs
    rank = lax.axis_index("repl")
    for d, part in enumerate(parts):
        width = part.shape[1]
        start = pl.multiple_of((rank ^ d) * width, width)
        if len(part.shape) == 2:
            out_ref[:, pl.ds(start, width)] = part[...]
            continue
        tile = part.shape[2]
        for b in range(part.shape[0]):
            out_ref[pl.ds(b * tile, tile), pl.ds(start, width)] = part[b].T


def placed(parts):
    blocks, width, tile = parts[0].shape
    shape = (blocks * tile, width * len(parts))
    return pl.pallas_call(
        place_kernel,
        in_specs=[spec_vmem()] * len(parts),
        out_shape=jax.ShapeDtypeStruct(shape, BF16),
        compiler_params=PARAMS,
        cost_estimate=cost(0, 2 * 2 * shape[0] * shape[1]),
    )(*parts)


def rows_kernel(scale, *refs):
    out_ref = refs[-1]
    size = refs[0].shape[0]
    core = lax.axis_index("repl") & 1
    even = parity()
    for n, ref in enumerate(refs[:-1]):
        start = ((core ^ (n & 1)) + 2 * (even ^ (n // 2))) * size
        out_ref[pl.ds(pl.multiple_of(start, size), size), :] = ref[...].astype(F32) * scale


def rows_placed(parts, scale):
    size, columns = parts[0].shape
    return pl.pallas_call(
        functools.partial(rows_kernel, scale),
        in_specs=[spec_vmem()] * len(parts),
        out_shape=jax.ShapeDtypeStruct((size * len(parts), columns), F32),
        compiler_params=PARAMS,
        cost_estimate=cost(0, 6 * size * len(parts) * columns),
    )(*parts)


def local(feats, weight, tile_vals, tile_cols, tile_count, cotangent):
    node_rows = feats.shape[0]
    cycle = lax.axis_size("blk")
    group = lax.axis_size("repl")
    assert group == 4 and cycle & (cycle - 1) == 0
    block_rows = node_rows // TILE
    panel_blocks = block_rows * group
    spare = SPAN * panel_blocks
    far_side = group // 2

    sent = split_columns(feats, tile_cols, tile_count, panel_blocks, cycle, group)
    mine = [sent[0]] + [swapped(sent[d], "repl", d) for d in range(1, group)]
    panel, index = joined_panel(mine, block_rows, spare)

    ahead = mirrored(panel, -2)
    beside = mirrored(panel, 1)
    behind = mirrored(after(panel, ahead), 2)
    relayed = mirrored(after(ahead, beside), 1)
    window = window_with([behind, panel, beside, ahead], [0, 2, 3, 4])
    window = window_with([relayed], [1], window)

    half = block_rows // 2
    ready = after(tile_vals, mine[far_side])
    own_vals = [ready[:half], ready[half:]]
    crossed = [swapped(part, "repl", far_side) for part in own_vals]
    near = range(1, far_side)
    vals = own_vals + [swapped(after(tile_vals, panel), "repl", d) for d in near]
    vals += crossed + [swapped(part, "repl", d) for d in near for part in crossed]
    columns = sparse_gather(index, vals, window, group)
    aggregate = [columns[0]] + [swapped(columns[d], "repl", d) for d in range(1, group)]

    made = dense(aggregate, *prepared(after(weight, panel), group), cotangent)
    output, slope, backs = made[0], made[1], made[2:]
    backs = [backs[0]] + [swapped(backs[d], "repl", d) for d in range(1, group)]

    kept, given = weight_terms(aggregate, slope)
    arrived = swapped(given, "repl", 1)
    kept, given = halved(after(kept, backs[1]), arrived, parity_on_side)
    backs[0] = after(backs[0], given)
    arrived = swapped(given, "blk", 1)

    far, relay, own, near_share, joined = sparse_scatter(index, vals, backs)
    chunk = after(kept, own).astype(F32) + arrived.astype(F32)
    sums = [lax.optimization_barrier(chunk.astype(BF16))]
    mask = cycle // 2
    relay_in = mirrored(relay, 1)
    joined = summed([joined, relay_in], [0, 0], panel_blocks // 2, 2)
    summed_first = joined[0]
    while mask > 1:
        other = swapped(sums[-1], "blk", mask)
        if mask == 2:
            near_share = after(near_share, sums[-1])
        chunk = sums[-1].astype(F32) + other.astype(F32)
        sums.append(lax.optimization_barrier(chunk.astype(BF16)))
        mask //= 2
    near_in = mirrored(near_share, 1)
    far_in = mirrored(after(far, sums[1]), -2)
    owned = []
    for part in reversed(joined):
        joined_in = mirrored(part, 2)
        base = 0 if owned else part.shape[0]
        terms = [after(own, *owned[:1]), far_in, near_in, joined_in]
        owned = [*summed(terms, [base, base, base, 0], block_rows, far_side), *owned]
    gathered = [owned[0]] + [swapped(owned[d], "repl", d) for d in range(1, group)]
    grad_rows = placed([*gathered[:far_side], *turned(gathered[far_side:])])

    chunk = sums[-1].astype(F32) + swapped(sums[-1], "repl", far_side).astype(F32)
    first = chunk.astype(BF16)
    second = after(swapped(first, "blk", 1), owned[far_side])
    parts = [first, swapped(first, "repl", 1), second, swapped(second, "repl", 1)]
    weight_grad = rows_placed(parts, 1.0 / math.sqrt(node_rows * group * cycle))
    return (output, weight_grad, grad_rows)


def solution(mesh):
    in_specs = (
        P(("blk", "repl"), None),
        P(),
        P(("blk", "repl"), None, None, None),
        P(("blk", "repl"), None),
        P(("blk", "repl")),
        P(("blk", "repl"), None),
    )
    out_specs = (P(("blk", "repl"), None), P(), P(("blk", "repl"), None))
    return jax.shard_map(local, mesh=mesh, in_specs=in_specs, out_specs=out_specs, check_vma=False)
```

```python
import functools
import math

import jax
import jax.numpy as jnp
from jax import lax
from jax.experimental import pallas as pl
from jax.experimental.pallas import tpu as pltpu
from jax.sharding import PartitionSpec as P

TILE = 128
REACH = 2
SPAN = 2 * REACH + 1
VMEM_LIMIT = 32 * 1024 * 1024
PARAMS = pltpu.CompilerParams(vmem_limit_bytes=VMEM_LIMIT)
FIRST_PARAMS = pltpu.CompilerParams(vmem_limit_bytes=60 * 1024 * 1024)
EXTRA = 16
BF16 = jnp.bfloat16
F32 = jnp.float32


def mirrored(value, steps):
    count = lax.axis_size("blk")
    pairs = [(k, (k + steps * (1 - 2 * (k & 1))) % count) for k in range(count)]
    return lax.ppermute(value, "blk", pairs)


def after(value, *others):
    return lax.optimization_barrier((value, *others))[0]


def swapped(value, axis, mask):
    count = lax.axis_size(axis)
    return lax.ppermute(value, axis, [(source, source ^ mask) for source in range(count)])


def crossed(value):
    panels, members = lax.axis_size("blk"), lax.axis_size("repl")
    pairs = [
        (k * members + r, (k ^ 1) * members + (r ^ 1)) for k in range(panels) for r in range(members)
    ]
    return lax.ppermute(value, ("blk", "repl"), pairs)


def spec_smem():
    return pl.BlockSpec(memory_space=pltpu.SMEM)


def spec_vmem():
    return pl.BlockSpec(memory_space=pltpu.VMEM)


def spec_hbm():
    return pl.BlockSpec(memory_space=pltpu.HBM)


def cost(flops, bytes_accessed):
    return pl.CostEstimate(flops=flops, bytes_accessed=bytes_accessed, transcendentals=0)


def split_kernel(panel_blocks, cycle, cols_hbm, count_hbm, feats_hbm, *refs):
    cols_ref, count_ref, place_ref, sems = refs[-4:]
    outs = refs[:-4]
    group = len(outs)
    rows, width = feats_hbm.shape[0], outs[0].shape[1]
    block_rows, slots = cols_ref.shape
    rank = lax.axis_index("repl")
    center = lax.axis_index("blk")
    small = [
        pltpu.make_async_copy(cols_hbm, cols_ref, sems.at[group]),
        pltpu.make_async_copy(count_hbm, count_ref, sems.at[group + 1]),
    ]
    large = []
    for d, out_ref in enumerate(outs):
        start = pl.multiple_of((rank ^ d) * width, width)
        large.append(
            pltpu.make_async_copy(
                feats_hbm.at[:, pl.ds(start, width)], out_ref.at[pl.ds(0, rows)], sems.at[d]
            )
        )
    for copy in small + large:
        copy.start()
    for copy in small:
        copy.wait()
    sign = 1 - 2 * (center & 1)
    cols = cols_ref[...]
    offset = (cols // panel_blocks - center) & (cycle - 1)
    offset = jnp.where(offset > REACH, offset - cycle, offset) * sign
    place = (offset + REACH) * panel_blocks + (cols & (panel_blocks - 1))
    row = lax.broadcasted_iota(jnp.int32, cols.shape, 0)
    slot = lax.broadcasted_iota(jnp.int32, cols.shape, 1)
    live = jnp.zeros(cols.shape, jnp.int32)
    for r in range(block_rows):
        live = jnp.where(row == r, count_ref[r], live)
    place = jnp.where(slot < live, place, SPAN * panel_blocks)
    place_ref[...] = jnp.zeros_like(place_ref)
    place_ref[pl.ds(0, block_rows), pl.ds(0, slots)] = place.astype(F32)
    for out_ref in outs:
        out_ref[pl.ds(rows, EXTRA), :] = place_ref[...].astype(BF16)
    for copy in large:
        copy.wait()


def split_columns(feats, tile_cols, tile_count, panel_blocks, cycle, group):
    rows, columns = feats.shape
    width = columns // group
    return pl.pallas_call(
        functools.partial(split_kernel, panel_blocks, cycle),
        in_specs=[spec_hbm()] * 3,
        out_shape=[jax.ShapeDtypeStruct((rows + EXTRA, width), feats.dtype)] * group,
        scratch_shapes=[
            pltpu.VMEM(tile_cols.shape, jnp.int32),
            pltpu.SMEM(tile_count.shape, jnp.int32),
            pltpu.VMEM((EXTRA, width), F32),
            pltpu.SemaphoreType.DMA((group + 2,)),
        ],
        compiler_params=FIRST_PARAMS,
        cost_estimate=cost(0, 2 * rows * columns * 2),
    )(tile_cols, tile_count, feats)


def place_rows(piece, rows, block_rows, spare):
    place = piece[pl.ds(rows, EXTRA), :].astype(F32).astype(jnp.int32)[:block_rows]
    return jnp.where(place < spare, place ^ (lax.axis_index("repl") * block_rows), place)


def join_kernel(block_rows, spare, own_hbm, *refs):
    *pieces, panel_ref, index_ref, own_ref, sem = refs
    copy = pltpu.make_async_copy(own_hbm, own_ref, sem)
    copy.start()
    rows = own_ref.shape[0] - EXTRA
    for d, piece in enumerate(pieces, 1):
        panel_ref[pl.ds(d * rows, rows), :] = piece[pl.ds(0, rows), :]
        place = place_rows(piece, rows, block_rows, spare)
        index_ref[pl.ds(d * block_rows, block_rows), :] = place
    copy.wait()
    panel_ref[pl.ds(0, rows), :] = own_ref[pl.ds(0, rows), :]
    index_ref[pl.ds(0, block_rows), :] = place_rows(own_ref, rows, block_rows, spare)


def joined_panel(pieces, block_rows, spare):
    rows, width = pieces[0].shape
    count = len(pieces)
    shape = (count * (rows - EXTRA), width)
    panel, index = pl.pallas_call(
        functools.partial(join_kernel, block_rows, spare),
        in_specs=[spec_hbm()] + [spec_vmem()] * (count - 1),
        out_shape=[
            jax.ShapeDtypeStruct(shape, BF16),
            jax.ShapeDtypeStruct((count * block_rows, width), jnp.int32),
        ],
        scratch_shapes=[pltpu.VMEM((rows, width), BF16), pltpu.SemaphoreType.DMA(())],
        compiler_params=PARAMS,
        cost_estimate=cost(0, 4 * shape[0] * width),
    )(*pieces)
    return panel.reshape(-1, TILE, width), index


def window_kernel(places, *refs):
    pieces = refs[: len(places)]
    window, sems = refs[-2:]
    copies = [
        pltpu.make_async_copy(
            piece, window.at[pl.ds(place * piece.shape[0], piece.shape[0])], sems.at[n]
        )
        for n, (piece, place) in enumerate(zip(pieces, places))
    ]
    for copy in copies:
        copy.start()
    if len(places) > 1:
        window[window.shape[0] - 1] = jnp.zeros(window.shape[1:], window.dtype)
    for copy in copies:
        copy.wait()


def window_with(pieces, places, window=None):
    size, tile, width = pieces[0].shape
    begun = [] if window is None else [window]
    return pl.pallas_call(
        functools.partial(window_kernel, places),
        in_specs=[spec_vmem()] * len(pieces) + [spec_vmem()] * len(begun),
        out_specs=spec_vmem(),
        out_shape=jax.ShapeDtypeStruct((SPAN * size + 1, tile, width), BF16),
        input_output_aliases={len(pieces): 0} if begun else {},
        scratch_shapes=[pltpu.SemaphoreType.DMA((len(pieces),))],
        compiler_params=PARAMS,
        cost_estimate=cost(0, 4 * len(pieces) * size * tile * width),
    )(*pieces, *begun)


def gather_kernel(group, index, window, *refs):
    outs = refs[-group:]
    vals = refs[:-group]
    block_rows = outs[0].shape[0]
    part = vals[-1].shape[0]

    @pl.loop(0, part)
    def _(i):
        row = 0
        for val in vals:
            for b in range(0, val.shape[0], part):
                slots = range(val.shape[1])
                lhs = jnp.concatenate([val[b + i, s] for s in slots], axis=1)
                rhs = jnp.concatenate([window[index[row + i, s]] for s in slots], axis=0)
                made = jnp.dot(lhs, rhs, preferred_element_type=F32).astype(BF16)
                outs[row // block_rows][row % block_rows + i] = made
                row += part


def sparse_gather(index, vals, window, group):
    rows = sum(val.shape[0] for val in vals)
    slots = vals[0].shape[1]
    blocks, _, width = window.shape
    return pl.pallas_call(
        functools.partial(gather_kernel, group),
        in_specs=[spec_smem()] + [spec_vmem()] * (len(vals) + 1),
        out_shape=[jax.ShapeDtypeStruct((rows // group, TILE, width), BF16)] * group,
        compiler_params=PARAMS,
        cost_estimate=cost(
            rows * slots * TILE * TILE * width * 2,
            rows * slots * TILE * TILE * 2 + blocks * TILE * width * 2,
        ),
    )(index, window, *vals)


def prepare_kernel(group, weight_ref, rows_ref, turned_ref):
    width = weight_ref.shape[0] // group
    rank = lax.axis_index("repl")
    for d in range(group):
        start = pl.multiple_of((rank ^ d) * width, width)
        chunk = weight_ref[pl.ds(start, width), :]
        rows_ref[pl.ds(d * width, width), :] = chunk
        turned_ref[:, pl.ds(d * width, width)] = chunk.T


def prepared(weight, group):
    rows, columns = weight.shape
    return pl.pallas_call(
        functools.partial(prepare_kernel, group),
        in_specs=[spec_vmem()],
        out_shape=[
            jax.ShapeDtypeStruct((rows, columns), BF16),
            jax.ShapeDtypeStruct((columns, rows), BF16),
        ],
        compiler_params=PARAMS,
        cost_estimate=cost(0, 6 * rows * columns),
    )(weight)


def dense_kernel(group, *refs):
    parts = refs[:group]
    weight_ref, turned_ref, cotangent_ref, output_ref, slope_ref = refs[group : group + 5]
    backs = refs[group + 5 :]
    blocks, tile, width = parts[0].shape
    steps = 2
    blocks = blocks // steps
    rows = blocks * tile

    for g in range(steps):
        at = pl.ds(g * rows, rows)
        blocks_at = pl.ds(g * blocks, blocks)
        aggregate = jnp.concatenate([p[blocks_at].reshape(rows, width) for p in parts], axis=1)
        preact = jnp.dot(aggregate, weight_ref[...], preferred_element_type=F32)
        sigma = jax.nn.sigmoid(preact)
        output_ref[at, :] = (preact * sigma).astype(BF16)
        slope = sigma * (1.0 + preact * (1.0 - sigma))
        slope = (cotangent_ref[at, :].astype(F32) * slope).astype(BF16)
        slope_ref[at, :] = slope
        backward = jnp.dot(slope, turned_ref[...], preferred_element_type=F32).astype(BF16)
        for d in range(group):
            piece = backward[:, d * width : (d + 1) * width]
            backs[d][blocks_at] = piece.reshape(blocks, tile, width)


def dense(parts, weight, turned, cotangent):
    group = len(parts)
    node_rows, feat_out = cotangent.shape
    feat_in = weight.shape[0]
    return pl.pallas_call(
        functools.partial(dense_kernel, group),
        in_specs=[spec_vmem()] * (group + 3),
        out_shape=[jax.ShapeDtypeStruct((node_rows, feat_out), BF16)] * 2
        + [jax.ShapeDtypeStruct(parts[0].shape, BF16)] * group,
        compiler_params=PARAMS,
        cost_estimate=cost(
            4 * node_rows * feat_in * feat_out,
            2 * (5 * node_rows * feat_out + 2 * feat_in * feat_out),
        ),
    )(*parts, weight, turned, cotangent)


def term_kernel(slope_ref, *refs):
    *parts, kept_ref, given_ref = refs
    slope = slope_ref[...]
    for d, part in enumerate(parts):
        part = part[...].reshape(slope.shape[0], -1)
        term = lax.dot_general(part, slope, (((0,), (0,)), ((), ())), preferred_element_type=F32)
        out_ref = given_ref if d & 1 else kept_ref
        out_ref[pl.ds(d // 2 * term.shape[0], term.shape[0]), :] = term.astype(BF16)


def weight_terms(parts, slope):
    group = len(parts)
    width = parts[0].shape[-1]
    node_rows, feat_out = slope.shape
    return pl.pallas_call(
        term_kernel,
        in_specs=[spec_vmem()] * (group + 1),
        out_shape=[jax.ShapeDtypeStruct((group // 2 * width, feat_out), BF16)] * 2,
        compiler_params=PARAMS,
        cost_estimate=cost(
            2 * node_rows * width * group * feat_out, 2 * 3 * node_rows * feat_out
        ),
    )(slope, *parts)


def halve_kernel(own_first, kept_ref, arrived_ref, keep_ref, give_ref):
    size = keep_ref.shape[0]
    kept = own_first()
    for out_ref, at in ((keep_ref, kept), (give_ref, 1 - kept)):
        rows = pl.ds(pl.multiple_of(at * size, size), size)
        total = kept_ref[rows, :].astype(F32) + arrived_ref[rows, :].astype(F32)
        out_ref[...] = total.astype(BF16)


def halved(kept, arrived, which):
    rows, columns = kept.shape
    return pl.pallas_call(
        functools.partial(halve_kernel, which),
        in_specs=[spec_vmem()] * 2,
        out_shape=[jax.ShapeDtypeStruct((rows // 2, columns), BF16)] * 2,
        compiler_params=PARAMS,
        cost_estimate=cost(0, 6 * rows * columns),
    )(kept, arrived)


def side():
    return lax.axis_index("repl") // (lax.axis_size("repl") // 2)


def parity():
    return lax.axis_index("blk") & 1


def parity_on_side():
    return parity() ^ side()


def scatter_kernel(group, index, *refs):
    total = refs[-1]
    outs = refs[-1 - SPAN : -1]
    backs = refs[-1 - SPAN - group : -1 - SPAN]
    vals = refs[: -1 - SPAN - group]
    size = outs[0].shape[0]
    block_rows = backs[0].shape[0]
    part = vals[-1].shape[0]
    total[...] = jnp.zeros_like(total)

    @pl.loop(0, part)
    def _(i):
        row = 0
        for val in vals:
            for b in range(0, val.shape[0], part):
                turned = backs[row // block_rows][row % block_rows + i].T
                for s in range(0, val.shape[1], 2):
                    rhs = jnp.concatenate([val[b + i, s], val[b + i, s + 1]], axis=1)
                    made = jnp.dot(turned, rhs, preferred_element_type=F32)
                    total[index[row + i, s]] += made[:, :TILE]
                    total[index[row + i, s + 1]] += made[:, TILE:]
                row += part

    for n in range(SPAN):
        outs[n][...] = total[pl.ds(n * size, size)].astype(BF16)


def sparse_scatter(index, vals, backs):
    group = len(backs)
    rows = sum(val.shape[0] for val in vals)
    slots = vals[0].shape[1]
    width = backs[0].shape[-1]
    return pl.pallas_call(
        functools.partial(scatter_kernel, group),
        in_specs=[spec_smem()] + [spec_vmem()] * (len(vals) + group),
        out_shape=[jax.ShapeDtypeStruct((rows, width, TILE), BF16)] * SPAN,
        scratch_shapes=[pltpu.VMEM((SPAN * rows + 1, width, TILE), F32)],
        compiler_params=PARAMS,
        cost_estimate=cost(
            rows * slots * TILE * TILE * width * 2,
            rows * slots * TILE * TILE * 2 + 6 * rows * TILE * width * 2,
        ),
    )(index, *vals, *backs)


def sum_kernel(bases, size, *refs):
    terms = refs[: len(bases)]
    for n, out_ref in enumerate(refs[len(bases) :]):
        total = jnp.zeros(out_ref.shape, F32)
        for ref, base in zip(terms, bases):
            total += ref[pl.ds(base + n * size, size)].astype(F32)
        out_ref[...] = total.astype(BF16)


def summed(terms, bases, size, count):
    shape = (size, *terms[0].shape[1:])
    return pl.pallas_call(
        functools.partial(sum_kernel, bases, size),
        in_specs=[spec_vmem()] * len(terms),
        out_shape=[jax.ShapeDtypeStruct(shape, BF16)] * count,
        compiler_params=PARAMS,
        cost_estimate=cost(0, count * math.prod(shape) * 2 * (len(terms) + 1)),
    )(*terms)


def turn_kernel(*refs):
    count = len(refs) // 2
    for part, out_ref in zip(refs[:count], refs[count:]):
        tile = part.shape[2]
        for b in range(part.shape[0]):
            out_ref[pl.ds(b * tile, tile), :] = part[b].T


def turned(parts):
    blocks, width, tile = parts[0].shape
    return pl.pallas_call(
        turn_kernel,
        in_specs=[spec_vmem()] * len(parts),
        out_shape=[jax.ShapeDtypeStruct((blocks * tile, width), BF16)] * len(parts),
        compiler_params=PARAMS,
        cost_estimate=cost(0, 4 * len(parts) * blocks * tile * width),
    )(*parts)


def place_kernel(*refs):
    *parts, out_ref = refs
    rank = lax.axis_index("repl")
    for d, part in enumerate(parts):
        width = part.shape[1]
        start = pl.multiple_of((rank ^ d) * width, width)
        if len(part.shape) == 2:
            out_ref[:, pl.ds(start, width)] = part[...]
            continue
        tile = part.shape[2]
        for b in range(part.shape[0]):
            out_ref[pl.ds(b * tile, tile), pl.ds(start, width)] = part[b].T


def placed(parts):
    blocks, width, tile = parts[0].shape
    shape = (blocks * tile, width * len(parts))
    return pl.pallas_call(
        place_kernel,
        in_specs=[spec_vmem()] * len(parts),
        out_shape=jax.ShapeDtypeStruct(shape, BF16),
        compiler_params=PARAMS,
        cost_estimate=cost(0, 2 * 2 * shape[0] * shape[1]),
    )(*parts)


def rows_kernel(scale, *refs):
    out_ref = refs[-1]
    size = refs[0].shape[0]
    core = lax.axis_index("repl") & 1
    even = parity()
    for n, ref in enumerate(refs[:-1]):
        start = ((core ^ (n & 1)) + 2 * (even ^ (n // 2))) * size
        out_ref[pl.ds(pl.multiple_of(start, size), size), :] = ref[...].astype(F32) * scale


def rows_placed(parts, scale):
    size, columns = parts[0].shape
    return pl.pallas_call(
        functools.partial(rows_kernel, scale),
        in_specs=[spec_vmem()] * len(parts),
        out_shape=jax.ShapeDtypeStruct((size * len(parts), columns), F32),
        compiler_params=PARAMS,
        cost_estimate=cost(0, 6 * size * len(parts) * columns),
    )(*parts)


def local(feats, weight, tile_vals, tile_cols, tile_count, cotangent):
    node_rows = feats.shape[0]
    cycle = lax.axis_size("blk")
    group = lax.axis_size("repl")
    assert group == 4 and cycle & (cycle - 1) == 0
    block_rows = node_rows // TILE
    panel_blocks = block_rows * group
    spare = SPAN * panel_blocks
    far_side = group // 2

    sent = split_columns(feats, tile_cols, tile_count, panel_blocks, cycle, group)
    mine = [sent[0]] + [swapped(sent[d], "repl", d) for d in range(1, group)]
    panel, index = joined_panel(mine, block_rows, spare)

    ahead = mirrored(panel, -2)
    beside = mirrored(panel, 1)
    behind = mirrored(after(panel, ahead), 2)
    relayed = mirrored(after(ahead, beside), 1)
    window = window_with([behind, panel, beside, ahead], [0, 2, 3, 4])
    window = window_with([relayed], [1], window)

    half = block_rows // 2
    ready = after(tile_vals, mine[far_side])
    own_vals = [ready[:half], ready[half:]]
    carried = [swapped(part, "repl", far_side) for part in own_vals]
    near = range(1, far_side)
    vals = own_vals + [swapped(after(tile_vals, panel), "repl", d) for d in near]
    vals += carried + [swapped(part, "repl", d) for d in near for part in carried]
    columns = sparse_gather(index, vals, window, group)
    aggregate = [columns[0]] + [swapped(columns[d], "repl", d) for d in range(1, group)]

    made = dense(aggregate, *prepared(after(weight, panel), group), cotangent)
    output, slope, backs = made[0], made[1], made[2:]
    backs = [backs[0]] + [swapped(backs[d], "repl", d) for d in range(1, group)]

    kept, given = weight_terms(aggregate, slope)
    arrived = swapped(given, "repl", 1)
    kept, given = halved(after(kept, backs[1]), arrived, parity_on_side)
    backs[0] = after(backs[0], given)
    arrived = swapped(given, "blk", 1)

    far, relay, own, near_share, joined = sparse_scatter(index, vals, backs)
    chunk = after(kept, own).astype(F32) + arrived.astype(F32)
    sums = [lax.optimization_barrier(chunk.astype(BF16))]
    relay_in = mirrored(relay, 1)
    far_in = mirrored(far, -2)
    joined = summed([joined, relay_in], [0, 0], panel_blocks // 2, 2)
    side_sum = sums[-1].astype(F32) + swapped(sums[-1], "repl", far_side).astype(F32)
    sums.append(lax.optimization_barrier(side_sum.astype(BF16)))
    mask = 2
    while mask * 2 < cycle:
        chunk = sums[-1].astype(F32) + swapped(sums[-1], "blk", mask).astype(F32)
        sums.append(lax.optimization_barrier(chunk.astype(BF16)))
        mask *= 2
    other = swapped(sums[-1], "blk", mask)
    near_in = mirrored(near_share, 1)
    joined = [after(part, far_in) for part in joined]
    owned = []
    for part in reversed(joined):
        joined_in = mirrored(part, 2)
        base = 0 if owned else part.shape[0]
        terms = [after(own, *owned[:1]), far_in, near_in, joined_in]
        owned = [*summed(terms, [base, base, base, 0], block_rows, far_side), *owned]
    gathered = [owned[0]] + [swapped(owned[d], "repl", d) for d in range(1, group)]
    grad_rows = placed([*gathered[:far_side], *turned(gathered[far_side:])])

    chunk = after(sums[-1], owned[far_side]).astype(F32) + other.astype(F32)
    sums.append(lax.optimization_barrier(chunk.astype(BF16)))
    first = sums[-1]
    parts = [first, swapped(first, "repl", 1), swapped(first, "blk", 1), crossed(first)]
    weight_grad = rows_placed(parts, 1.0 / math.sqrt(node_rows * group * cycle))
    return (output, weight_grad, grad_rows)


def solution(mesh):
    in_specs = (
        P(("blk", "repl"), None),
        P(),
        P(("blk", "repl"), None, None, None),
        P(("blk", "repl"), None),
        P(("blk", "repl")),
        P(("blk", "repl"), None),
    )
    out_specs = (P(("blk", "repl"), None), P(), P(("blk", "repl"), None))
    return jax.shard_map(local, mesh=mesh, in_specs=in_specs, out_specs=out_specs, check_vma=False)
```

```python
import functools
import math

import jax
import jax.numpy as jnp
from jax import lax
from jax.experimental import pallas as pl
from jax.experimental.pallas import tpu as pltpu
from jax.sharding import PartitionSpec as P

TILE = 128
REACH = 2
SPAN = 2 * REACH + 1
VMEM_LIMIT = 32 * 1024 * 1024
PARAMS = pltpu.CompilerParams(vmem_limit_bytes=VMEM_LIMIT)
FIRST_PARAMS = pltpu.CompilerParams(vmem_limit_bytes=60 * 1024 * 1024)
EXTRA = 16
BF16 = jnp.bfloat16
F32 = jnp.float32


def mirrored(value, steps):
    count = lax.axis_size("blk")
    pairs = [(k, (k + steps * (1 - 2 * (k & 1))) % count) for k in range(count)]
    return lax.ppermute(value, "blk", pairs)


def after(value, *others):
    return lax.optimization_barrier((value, *others))[0]


def swapped(value, axis, mask):
    count = lax.axis_size(axis)
    return lax.ppermute(value, axis, [(source, source ^ mask) for source in range(count)])


def spec_smem():
    return pl.BlockSpec(memory_space=pltpu.SMEM)


def spec_vmem():
    return pl.BlockSpec(memory_space=pltpu.VMEM)


def spec_hbm():
    return pl.BlockSpec(memory_space=pltpu.HBM)


def cost(flops, bytes_accessed):
    return pl.CostEstimate(flops=flops, bytes_accessed=bytes_accessed, transcendentals=0)


def split_kernel(panel_blocks, cycle, cols_hbm, count_hbm, feats_hbm, *refs):
    cols_ref, count_ref, place_ref, sems = refs[-4:]
    outs = refs[:-4]
    group = len(outs)
    rows, width = feats_hbm.shape[0], outs[0].shape[1]
    block_rows, slots = cols_ref.shape
    rank = lax.axis_index("repl")
    center = lax.axis_index("blk")
    small = [
        pltpu.make_async_copy(cols_hbm, cols_ref, sems.at[group]),
        pltpu.make_async_copy(count_hbm, count_ref, sems.at[group + 1]),
    ]
    large = []
    for d, out_ref in enumerate(outs):
        start = pl.multiple_of((rank ^ d) * width, width)
        large.append(
            pltpu.make_async_copy(
                feats_hbm.at[:, pl.ds(start, width)], out_ref.at[pl.ds(0, rows)], sems.at[d]
            )
        )
    for copy in small + large:
        copy.start()
    for copy in small:
        copy.wait()
    sign = 1 - 2 * (center & 1)
    cols = cols_ref[...]
    offset = (cols // panel_blocks - center) & (cycle - 1)
    offset = jnp.where(offset > REACH, offset - cycle, offset) * sign
    place = (offset + REACH) * panel_blocks + (cols & (panel_blocks - 1))
    row = lax.broadcasted_iota(jnp.int32, cols.shape, 0)
    slot = lax.broadcasted_iota(jnp.int32, cols.shape, 1)
    live = jnp.zeros(cols.shape, jnp.int32)
    for r in range(block_rows):
        live = jnp.where(row == r, count_ref[r], live)
    place = jnp.where(slot < live, place, SPAN * panel_blocks)
    place_ref[...] = jnp.zeros_like(place_ref)
    place_ref[pl.ds(0, block_rows), pl.ds(0, slots)] = place.astype(F32)
    for out_ref in outs:
        out_ref[pl.ds(rows, EXTRA), :] = place_ref[...].astype(BF16)
    for copy in large:
        copy.wait()


def split_columns(feats, tile_cols, tile_count, panel_blocks, cycle, group):
    rows, columns = feats.shape
    width = columns // group
    return pl.pallas_call(
        functools.partial(split_kernel, panel_blocks, cycle),
        in_specs=[spec_hbm()] * 3,
        out_shape=[jax.ShapeDtypeStruct((rows + EXTRA, width), feats.dtype)] * group,
        scratch_shapes=[
            pltpu.VMEM(tile_cols.shape, jnp.int32),
            pltpu.SMEM(tile_count.shape, jnp.int32),
            pltpu.VMEM((EXTRA, width), F32),
            pltpu.SemaphoreType.DMA((group + 2,)),
        ],
        compiler_params=FIRST_PARAMS,
        cost_estimate=cost(0, 2 * rows * columns * 2),
    )(tile_cols, tile_count, feats)


def place_rows(piece, rows, block_rows, spare):
    place = piece[pl.ds(rows, EXTRA), :].astype(F32).astype(jnp.int32)[:block_rows]
    return jnp.where(place < spare, place ^ (lax.axis_index("repl") * block_rows), place)


def join_near_kernel(block_rows, spare, own_hbm, *refs):
    *pieces, part_ref, index_ref, own_ref, sem = refs
    copy = pltpu.make_async_copy(own_hbm, own_ref, sem)
    copy.start()
    rows = own_ref.shape[0] - EXTRA
    for d, piece in enumerate(pieces, 1):
        part_ref[pl.ds(d * rows, rows), :] = piece[pl.ds(0, rows), :]
        place = place_rows(piece, rows, block_rows, spare)
        index_ref[pl.ds(d * block_rows, block_rows), :] = place
    copy.wait()
    part_ref[pl.ds(0, rows), :] = own_ref[pl.ds(0, rows), :]
    index_ref[pl.ds(0, block_rows), :] = place_rows(own_ref, rows, block_rows, spare)


def join_near(pieces, block_rows, spare):
    rows, width = pieces[0].shape
    count = len(pieces)
    shape = (count * (rows - EXTRA), width)
    return pl.pallas_call(
        functools.partial(join_near_kernel, block_rows, spare),
        in_specs=[spec_hbm()] + [spec_vmem()] * (count - 1),
        out_shape=[
            jax.ShapeDtypeStruct(shape, BF16),
            jax.ShapeDtypeStruct((count * block_rows, width), jnp.int32),
        ],
        scratch_shapes=[pltpu.VMEM((rows, width), BF16), pltpu.SemaphoreType.DMA(())],
        compiler_params=PARAMS,
        cost_estimate=cost(0, 4 * shape[0] * width),
    )(*pieces)


def join_far_kernel(block_rows, spare, near_ref, near_index_ref, *refs):
    *pieces, part_ref, index_ref, whole_ref = refs
    begin = near_ref.shape[0]
    begin_index = near_index_ref.shape[0]
    rows = part_ref.shape[0] // len(pieces)
    whole_ref[pl.ds(0, begin), :] = near_ref[...]
    index_ref[pl.ds(0, begin_index), :] = near_index_ref[...]
    for d, piece in enumerate(pieces):
        values = piece[pl.ds(0, rows), :]
        part_ref[pl.ds(d * rows, rows), :] = values
        whole_ref[pl.ds(begin + d * rows, rows), :] = values
        place = place_rows(piece, rows, block_rows, spare)
        index_ref[pl.ds(begin_index + d * block_rows, block_rows), :] = place


def join_far(near_rows, near_index, pieces, block_rows, spare):
    rows, width = pieces[0].shape
    count = len(pieces)
    shape = (count * (rows - EXTRA), width)
    return pl.pallas_call(
        functools.partial(join_far_kernel, block_rows, spare),
        in_specs=[spec_vmem()] * (count + 2),
        out_shape=[
            jax.ShapeDtypeStruct(shape, BF16),
            jax.ShapeDtypeStruct((near_index.shape[0] + count * block_rows, width), jnp.int32),
            jax.ShapeDtypeStruct((near_rows.shape[0] + shape[0], width), BF16),
        ],
        compiler_params=PARAMS,
        cost_estimate=cost(0, 8 * shape[0] * width),
    )(near_rows, near_index, *pieces)


def window_kernel(places, *refs):
    pieces = refs[: len(places)]
    window, sems = refs[-2:]
    copies = [
        pltpu.make_async_copy(piece, window.at[pl.ds(place, piece.shape[0])], sems.at[n])
        for n, (piece, place) in enumerate(zip(pieces, places))
    ]
    for copy in copies:
        copy.start()
    if len(places) > 1:
        window[window.shape[0] - 1] = jnp.zeros(window.shape[1:], window.dtype)
    for copy in copies:
        copy.wait()


def window_with(pieces, places, blocks, window=None):
    _, tile, width = pieces[0].shape
    begun = [] if window is None else [window]
    return pl.pallas_call(
        functools.partial(window_kernel, places),
        in_specs=[spec_vmem()] * (len(pieces) + len(begun)),
        out_specs=spec_vmem(),
        out_shape=jax.ShapeDtypeStruct((blocks, tile, width), BF16),
        input_output_aliases={len(pieces): 0} if begun else {},
        scratch_shapes=[pltpu.SemaphoreType.DMA((len(pieces),))],
        compiler_params=PARAMS,
        cost_estimate=cost(0, 4 * sum(math.prod(piece.shape) for piece in pieces)),
    )(*pieces, *begun)


def stack_kernel(*refs):
    *pieces, out_ref, sems = refs
    copies = []
    base = 0
    for n, piece in enumerate(pieces):
        size = piece.shape[0]
        copies.append(pltpu.make_async_copy(piece, out_ref.at[pl.ds(base, size)], sems.at[n]))
        base += size
    for copy in copies:
        copy.start()
    for copy in copies:
        copy.wait()


def stacked(pieces):
    shape = (sum(piece.shape[0] for piece in pieces), *pieces[0].shape[1:])
    return pl.pallas_call(
        stack_kernel,
        in_specs=[spec_vmem()] * len(pieces),
        out_shape=jax.ShapeDtypeStruct(shape, BF16),
        scratch_shapes=[pltpu.SemaphoreType.DMA((len(pieces),))],
        compiler_params=PARAMS,
        cost_estimate=cost(0, 4 * math.prod(shape)),
    )(*pieces)


def gather_kernel(group, index, window, *refs):
    outs = refs[-group:]
    vals = refs[:-group]
    block_rows = outs[0].shape[0]
    part = vals[-1].shape[0]

    @pl.loop(0, part)
    def _(i):
        row = 0
        for val in vals:
            for b in range(0, val.shape[0], part):
                slots = range(val.shape[1])
                lhs = jnp.concatenate([val[b + i, s] for s in slots], axis=1)
                rhs = jnp.concatenate([window[index[row + i, s]] for s in slots], axis=0)
                made = jnp.dot(lhs, rhs, preferred_element_type=F32).astype(BF16)
                outs[row // block_rows][row % block_rows + i] = made
                row += part


def sparse_gather(index, vals, window, group):
    rows = sum(val.shape[0] for val in vals)
    slots = vals[0].shape[1]
    blocks, _, width = window.shape
    return pl.pallas_call(
        functools.partial(gather_kernel, group),
        in_specs=[spec_smem()] + [spec_vmem()] * (len(vals) + 1),
        out_shape=[jax.ShapeDtypeStruct((rows // group, TILE, width), BF16)] * group,
        compiler_params=PARAMS,
        cost_estimate=cost(
            rows * slots * TILE * TILE * width * 2,
            rows * slots * TILE * TILE * 2 + blocks * TILE * width * 2,
        ),
    )(index, window, *vals)


def prepare_kernel(group, weight_ref, rows_ref, turned_ref):
    width = weight_ref.shape[0] // group
    rank = lax.axis_index("repl")
    for d in range(group):
        start = pl.multiple_of((rank ^ d) * width, width)
        chunk = weight_ref[pl.ds(start, width), :]
        rows_ref[pl.ds(d * width, width), :] = chunk
        turned_ref[:, pl.ds(d * width, width)] = chunk.T


def prepared(weight, group):
    rows, columns = weight.shape
    return pl.pallas_call(
        functools.partial(prepare_kernel, group),
        in_specs=[spec_vmem()],
        out_shape=[
            jax.ShapeDtypeStruct((rows, columns), BF16),
            jax.ShapeDtypeStruct((columns, rows), BF16),
        ],
        compiler_params=PARAMS,
        cost_estimate=cost(0, 6 * rows * columns),
    )(weight)


def dense_kernel(group, *refs):
    parts = refs[:group]
    weight_ref, turned_ref, cotangent_ref, output_ref, slope_ref = refs[group : group + 5]
    backs = refs[group + 5 :]
    blocks, tile, width = parts[0].shape
    steps = 2
    blocks = blocks // steps
    rows = blocks * tile

    for g in range(steps):
        at = pl.ds(g * rows, rows)
        blocks_at = pl.ds(g * blocks, blocks)
        aggregate = jnp.concatenate([p[blocks_at].reshape(rows, width) for p in parts], axis=1)
        preact = jnp.dot(aggregate, weight_ref[...], preferred_element_type=F32)
        sigma = jax.nn.sigmoid(preact)
        output_ref[at, :] = (preact * sigma).astype(BF16)
        slope = sigma * (1.0 + preact * (1.0 - sigma))
        slope = (cotangent_ref[at, :].astype(F32) * slope).astype(BF16)
        slope_ref[at, :] = slope
        backward = jnp.dot(slope, turned_ref[...], preferred_element_type=F32).astype(BF16)
        for d in range(group):
            piece = backward[:, d * width : (d + 1) * width]
            backs[d][blocks_at] = piece.reshape(blocks, tile, width)


def dense(parts, weight, turned, cotangent):
    group = len(parts)
    node_rows, feat_out = cotangent.shape
    feat_in = weight.shape[0]
    return pl.pallas_call(
        functools.partial(dense_kernel, group),
        in_specs=[spec_vmem()] * (group + 3),
        out_shape=[jax.ShapeDtypeStruct((node_rows, feat_out), BF16)] * 2
        + [jax.ShapeDtypeStruct(parts[0].shape, BF16)] * group,
        compiler_params=PARAMS,
        cost_estimate=cost(
            4 * node_rows * feat_in * feat_out,
            2 * (5 * node_rows * feat_out + 2 * feat_in * feat_out),
        ),
    )(*parts, weight, turned, cotangent)


def term_kernel(slope_ref, *refs):
    group = len(refs) // 2
    slope = slope_ref[...]
    for d in range(group):
        part = refs[d][...].reshape(slope.shape[0], -1)
        term = lax.dot_general(part, slope, (((0,), (0,)), ((), ())), preferred_element_type=F32)
        refs[group + d][...] = term.astype(BF16)


def weight_terms(parts, slope):
    group = len(parts)
    width = parts[0].shape[-1]
    node_rows, feat_out = slope.shape
    return pl.pallas_call(
        term_kernel,
        in_specs=[spec_vmem()] * (group + 1),
        out_shape=[jax.ShapeDtypeStruct((width, feat_out), BF16)] * group,
        compiler_params=PARAMS,
        cost_estimate=cost(
            2 * node_rows * width * group * feat_out, 2 * 3 * node_rows * feat_out
        ),
    )(slope, *parts)


def scatter_kernel(group, index, *refs):
    total = refs[-1]
    outs = refs[-1 - SPAN : -1]
    backs = refs[-1 - SPAN - group : -1 - SPAN]
    vals = refs[: -1 - SPAN - group]
    size = outs[0].shape[0]
    block_rows = backs[0].shape[0]
    part = vals[-1].shape[0]
    total[...] = jnp.zeros_like(total)

    @pl.loop(0, part)
    def _(i):
        row = 0
        for val in vals:
            for b in range(0, val.shape[0], part):
                turned = backs[row // block_rows][row % block_rows + i].T
                for s in range(0, val.shape[1], 2):
                    rhs = jnp.concatenate([val[b + i, s], val[b + i, s + 1]], axis=1)
                    made = jnp.dot(turned, rhs, preferred_element_type=F32)
                    total[index[row + i, s]] += made[:, :TILE]
                    total[index[row + i, s + 1]] += made[:, TILE:]
                row += part

    for n in range(SPAN):
        outs[n][...] = total[pl.ds(n * size, size)].astype(BF16)


def sparse_scatter(index, vals, backs):
    group = len(backs)
    rows = sum(val.shape[0] for val in vals)
    slots = vals[0].shape[1]
    width = backs[0].shape[-1]
    return pl.pallas_call(
        functools.partial(scatter_kernel, group),
        in_specs=[spec_smem()] + [spec_vmem()] * (len(vals) + group),
        out_shape=[jax.ShapeDtypeStruct((rows, width, TILE), BF16)] * SPAN,
        scratch_shapes=[pltpu.VMEM((SPAN * rows + 1, width, TILE), F32)],
        compiler_params=PARAMS,
        cost_estimate=cost(
            rows * slots * TILE * TILE * width * 2,
            rows * slots * TILE * TILE * 2 + 6 * rows * TILE * width * 2,
        ),
    )(index, *vals, *backs)


def sum_kernel(bases, size, *refs):
    terms = refs[: len(bases)]
    for n, out_ref in enumerate(refs[len(bases) :]):
        total = jnp.zeros(out_ref.shape, F32)
        for ref, base in zip(terms, bases):
            total += ref[pl.ds(base + n * size, size)].astype(F32)
        out_ref[...] = total.astype(BF16)


def summed(terms, bases, size, count):
    shape = (size, *terms[0].shape[1:])
    return pl.pallas_call(
        functools.partial(sum_kernel, bases, size),
        in_specs=[spec_vmem()] * len(terms),
        out_shape=[jax.ShapeDtypeStruct(shape, BF16)] * count,
        compiler_params=PARAMS,
        cost_estimate=cost(0, count * math.prod(shape) * 2 * (len(terms) + 1)),
    )(*terms)


def place_kernel(rank_ref, *refs):
    out_ref = refs[-1]
    for d, ref in enumerate(refs[:-1]):
        blocks, width, tile = ref.shape
        start = pl.multiple_of((rank_ref[0] ^ d) * width, width)
        for b in range(blocks):
            out_ref[pl.ds(b * tile, tile), pl.ds(start, width)] = ref[b].T


def placed(rank, parts):
    blocks, width, tile = parts[0].shape
    shape = (blocks * tile, width * len(parts))
    return pl.pallas_call(
        place_kernel,
        in_specs=[spec_smem()] + [spec_vmem()] * len(parts),
        out_shape=jax.ShapeDtypeStruct(shape, BF16),
        compiler_params=PARAMS,
        cost_estimate=cost(0, 2 * 2 * shape[0] * shape[1]),
    )(rank, *parts)


def rows_kernel(scale, rank_ref, *refs):
    out_ref = refs[-1]
    for d, ref in enumerate(refs[:-1]):
        size = ref.shape[0]
        start = pl.multiple_of((rank_ref[0] ^ d) * size, size)
        out_ref[pl.ds(start, size), :] = ref[...].astype(F32) * scale


def rows_placed(rank, parts, scale):
    size, columns = parts[0].shape
    return pl.pallas_call(
        functools.partial(rows_kernel, scale),
        in_specs=[spec_smem()] + [spec_vmem()] * len(parts),
        out_shape=jax.ShapeDtypeStruct((size * len(parts), columns), F32),
        compiler_params=PARAMS,
        cost_estimate=cost(0, 6 * size * len(parts) * columns),
    )(rank, *parts)


def local(feats, weight, tile_vals, tile_cols, tile_count, cotangent):
    node_rows = feats.shape[0]
    cycle = lax.axis_size("blk")
    group = lax.axis_size("repl")
    assert group & (group - 1) == 0 and cycle & (cycle - 1) == 0
    block_rows = node_rows // TILE
    panel_blocks = block_rows * group
    spare = SPAN * panel_blocks
    far_side = group // 2
    where = jnp.reshape(lax.axis_index("repl"), (1,)).astype(jnp.int32)

    sent = split_columns(feats, tile_cols, tile_count, panel_blocks, cycle, group)
    mine = [sent[0]] + [swapped(sent[d], "repl", d) for d in range(1, group)]
    half = block_rows // 2
    ready = after(tile_vals, sent[1])
    own_vals = [ready[:half], ready[half:]]
    mine[1] = after(mine[1], *own_vals)
    near_rows, near_index = join_near(mine[:far_side], block_rows, spare)
    far_rows, index, rows = join_far(
        near_rows, near_index, mine[far_side:], block_rows, spare
    )
    near_part, far_part, panel = [
        value.reshape(-1, TILE, value.shape[-1]) for value in (near_rows, far_rows, rows)
    ]

    ahead_near = mirrored(near_part, -2)
    ahead = stacked([ahead_near, mirrored(after(far_part, ahead_near), -2)])
    beside = mirrored(panel, 1)
    behind = mirrored(after(panel, ahead), 2)
    relayed = mirrored(after(ahead, beside), 1)
    places = [n * panel_blocks for n in range(SPAN)]
    window = window_with([behind, panel, beside, ahead], [places[n] for n in (0, 2, 3, 4)], spare + 1)
    window = window_with([relayed], [places[1]], spare + 1, window)

    carried = [swapped(after(part, mine[far_side]), "repl", far_side) for part in own_vals]
    near = range(1, far_side)
    vals = own_vals + [swapped(after(tile_vals, sent[1]), "repl", d) for d in near]
    vals += carried + [swapped(part, "repl", d) for d in near for part in carried]
    columns = sparse_gather(index, vals, window, group)
    aggregate = [columns[0]] + [swapped(columns[d], "repl", d) for d in range(1, group)]

    made = dense(aggregate, *prepared(after(weight, panel), group), cotangent)
    output, slope, backs = made[0], made[1], made[2:]
    backs = [backs[0]] + [swapped(backs[d], "repl", d) for d in range(1, group)]

    terms = weight_terms(aggregate, after(slope, backs[1]))
    arrived = [swapped(terms[d], "repl", d) for d in range(1, group)]
    backs[0] = after(backs[0], terms[0])
    chunk = terms[0].astype(F32)
    for term in arrived:
        chunk = chunk + term.astype(F32)
    rounded = lax.optimization_barrier(chunk.astype(BF16))

    far, relay, own, near_share, joined = sparse_scatter(index, vals, backs)
    relay_in = mirrored(relay, 1)
    far_in = mirrored(far, -2)
    near_in = mirrored(near_share, 1)
    (joined,) = summed([joined, relay_in], [0, 0], panel_blocks, 1)
    joined_in = mirrored(after(joined, far_in), 2)
    owned = summed([own, far_in, near_in, joined_in], [0] * 4, block_rows, group)
    gathered = [owned[0]] + [swapped(owned[d], "repl", d) for d in range(1, group)]
    grad_rows = placed(where, gathered)

    rounded = after(rounded, own)
    masks = [1 << n for n in range(cycle.bit_length() - 1)]
    masks[:2] = masks[1::-1]
    waits = {masks[-1]: owned[0], masks[0]: joined}
    for mask in masks:
        other = swapped(rounded, "blk", mask)
        if mask in waits:
            rounded = after(rounded, waits[mask])
        chunk = rounded.astype(F32) + other.astype(F32)
        rounded = lax.optimization_barrier(chunk.astype(BF16))
    chunks = [rounded] + [swapped(rounded, "repl", d) for d in range(1, group)]
    scale = 1.0 / math.sqrt(node_rows * group * cycle)
    weight_grad = rows_placed(after(where, grad_rows), chunks, scale)
    return (output, weight_grad, grad_rows)


def solution(mesh):
    in_specs = (
        P(("blk", "repl"), None),
        P(),
        P(("blk", "repl"), None, None, None),
        P(("blk", "repl"), None),
        P(("blk", "repl")),
        P(("blk", "repl"), None),
    )
    out_specs = (P(("blk", "repl"), None), P(), P(("blk", "repl"), None))
    return jax.shard_map(local, mesh=mesh, in_specs=in_specs, out_specs=out_specs, check_vma=False)
```

```python
import functools
import math

import jax
import jax.numpy as jnp
from jax import lax
from jax.experimental import pallas as pl
from jax.experimental.pallas import tpu as pltpu
from jax.sharding import PartitionSpec as P

TILE = 128
REACH = 2
SPAN = 2 * REACH + 1
VMEM_LIMIT = 32 * 1024 * 1024
PARAMS = pltpu.CompilerParams(vmem_limit_bytes=VMEM_LIMIT)
FIRST_PARAMS = pltpu.CompilerParams(vmem_limit_bytes=60 * 1024 * 1024)
EXTRA = 16
BF16 = jnp.bfloat16
F32 = jnp.float32


def mirrored(value, steps):
    count = lax.axis_size("blk")
    pairs = [(k, (k + steps * (1 - 2 * (k & 1))) % count) for k in range(count)]
    return lax.ppermute(value, "blk", pairs)


def after(value, *others):
    return lax.optimization_barrier((value, *others))[0]


def swapped(value, axis, mask):
    count = lax.axis_size(axis)
    return lax.ppermute(value, axis, [(source, source ^ mask) for source in range(count)])


def spec_smem():
    return pl.BlockSpec(memory_space=pltpu.SMEM)


def spec_vmem():
    return pl.BlockSpec(memory_space=pltpu.VMEM)


def spec_hbm():
    return pl.BlockSpec(memory_space=pltpu.HBM)


def cost(flops, bytes_accessed):
    return pl.CostEstimate(flops=flops, bytes_accessed=bytes_accessed, transcendentals=0)


def split_kernel(panel_blocks, cycle, cols_hbm, count_hbm, feats_hbm, *refs):
    cols_ref, count_ref, place_ref, sems = refs[-4:]
    outs = refs[:-4]
    group = len(outs)
    rows, width = feats_hbm.shape[0], outs[0].shape[1]
    block_rows, slots = cols_ref.shape
    rank = lax.axis_index("repl")
    center = lax.axis_index("blk")
    small = [
        pltpu.make_async_copy(cols_hbm, cols_ref, sems.at[group]),
        pltpu.make_async_copy(count_hbm, count_ref, sems.at[group + 1]),
    ]
    large = []
    for d, out_ref in enumerate(outs):
        start = pl.multiple_of((rank ^ d) * width, width)
        large.append(
            pltpu.make_async_copy(
                feats_hbm.at[:, pl.ds(start, width)], out_ref.at[pl.ds(0, rows)], sems.at[d]
            )
        )
    for copy in small + large:
        copy.start()
    for copy in small:
        copy.wait()
    sign = 1 - 2 * (center & 1)
    cols = cols_ref[...]
    offset = (cols // panel_blocks - center) & (cycle - 1)
    offset = jnp.where(offset > REACH, offset - cycle, offset) * sign
    place = (offset + REACH) * panel_blocks + (cols & (panel_blocks - 1))
    row = lax.broadcasted_iota(jnp.int32, cols.shape, 0)
    slot = lax.broadcasted_iota(jnp.int32, cols.shape, 1)
    live = jnp.zeros(cols.shape, jnp.int32)
    for r in range(block_rows):
        live = jnp.where(row == r, count_ref[r], live)
    place = jnp.where(slot < live, place, SPAN * panel_blocks)
    place_ref[...] = jnp.zeros_like(place_ref)
    place_ref[pl.ds(0, block_rows), pl.ds(0, slots)] = place.astype(F32)
    for out_ref in outs:
        out_ref[pl.ds(rows, EXTRA), :] = place_ref[...].astype(BF16)
    for copy in large:
        copy.wait()


def split_columns(feats, tile_cols, tile_count, panel_blocks, cycle, group):
    rows, columns = feats.shape
    width = columns // group
    return pl.pallas_call(
        functools.partial(split_kernel, panel_blocks, cycle),
        in_specs=[spec_hbm()] * 3,
        out_shape=[jax.ShapeDtypeStruct((rows + EXTRA, width), feats.dtype)] * group,
        scratch_shapes=[
            pltpu.VMEM(tile_cols.shape, jnp.int32),
            pltpu.SMEM(tile_count.shape, jnp.int32),
            pltpu.VMEM((EXTRA, width), F32),
            pltpu.SemaphoreType.DMA((group + 2,)),
        ],
        compiler_params=FIRST_PARAMS,
        cost_estimate=cost(0, 2 * rows * columns * 2),
    )(tile_cols, tile_count, feats)


def place_rows(piece, rows, block_rows, spare):
    place = piece[pl.ds(rows, EXTRA), :].astype(F32).astype(jnp.int32)[:block_rows]
    return jnp.where(place < spare, place ^ (lax.axis_index("repl") * block_rows), place)


def join_near_kernel(block_rows, spare, own_hbm, *refs):
    *pieces, part_ref, index_ref, own_ref, sem = refs
    copy = pltpu.make_async_copy(own_hbm, own_ref, sem)
    copy.start()
    rows = own_ref.shape[0] - EXTRA
    for d, piece in enumerate(pieces, 1):
        part_ref[pl.ds(d * rows, rows), :] = piece[pl.ds(0, rows), :]
        place = place_rows(piece, rows, block_rows, spare)
        index_ref[pl.ds(d * block_rows, block_rows), :] = place
    copy.wait()
    part_ref[pl.ds(0, rows), :] = own_ref[pl.ds(0, rows), :]
    index_ref[pl.ds(0, block_rows), :] = place_rows(own_ref, rows, block_rows, spare)


def join_near(pieces, block_rows, spare):
    rows, width = pieces[0].shape
    count = len(pieces)
    shape = (count * (rows - EXTRA), width)
    return pl.pallas_call(
        functools.partial(join_near_kernel, block_rows, spare),
        in_specs=[spec_hbm()] + [spec_vmem()] * (count - 1),
        out_shape=[
            jax.ShapeDtypeStruct(shape, BF16),
            jax.ShapeDtypeStruct((count * block_rows, width), jnp.int32),
        ],
        scratch_shapes=[pltpu.VMEM((rows, width), BF16), pltpu.SemaphoreType.DMA(())],
        compiler_params=PARAMS,
        cost_estimate=cost(0, 4 * shape[0] * width),
    )(*pieces)


def join_far_kernel(block_rows, spare, near_ref, near_index_ref, *refs):
    *pieces, part_ref, index_ref, whole_ref = refs
    begin = near_ref.shape[0]
    begin_index = near_index_ref.shape[0]
    rows = part_ref.shape[0] // len(pieces)
    whole_ref[pl.ds(0, begin), :] = near_ref[...]
    index_ref[pl.ds(0, begin_index), :] = near_index_ref[...]
    for d, piece in enumerate(pieces):
        values = piece[pl.ds(0, rows), :]
        part_ref[pl.ds(d * rows, rows), :] = values
        whole_ref[pl.ds(begin + d * rows, rows), :] = values
        place = place_rows(piece, rows, block_rows, spare)
        index_ref[pl.ds(begin_index + d * block_rows, block_rows), :] = place


def join_far(near_rows, near_index, pieces, block_rows, spare):
    rows, width = pieces[0].shape
    count = len(pieces)
    shape = (count * (rows - EXTRA), width)
    return pl.pallas_call(
        functools.partial(join_far_kernel, block_rows, spare),
        in_specs=[spec_vmem()] * (count + 2),
        out_shape=[
            jax.ShapeDtypeStruct(shape, BF16),
            jax.ShapeDtypeStruct((near_index.shape[0] + count * block_rows, width), jnp.int32),
            jax.ShapeDtypeStruct((near_rows.shape[0] + shape[0], width), BF16),
        ],
        compiler_params=PARAMS,
        cost_estimate=cost(0, 8 * shape[0] * width),
    )(near_rows, near_index, *pieces)


def window_kernel(places, *refs):
    pieces = refs[: len(places)]
    window, sems = refs[-2:]
    copies = [
        pltpu.make_async_copy(piece, window.at[pl.ds(place, piece.shape[0])], sems.at[n])
        for n, (piece, place) in enumerate(zip(pieces, places))
    ]
    for copy in copies:
        copy.start()
    if len(places) > 1:
        window[window.shape[0] - 1] = jnp.zeros(window.shape[1:], window.dtype)
    for copy in copies:
        copy.wait()


def window_with(pieces, places, blocks, window=None):
    _, tile, width = pieces[0].shape
    begun = [] if window is None else [window]
    return pl.pallas_call(
        functools.partial(window_kernel, places),
        in_specs=[spec_vmem()] * (len(pieces) + len(begun)),
        out_specs=spec_vmem(),
        out_shape=jax.ShapeDtypeStruct((blocks, tile, width), BF16),
        input_output_aliases={len(pieces): 0} if begun else {},
        scratch_shapes=[pltpu.SemaphoreType.DMA((len(pieces),))],
        compiler_params=PARAMS,
        cost_estimate=cost(0, 4 * sum(math.prod(piece.shape) for piece in pieces)),
    )(*pieces, *begun)


def stack_kernel(*refs):
    *pieces, out_ref, sems = refs
    copies = []
    base = 0
    for n, piece in enumerate(pieces):
        size = piece.shape[0]
        copies.append(pltpu.make_async_copy(piece, out_ref.at[pl.ds(base, size)], sems.at[n]))
        base += size
    for copy in copies:
        copy.start()
    for copy in copies:
        copy.wait()


def stacked(pieces):
    shape = (sum(piece.shape[0] for piece in pieces), *pieces[0].shape[1:])
    return pl.pallas_call(
        stack_kernel,
        in_specs=[spec_vmem()] * len(pieces),
        out_shape=jax.ShapeDtypeStruct(shape, BF16),
        scratch_shapes=[pltpu.SemaphoreType.DMA((len(pieces),))],
        compiler_params=PARAMS,
        cost_estimate=cost(0, 4 * math.prod(shape)),
    )(*pieces)


def gather_kernel(group, index, window, *refs):
    outs = refs[-group:]
    vals = refs[:-group]
    block_rows = outs[0].shape[0]
    part = vals[-1].shape[0]

    @pl.loop(0, part)
    def _(i):
        row = 0
        for val in vals:
            for b in range(0, val.shape[0], part):
                slots = range(val.shape[1])
                lhs = jnp.concatenate([val[b + i, s] for s in slots], axis=1)
                rhs = jnp.concatenate([window[index[row + i, s]] for s in slots], axis=0)
                made = jnp.dot(lhs, rhs, preferred_element_type=F32).astype(BF16)
                outs[row // block_rows][row % block_rows + i] = made
                row += part


def sparse_gather(index, vals, window, group):
    rows = sum(val.shape[0] for val in vals)
    slots = vals[0].shape[1]
    blocks, _, width = window.shape
    return pl.pallas_call(
        functools.partial(gather_kernel, group),
        in_specs=[spec_smem()] + [spec_vmem()] * (len(vals) + 1),
        out_shape=[jax.ShapeDtypeStruct((rows // group, TILE, width), BF16)] * group,
        compiler_params=PARAMS,
        cost_estimate=cost(
            rows * slots * TILE * TILE * width * 2,
            rows * slots * TILE * TILE * 2 + blocks * TILE * width * 2,
        ),
    )(index, window, *vals)


def prepare_kernel(group, weight_ref, rows_ref, turned_ref):
    width = weight_ref.shape[0] // group
    rank = lax.axis_index("repl")
    for d in range(group):
        start = pl.multiple_of((rank ^ d) * width, width)
        chunk = weight_ref[pl.ds(start, width), :]
        rows_ref[pl.ds(d * width, width), :] = chunk
        turned_ref[:, pl.ds(d * width, width)] = chunk.T


def prepared(weight, group):
    rows, columns = weight.shape
    return pl.pallas_call(
        functools.partial(prepare_kernel, group),
        in_specs=[spec_vmem()],
        out_shape=[
            jax.ShapeDtypeStruct((rows, columns), BF16),
            jax.ShapeDtypeStruct((columns, rows), BF16),
        ],
        compiler_params=PARAMS,
        cost_estimate=cost(0, 6 * rows * columns),
    )(weight)


def dense_kernel(group, *refs):
    parts = refs[:group]
    weight_ref, turned_ref, cotangent_ref, output_ref, slope_ref = refs[group : group + 5]
    backs = refs[group + 5 :]
    blocks, tile, width = parts[0].shape
    steps = 2
    blocks = blocks // steps
    rows = blocks * tile

    for g in range(steps):
        at = pl.ds(g * rows, rows)
        blocks_at = pl.ds(g * blocks, blocks)
        aggregate = jnp.concatenate([p[blocks_at].reshape(rows, width) for p in parts], axis=1)
        preact = jnp.dot(aggregate, weight_ref[...], preferred_element_type=F32)
        sigma = jax.nn.sigmoid(preact)
        output_ref[at, :] = (preact * sigma).astype(BF16)
        slope = sigma * (1.0 + preact * (1.0 - sigma))
        slope = (cotangent_ref[at, :].astype(F32) * slope).astype(BF16)
        slope_ref[at, :] = slope
        backward = jnp.dot(slope, turned_ref[...], preferred_element_type=F32).astype(BF16)
        for d in range(group):
            piece = backward[:, d * width : (d + 1) * width]
            backs[d][blocks_at] = piece.reshape(blocks, tile, width)


def dense(parts, weight, turned, cotangent):
    group = len(parts)
    node_rows, feat_out = cotangent.shape
    feat_in = weight.shape[0]
    return pl.pallas_call(
        functools.partial(dense_kernel, group),
        in_specs=[spec_vmem()] * (group + 3),
        out_shape=[jax.ShapeDtypeStruct((node_rows, feat_out), BF16)] * 2
        + [jax.ShapeDtypeStruct(parts[0].shape, BF16)] * group,
        compiler_params=PARAMS,
        cost_estimate=cost(
            4 * node_rows * feat_in * feat_out,
            2 * (5 * node_rows * feat_out + 2 * feat_in * feat_out),
        ),
    )(*parts, weight, turned, cotangent)


def term_kernel(slope_ref, *refs):
    group = len(refs) // 2
    slope = slope_ref[...]
    for d in range(group):
        part = refs[d][...].reshape(slope.shape[0], -1)
        term = lax.dot_general(part, slope, (((0,), (0,)), ((), ())), preferred_element_type=F32)
        refs[group + d][...] = term.astype(BF16)


def weight_terms(parts, slope):
    group = len(parts)
    width = parts[0].shape[-1]
    node_rows, feat_out = slope.shape
    return pl.pallas_call(
        term_kernel,
        in_specs=[spec_vmem()] * (group + 1),
        out_shape=[jax.ShapeDtypeStruct((width, feat_out), BF16)] * group,
        compiler_params=PARAMS,
        cost_estimate=cost(
            2 * node_rows * width * group * feat_out, 2 * 3 * node_rows * feat_out
        ),
    )(slope, *parts)


def scatter_kernel(group, cuts, index, *refs):
    total = refs[-1]
    outs = refs[-1 - len(cuts) : -1]
    backs = refs[-1 - len(cuts) - group : -1 - len(cuts)]
    vals = refs[: -1 - len(cuts) - group]
    block_rows = backs[0].shape[0]
    part = vals[-1].shape[0]
    total[...] = jnp.zeros_like(total)

    @pl.loop(0, part)
    def _(i):
        row = 0
        for val in vals:
            for b in range(0, val.shape[0], part):
                turned = backs[row // block_rows][row % block_rows + i].T
                for s in range(0, val.shape[1], 2):
                    rhs = jnp.concatenate([val[b + i, s], val[b + i, s + 1]], axis=1)
                    made = jnp.dot(turned, rhs, preferred_element_type=F32)
                    total[index[row + i, s]] += made[:, :TILE]
                    total[index[row + i, s + 1]] += made[:, TILE:]
                row += part

    for out_ref, (start, size) in zip(outs, cuts):
        out_ref[...] = total[pl.ds(start, size)].astype(BF16)


def sparse_scatter(index, vals, backs, cuts):
    group = len(backs)
    rows = sum(val.shape[0] for val in vals)
    slots = vals[0].shape[1]
    width = backs[0].shape[-1]
    return pl.pallas_call(
        functools.partial(scatter_kernel, group, cuts),
        in_specs=[spec_smem()] + [spec_vmem()] * (len(vals) + group),
        out_shape=[jax.ShapeDtypeStruct((size, width, TILE), BF16) for _, size in cuts],
        scratch_shapes=[pltpu.VMEM((SPAN * rows + 1, width, TILE), F32)],
        compiler_params=PARAMS,
        cost_estimate=cost(
            rows * slots * TILE * TILE * width * 2,
            rows * slots * TILE * TILE * 2 + 6 * rows * TILE * width * 2,
        ),
    )(index, *vals, *backs)


def sum_kernel(bases, size, *refs):
    terms = refs[: len(bases)]
    for n, out_ref in enumerate(refs[len(bases) :]):
        total = jnp.zeros(out_ref.shape, F32)
        for ref, base in zip(terms, bases):
            total += ref[pl.ds(base + n * size, size)].astype(F32)
        out_ref[...] = total.astype(BF16)


def summed(terms, bases, size, count):
    shape = (size, *terms[0].shape[1:])
    return pl.pallas_call(
        functools.partial(sum_kernel, bases, size),
        in_specs=[spec_vmem()] * len(terms),
        out_shape=[jax.ShapeDtypeStruct(shape, BF16)] * count,
        compiler_params=PARAMS,
        cost_estimate=cost(0, count * math.prod(shape) * 2 * (len(terms) + 1)),
    )(*terms)


def place_kernel(rank_ref, *refs):
    out_ref = refs[-1]
    for d, ref in enumerate(refs[:-1]):
        blocks, width, tile = ref.shape
        start = pl.multiple_of((rank_ref[0] ^ d) * width, width)
        for b in range(blocks):
            out_ref[pl.ds(b * tile, tile), pl.ds(start, width)] = ref[b].T


def placed(rank, parts):
    blocks, width, tile = parts[0].shape
    shape = (blocks * tile, width * len(parts))
    return pl.pallas_call(
        place_kernel,
        in_specs=[spec_smem()] + [spec_vmem()] * len(parts),
        out_shape=jax.ShapeDtypeStruct(shape, BF16),
        compiler_params=PARAMS,
        cost_estimate=cost(0, 2 * 2 * shape[0] * shape[1]),
    )(rank, *parts)


def rows_kernel(scale, rank_ref, *refs):
    out_ref = refs[-1]
    for d, ref in enumerate(refs[:-1]):
        size = ref.shape[0]
        start = pl.multiple_of((rank_ref[0] ^ d) * size, size)
        out_ref[pl.ds(start, size), :] = ref[...].astype(F32) * scale


def rows_placed(rank, parts, scale):
    size, columns = parts[0].shape
    return pl.pallas_call(
        functools.partial(rows_kernel, scale),
        in_specs=[spec_smem()] + [spec_vmem()] * len(parts),
        out_shape=jax.ShapeDtypeStruct((size * len(parts), columns), F32),
        compiler_params=PARAMS,
        cost_estimate=cost(0, 6 * size * len(parts) * columns),
    )(rank, *parts)


def local(feats, weight, tile_vals, tile_cols, tile_count, cotangent):
    node_rows = feats.shape[0]
    cycle = lax.axis_size("blk")
    group = lax.axis_size("repl")
    assert group & (group - 1) == 0 and cycle & (cycle - 1) == 0
    block_rows = node_rows // TILE
    panel_blocks = block_rows * group
    spare = SPAN * panel_blocks
    far_side = group // 2
    where = jnp.reshape(lax.axis_index("repl"), (1,)).astype(jnp.int32)

    sent = split_columns(feats, tile_cols, tile_count, panel_blocks, cycle, group)
    mine = [sent[0]] + [swapped(sent[d], "repl", d) for d in range(1, group)]
    half = block_rows // 2
    ready = after(tile_vals, sent[1])
    own_vals = [ready[:half], ready[half:]]
    mine[1] = after(mine[1], *own_vals)
    near_rows, near_index = join_near(mine[:far_side], block_rows, spare)
    far_rows, index, rows = join_far(
        near_rows, near_index, mine[far_side:], block_rows, spare
    )
    near_part, far_part, panel = [
        value.reshape(-1, TILE, value.shape[-1]) for value in (near_rows, far_rows, rows)
    ]

    ahead_near = mirrored(near_part, -2)
    ahead = stacked([ahead_near, mirrored(after(far_part, ahead_near), -2)])
    beside = mirrored(panel, 1)
    behind = mirrored(after(panel, ahead), 2)
    relayed = mirrored(after(ahead, beside), 1)
    places = [n * panel_blocks for n in range(SPAN)]
    window = window_with([behind, panel, beside, ahead], [places[n] for n in (0, 2, 3, 4)], spare + 1)
    window = window_with([relayed], [places[1]], spare + 1, window)

    carried = [swapped(after(part, mine[far_side]), "repl", far_side) for part in own_vals]
    near = range(1, far_side)
    vals = own_vals + [swapped(after(tile_vals, sent[1]), "repl", d) for d in near]
    vals += carried + [swapped(part, "repl", d) for d in near for part in carried]
    columns = sparse_gather(index, vals, window, group)
    aggregate = [columns[0]] + [swapped(columns[d], "repl", d) for d in range(1, group)]

    made = dense(aggregate, *prepared(after(weight, panel), group), cotangent)
    output, slope, backs = made[0], made[1], made[2:]
    backs = [backs[0]] + [swapped(backs[d], "repl", d) for d in range(1, group)]

    terms = weight_terms(aggregate, after(slope, backs[1]))
    arrived = [swapped(terms[d], "repl", d) for d in range(1, group)]
    backs[0] = after(backs[0], terms[0])
    chunk = terms[0].astype(F32)
    for term in arrived:
        chunk = chunk + term.astype(F32)
    rounded = lax.optimization_barrier(chunk.astype(BF16))

    member = panel_blocks // 2
    cuts = [(places[n], panel_blocks) for n in (0, 1, 2, 4)]
    cuts += [(places[3] + member, member), (places[3], member)]
    far, relay, own, joined, *beside_shares = sparse_scatter(index, vals, backs, cuts)
    relay_in = mirrored(relay, 1)
    far_in = mirrored(far, -2)
    (joined,) = summed([joined, relay_in], [0, 0], panel_blocks, 1)
    joined_in = mirrored(after(joined, far_in), 2)

    masks = [1 << n for n in range(cycle.bit_length() - 1)]
    masks[:2] = masks[1::-1]
    sums = [after(rounded, own)]
    others = []
    beside_in = [mirrored(beside_shares[0], 1)]
    for mask in masks:
        others.append(swapped(sums[-1], "blk", mask))
        if mask == masks[-1]:
            break
        base = after(sums[-1], joined if mask == masks[0] else beside_in[0])
        chunk = base.astype(F32) + others[-1].astype(F32)
        sums.append(lax.optimization_barrier(chunk.astype(BF16)))
        if mask == masks[0]:
            beside_in.append(mirrored(after(beside_shares[1], sums[-1]), 1))
    owned = []
    for n in (1, 0):
        terms = [own, far_in, joined_in, beside_in[1 - n]]
        base = n * member
        owned = [*summed(terms, [base, base, base, 0], block_rows, far_side), *owned]
    gathered = [owned[0]] + [swapped(owned[d], "repl", d) for d in range(1, group)]
    grad_rows = placed(where, gathered)
    chunk = after(sums[-1], owned[far_side]).astype(F32) + others[-1].astype(F32)
    rounded = lax.optimization_barrier(chunk.astype(BF16))
    chunks = [rounded] + [swapped(rounded, "repl", d) for d in range(1, group)]
    scale = 1.0 / math.sqrt(node_rows * group * cycle)
    weight_grad = rows_placed(after(where, grad_rows), chunks, scale)
    return (output, weight_grad, grad_rows)


def solution(mesh):
    in_specs = (
        P(("blk", "repl"), None),
        P(),
        P(("blk", "repl"), None, None, None),
        P(("blk", "repl"), None),
        P(("blk", "repl")),
        P(("blk", "repl"), None),
    )
    out_specs = (P(("blk", "repl"), None), P(), P(("blk", "repl"), None))
    return jax.shard_map(local, mesh=mesh, in_specs=in_specs, out_specs=out_specs, check_vma=False)
```

```python
import functools
import math

import jax
import jax.numpy as jnp
from jax import lax
from jax.experimental import pallas as pl
from jax.experimental.pallas import tpu as pltpu
from jax.sharding import PartitionSpec as P

TILE = 128
REACH = 2
SPAN = 2 * REACH + 1
VMEM_LIMIT = 32 * 1024 * 1024
PARAMS = pltpu.CompilerParams(vmem_limit_bytes=VMEM_LIMIT)
FIRST_PARAMS = pltpu.CompilerParams(vmem_limit_bytes=60 * 1024 * 1024)
EXTRA = 16
BF16 = jnp.bfloat16
F32 = jnp.float32


def mirrored(value, steps):
    count = lax.axis_size("blk")
    pairs = [(k, (k + steps * (1 - 2 * (k & 1))) % count) for k in range(count)]
    return lax.ppermute(value, "blk", pairs)


def after(value, *others):
    return lax.optimization_barrier((value, *others))[0]


def swapped(value, axis, mask):
    count = lax.axis_size(axis)
    return lax.ppermute(value, axis, [(source, source ^ mask) for source in range(count)])


def spec_smem():
    return pl.BlockSpec(memory_space=pltpu.SMEM)


def spec_vmem():
    return pl.BlockSpec(memory_space=pltpu.VMEM)


def spec_hbm():
    return pl.BlockSpec(memory_space=pltpu.HBM)


def cost(flops, bytes_accessed):
    return pl.CostEstimate(flops=flops, bytes_accessed=bytes_accessed, transcendentals=0)


def split_kernel(panel_blocks, cycle, cols_hbm, count_hbm, feats_hbm, *refs):
    cols_ref, count_ref, place_ref, sems = refs[-4:]
    outs = refs[:-4]
    group = len(outs)
    rows, width = feats_hbm.shape[0], outs[0].shape[1]
    block_rows, slots = cols_ref.shape
    rank = lax.axis_index("repl")
    center = lax.axis_index("blk")
    small = [
        pltpu.make_async_copy(cols_hbm, cols_ref, sems.at[group]),
        pltpu.make_async_copy(count_hbm, count_ref, sems.at[group + 1]),
    ]
    large = []
    for d, out_ref in enumerate(outs):
        start = pl.multiple_of((rank ^ d) * width, width)
        large.append(
            pltpu.make_async_copy(
                feats_hbm.at[:, pl.ds(start, width)], out_ref.at[pl.ds(0, rows)], sems.at[d]
            )
        )
    for copy in small + large:
        copy.start()
    for copy in small:
        copy.wait()
    sign = 1 - 2 * (center & 1)
    cols = cols_ref[...]
    offset = (cols // panel_blocks - center) & (cycle - 1)
    offset = jnp.where(offset > REACH, offset - cycle, offset) * sign
    place = (offset + REACH) * panel_blocks + (cols & (panel_blocks - 1))
    row = lax.broadcasted_iota(jnp.int32, cols.shape, 0)
    slot = lax.broadcasted_iota(jnp.int32, cols.shape, 1)
    live = jnp.zeros(cols.shape, jnp.int32)
    for r in range(block_rows):
        live = jnp.where(row == r, count_ref[r], live)
    place = jnp.where(slot < live, place, SPAN * panel_blocks)
    place_ref[...] = jnp.zeros_like(place_ref)
    place_ref[pl.ds(0, block_rows), pl.ds(0, slots)] = place.astype(F32)
    for out_ref in outs:
        out_ref[pl.ds(rows, EXTRA), :] = place_ref[...].astype(BF16)
    for copy in large:
        copy.wait()


def split_columns(feats, tile_cols, tile_count, panel_blocks, cycle, group):
    rows, columns = feats.shape
    width = columns // group
    return pl.pallas_call(
        functools.partial(split_kernel, panel_blocks, cycle),
        in_specs=[spec_hbm()] * 3,
        out_shape=[jax.ShapeDtypeStruct((rows + EXTRA, width), feats.dtype)] * group,
        scratch_shapes=[
            pltpu.VMEM(tile_cols.shape, jnp.int32),
            pltpu.SMEM(tile_count.shape, jnp.int32),
            pltpu.VMEM((EXTRA, width), F32),
            pltpu.SemaphoreType.DMA((group + 2,)),
        ],
        compiler_params=FIRST_PARAMS,
        cost_estimate=cost(0, 2 * rows * columns * 2),
    )(tile_cols, tile_count, feats)


def place_rows(piece, rows, block_rows, spare):
    place = piece[pl.ds(rows, EXTRA), :].astype(F32).astype(jnp.int32)[:block_rows]
    return jnp.where(place < spare, place ^ (lax.axis_index("repl") * block_rows), place)


def join_near_kernel(block_rows, spare, own_hbm, *refs):
    *pieces, part_ref, index_ref, own_ref, sem = refs
    copy = pltpu.make_async_copy(own_hbm, own_ref, sem)
    copy.start()
    rows = own_ref.shape[0] - EXTRA
    for d, piece in enumerate(pieces, 1):
        part_ref[pl.ds(d * rows, rows), :] = piece[pl.ds(0, rows), :]
        place = place_rows(piece, rows, block_rows, spare)
        index_ref[pl.ds(d * block_rows, block_rows), :] = place
    copy.wait()
    part_ref[pl.ds(0, rows), :] = own_ref[pl.ds(0, rows), :]
    index_ref[pl.ds(0, block_rows), :] = place_rows(own_ref, rows, block_rows, spare)


def join_near(pieces, block_rows, spare):
    rows, width = pieces[0].shape
    count = len(pieces)
    shape = (count * (rows - EXTRA), width)
    return pl.pallas_call(
        functools.partial(join_near_kernel, block_rows, spare),
        in_specs=[spec_hbm()] + [spec_vmem()] * (count - 1),
        out_shape=[
            jax.ShapeDtypeStruct(shape, BF16),
            jax.ShapeDtypeStruct((count * block_rows, width), jnp.int32),
        ],
        scratch_shapes=[pltpu.VMEM((rows, width), BF16), pltpu.SemaphoreType.DMA(())],
        compiler_params=PARAMS,
        cost_estimate=cost(0, 4 * shape[0] * width),
    )(*pieces)


def join_far_kernel(block_rows, spare, near_ref, near_index_ref, *refs):
    *pieces, part_ref, index_ref, whole_ref = refs
    begin = near_ref.shape[0]
    begin_index = near_index_ref.shape[0]
    rows = part_ref.shape[0] // len(pieces)
    whole_ref[pl.ds(0, begin), :] = near_ref[...]
    index_ref[pl.ds(0, begin_index), :] = near_index_ref[...]
    for d, piece in enumerate(pieces):
        values = piece[pl.ds(0, rows), :]
        part_ref[pl.ds(d * rows, rows), :] = values
        whole_ref[pl.ds(begin + d * rows, rows), :] = values
        place = place_rows(piece, rows, block_rows, spare)
        index_ref[pl.ds(begin_index + d * block_rows, block_rows), :] = place


def join_far(near_rows, near_index, pieces, block_rows, spare):
    rows, width = pieces[0].shape
    count = len(pieces)
    shape = (count * (rows - EXTRA), width)
    return pl.pallas_call(
        functools.partial(join_far_kernel, block_rows, spare),
        in_specs=[spec_vmem()] * (count + 2),
        out_shape=[
            jax.ShapeDtypeStruct(shape, BF16),
            jax.ShapeDtypeStruct((near_index.shape[0] + count * block_rows, width), jnp.int32),
            jax.ShapeDtypeStruct((near_rows.shape[0] + shape[0], width), BF16),
        ],
        compiler_params=PARAMS,
        cost_estimate=cost(0, 8 * shape[0] * width),
    )(near_rows, near_index, *pieces)


def window_kernel(places, *refs):
    pieces = refs[: len(places)]
    window, sems = refs[-2:]
    copies = [
        pltpu.make_async_copy(piece, window.at[pl.ds(place, piece.shape[0])], sems.at[n])
        for n, (piece, place) in enumerate(zip(pieces, places))
    ]
    for copy in copies:
        copy.start()
    if len(places) > 1:
        window[window.shape[0] - 1] = jnp.zeros(window.shape[1:], window.dtype)
    for copy in copies:
        copy.wait()


def window_with(pieces, places, blocks, window=None):
    _, tile, width = pieces[0].shape
    begun = [] if window is None else [window]
    return pl.pallas_call(
        functools.partial(window_kernel, places),
        in_specs=[spec_vmem()] * (len(pieces) + len(begun)),
        out_specs=spec_vmem(),
        out_shape=jax.ShapeDtypeStruct((blocks, tile, width), BF16),
        input_output_aliases={len(pieces): 0} if begun else {},
        scratch_shapes=[pltpu.SemaphoreType.DMA((len(pieces),))],
        compiler_params=PARAMS,
        cost_estimate=cost(0, 4 * sum(math.prod(piece.shape) for piece in pieces)),
    )(*pieces, *begun)


def stack_kernel(*refs):
    *pieces, out_ref, sems = refs
    copies = []
    base = 0
    for n, piece in enumerate(pieces):
        size = piece.shape[0]
        copies.append(pltpu.make_async_copy(piece, out_ref.at[pl.ds(base, size)], sems.at[n]))
        base += size
    for copy in copies:
        copy.start()
    for copy in copies:
        copy.wait()


def stacked(pieces):
    shape = (sum(piece.shape[0] for piece in pieces), *pieces[0].shape[1:])
    return pl.pallas_call(
        stack_kernel,
        in_specs=[spec_vmem()] * len(pieces),
        out_shape=jax.ShapeDtypeStruct(shape, BF16),
        scratch_shapes=[pltpu.SemaphoreType.DMA((len(pieces),))],
        compiler_params=PARAMS,
        cost_estimate=cost(0, 4 * math.prod(shape)),
    )(*pieces)


def gather_kernel(group, index, window, *refs):
    outs = refs[-group:]
    vals = refs[:-group]
    block_rows = outs[0].shape[0]
    part = vals[-1].shape[0]

    @pl.loop(0, part)
    def _(i):
        row = 0
        for val in vals:
            for b in range(0, val.shape[0], part):
                slots = range(val.shape[1])
                lhs = jnp.concatenate([val[b + i, s] for s in slots], axis=1)
                rhs = jnp.concatenate([window[index[row + i, s]] for s in slots], axis=0)
                made = jnp.dot(lhs, rhs, preferred_element_type=F32).astype(BF16)
                outs[row // block_rows][row % block_rows + i] = made
                row += part


def sparse_gather(index, vals, window, group):
    rows = sum(val.shape[0] for val in vals)
    slots = vals[0].shape[1]
    blocks, _, width = window.shape
    return pl.pallas_call(
        functools.partial(gather_kernel, group),
        in_specs=[spec_smem()] + [spec_vmem()] * (len(vals) + 1),
        out_shape=[jax.ShapeDtypeStruct((rows // group, TILE, width), BF16)] * group,
        compiler_params=PARAMS,
        cost_estimate=cost(
            rows * slots * TILE * TILE * width * 2,
            rows * slots * TILE * TILE * 2 + blocks * TILE * width * 2,
        ),
    )(index, window, *vals)


def prepare_kernel(group, weight_ref, rows_ref, turned_ref):
    width = weight_ref.shape[0] // group
    rank = lax.axis_index("repl")
    for d in range(group):
        start = pl.multiple_of((rank ^ d) * width, width)
        chunk = weight_ref[pl.ds(start, width), :]
        rows_ref[pl.ds(d * width, width), :] = chunk
        turned_ref[:, pl.ds(d * width, width)] = chunk.T


def prepared(weight, group):
    rows, columns = weight.shape
    return pl.pallas_call(
        functools.partial(prepare_kernel, group),
        in_specs=[spec_vmem()],
        out_shape=[
            jax.ShapeDtypeStruct((rows, columns), BF16),
            jax.ShapeDtypeStruct((columns, rows), BF16),
        ],
        compiler_params=PARAMS,
        cost_estimate=cost(0, 6 * rows * columns),
    )(weight)


def dense_kernel(group, *refs):
    parts = refs[:group]
    weight_ref, turned_ref, cotangent_ref, output_ref, slope_ref = refs[group : group + 5]
    backs = refs[group + 5 :]
    blocks, tile, width = parts[0].shape
    steps = 2
    blocks = blocks // steps
    rows = blocks * tile

    for g in range(steps):
        at = pl.ds(g * rows, rows)
        blocks_at = pl.ds(g * blocks, blocks)
        aggregate = jnp.concatenate([p[blocks_at].reshape(rows, width) for p in parts], axis=1)
        preact = jnp.dot(aggregate, weight_ref[...], preferred_element_type=F32)
        sigma = jax.nn.sigmoid(preact)
        output_ref[at, :] = (preact * sigma).astype(BF16)
        slope = sigma * (1.0 + preact * (1.0 - sigma))
        slope = (cotangent_ref[at, :].astype(F32) * slope).astype(BF16)
        slope_ref[at, :] = slope
        backward = jnp.dot(slope, turned_ref[...], preferred_element_type=F32).astype(BF16)
        for d in range(group):
            piece = backward[:, d * width : (d + 1) * width]
            backs[d][blocks_at] = piece.reshape(blocks, tile, width)


def dense(parts, weight, turned, cotangent):
    group = len(parts)
    node_rows, feat_out = cotangent.shape
    feat_in = weight.shape[0]
    return pl.pallas_call(
        functools.partial(dense_kernel, group),
        in_specs=[spec_vmem()] * (group + 3),
        out_shape=[jax.ShapeDtypeStruct((node_rows, feat_out), BF16)] * 2
        + [jax.ShapeDtypeStruct(parts[0].shape, BF16)] * group,
        compiler_params=PARAMS,
        cost_estimate=cost(
            4 * node_rows * feat_in * feat_out,
            2 * (5 * node_rows * feat_out + 2 * feat_in * feat_out),
        ),
    )(*parts, weight, turned, cotangent)


def term_kernel(slope_ref, *refs):
    group = len(refs) // 2
    slope = slope_ref[...]
    for d in range(group):
        part = refs[d][...].reshape(slope.shape[0], -1)
        term = lax.dot_general(part, slope, (((0,), (0,)), ((), ())), preferred_element_type=F32)
        refs[group + d][...] = term.astype(BF16)


def weight_terms(parts, slope):
    group = len(parts)
    width = parts[0].shape[-1]
    node_rows, feat_out = slope.shape
    return pl.pallas_call(
        term_kernel,
        in_specs=[spec_vmem()] * (group + 1),
        out_shape=[jax.ShapeDtypeStruct((width, feat_out), BF16)] * group,
        compiler_params=PARAMS,
        cost_estimate=cost(
            2 * node_rows * width * group * feat_out, 2 * 3 * node_rows * feat_out
        ),
    )(slope, *parts)


def scatter_kernel(group, cuts, index, *refs):
    total = refs[-1]
    outs = refs[-1 - len(cuts) : -1]
    backs = refs[-1 - len(cuts) - group : -1 - len(cuts)]
    vals = refs[: -1 - len(cuts) - group]
    block_rows = backs[0].shape[0]
    part = vals[-1].shape[0]
    total[...] = jnp.zeros_like(total)

    @pl.loop(0, part)
    def _(i):
        row = 0
        for val in vals:
            for b in range(0, val.shape[0], part):
                turned = backs[row // block_rows][row % block_rows + i].T
                for s in range(0, val.shape[1], 2):
                    rhs = jnp.concatenate([val[b + i, s], val[b + i, s + 1]], axis=1)
                    made = jnp.dot(turned, rhs, preferred_element_type=F32)
                    total[index[row + i, s]] += made[:, :TILE]
                    total[index[row + i, s + 1]] += made[:, TILE:]
                row += part

    for out_ref, (start, size) in zip(outs, cuts):
        out_ref[...] = total[pl.ds(start, size)].astype(BF16)


def sparse_scatter(index, vals, backs, cuts):
    group = len(backs)
    rows = sum(val.shape[0] for val in vals)
    slots = vals[0].shape[1]
    width = backs[0].shape[-1]
    return pl.pallas_call(
        functools.partial(scatter_kernel, group, cuts),
        in_specs=[spec_smem()] + [spec_vmem()] * (len(vals) + group),
        out_shape=[jax.ShapeDtypeStruct((size, width, TILE), BF16) for _, size in cuts],
        scratch_shapes=[pltpu.VMEM((SPAN * rows + 1, width, TILE), F32)],
        compiler_params=PARAMS,
        cost_estimate=cost(
            rows * slots * TILE * TILE * width * 2,
            rows * slots * TILE * TILE * 2 + 6 * rows * TILE * width * 2,
        ),
    )(index, *vals, *backs)


def sum_kernel(bases, size, *refs):
    terms = refs[: len(bases)]
    for n, out_ref in enumerate(refs[len(bases) :]):
        total = jnp.zeros(out_ref.shape, F32)
        for ref, base in zip(terms, bases):
            total += ref[pl.ds(base + n * size, size)].astype(F32)
        out_ref[...] = total.astype(BF16)


def summed(terms, bases, size, count):
    shape = (size, *terms[0].shape[1:])
    return pl.pallas_call(
        functools.partial(sum_kernel, bases, size),
        in_specs=[spec_vmem()] * len(terms),
        out_shape=[jax.ShapeDtypeStruct(shape, BF16)] * count,
        compiler_params=PARAMS,
        cost_estimate=cost(0, count * math.prod(shape) * 2 * (len(terms) + 1)),
    )(*terms)


def place_kernel(rank_ref, *refs):
    out_ref = refs[-1]
    for d, ref in enumerate(refs[:-1]):
        blocks, width, tile = ref.shape
        start = pl.multiple_of((rank_ref[0] ^ d) * width, width)
        for b in range(blocks):
            out_ref[pl.ds(b * tile, tile), pl.ds(start, width)] = ref[b].T


def placed(rank, parts):
    blocks, width, tile = parts[0].shape
    shape = (blocks * tile, width * len(parts))
    return pl.pallas_call(
        place_kernel,
        in_specs=[spec_smem()] + [spec_vmem()] * len(parts),
        out_shape=jax.ShapeDtypeStruct(shape, BF16),
        compiler_params=PARAMS,
        cost_estimate=cost(0, 2 * 2 * shape[0] * shape[1]),
    )(rank, *parts)


def rows_kernel(scale, rank_ref, *refs):
    out_ref = refs[-1]
    for d, ref in enumerate(refs[:-1]):
        size = ref.shape[0]
        start = pl.multiple_of((rank_ref[0] ^ d) * size, size)
        out_ref[pl.ds(start, size), :] = ref[...].astype(F32) * scale


def rows_placed(rank, parts, scale):
    size, columns = parts[0].shape
    return pl.pallas_call(
        functools.partial(rows_kernel, scale),
        in_specs=[spec_smem()] + [spec_vmem()] * len(parts),
        out_shape=jax.ShapeDtypeStruct((size * len(parts), columns), F32),
        compiler_params=PARAMS,
        cost_estimate=cost(0, 6 * size * len(parts) * columns),
    )(rank, *parts)


def local(feats, weight, tile_vals, tile_cols, tile_count, cotangent):
    node_rows = feats.shape[0]
    cycle = lax.axis_size("blk")
    group = lax.axis_size("repl")
    assert group & (group - 1) == 0 and cycle & (cycle - 1) == 0
    block_rows = node_rows // TILE
    panel_blocks = block_rows * group
    spare = SPAN * panel_blocks
    far_side = group // 2
    where = jnp.reshape(lax.axis_index("repl"), (1,)).astype(jnp.int32)

    sent = split_columns(feats, tile_cols, tile_count, panel_blocks, cycle, group)
    mine = [sent[0]] + [swapped(sent[d], "repl", d) for d in range(1, group)]
    half = block_rows // 2
    ready = after(tile_vals, mine[1])
    own_vals = [ready[:half], ready[half:]]
    mine[far_side] = after(mine[far_side], *own_vals)
    near_rows, near_index = join_near(mine[:far_side], block_rows, spare)
    far_rows, index, rows = join_far(
        near_rows, near_index, mine[far_side:], block_rows, spare
    )
    near_part, far_part, panel = [
        value.reshape(-1, TILE, value.shape[-1]) for value in (near_rows, far_rows, rows)
    ]

    ahead_near = mirrored(near_part, -2)
    ahead = stacked([ahead_near, mirrored(after(far_part, ahead_near), -2)])
    beside = mirrored(panel, 1)
    behind = mirrored(after(panel, ahead), 2)
    relayed = mirrored(after(ahead, beside), 1)
    places = [n * panel_blocks for n in range(SPAN)]
    window = window_with([behind, panel, beside, ahead], [places[n] for n in (0, 2, 3, 4)], spare + 1)
    window = window_with([relayed], [places[1]], spare + 1, window)

    carried = [swapped(after(part, mine[far_side]), "repl", far_side) for part in own_vals]
    near = range(1, far_side)
    vals = own_vals + [swapped(after(tile_vals, sent[1]), "repl", d) for d in near]
    vals += carried + [swapped(part, "repl", d) for d in near for part in carried]
    columns = sparse_gather(index, vals, window, group)
    aggregate = [columns[0]] + [swapped(columns[d], "repl", d) for d in range(1, group)]

    made = dense(aggregate, *prepared(after(weight, panel), group), cotangent)
    output, slope, backs = made[0], made[1], made[2:]
    backs = [backs[0]] + [swapped(backs[d], "repl", d) for d in range(1, group)]

    terms = weight_terms(aggregate, after(slope, backs[1]))
    arrived = [swapped(terms[d], "repl", d) for d in range(1, group)]
    backs[0] = after(backs[0], terms[0])
    chunk = terms[0].astype(F32)
    for term in arrived:
        chunk = chunk + term.astype(F32)
    rounded = lax.optimization_barrier(chunk.astype(BF16))

    member = panel_blocks // 2
    cuts = [(places[n], panel_blocks) for n in (0, 1, 2, 4)]
    cuts += [(places[3] + member, member), (places[3], member)]
    far, relay, own, joined, *beside_shares = sparse_scatter(index, vals, backs, cuts)
    relay_in = mirrored(relay, 1)
    far_in = mirrored(far, -2)
    (joined,) = summed([joined, relay_in], [0, 0], panel_blocks, 1)
    joined_in = mirrored(after(joined, far_in), 2)

    masks = [1 << n for n in range(cycle.bit_length() - 1)]
    masks[:2] = masks[1::-1]
    sums = [after(rounded, own)]
    others = []
    beside_in = [mirrored(beside_shares[0], 1)]
    for mask in masks:
        others.append(swapped(sums[-1], "blk", mask))
        if mask == masks[-1]:
            break
        base = after(sums[-1], joined if mask == masks[0] else beside_in[0])
        chunk = base.astype(F32) + others[-1].astype(F32)
        sums.append(lax.optimization_barrier(chunk.astype(BF16)))
        if mask == masks[0]:
            beside_in.append(mirrored(after(beside_shares[1], sums[-1]), 1))
    owned = []
    for n in (1, 0):
        terms = [own, far_in, joined_in, beside_in[1 - n]]
        base = n * member
        owned = [*summed(terms, [base, base, base, 0], block_rows, far_side), *owned]
    gathered = [owned[0]] + [swapped(owned[d], "repl", d) for d in range(1, group)]
    grad_rows = placed(where, gathered)
    chunk = after(sums[-1], owned[far_side]).astype(F32) + others[-1].astype(F32)
    rounded = lax.optimization_barrier(chunk.astype(BF16))
    chunks = [rounded] + [swapped(rounded, "repl", d) for d in range(1, group)]
    scale = 1.0 / math.sqrt(node_rows * group * cycle)
    weight_grad = rows_placed(after(where, grad_rows), chunks, scale)
    return (output, weight_grad, grad_rows)


def solution(mesh):
    in_specs = (
        P(("blk", "repl"), None),
        P(),
        P(("blk", "repl"), None, None, None),
        P(("blk", "repl"), None),
        P(("blk", "repl")),
        P(("blk", "repl"), None),
    )
    out_specs = (P(("blk", "repl"), None), P(), P(("blk", "repl"), None))
    return jax.shard_map(local, mesh=mesh, in_specs=in_specs, out_specs=out_specs, check_vma=False)
```

```python
import functools
import math

import jax
import jax.numpy as jnp
from jax import lax
from jax.experimental import pallas as pl
from jax.experimental.pallas import tpu as pltpu
from jax.sharding import PartitionSpec as P

TILE = 128
REACH = 2
SPAN = 2 * REACH + 1
VMEM_LIMIT = 32 * 1024 * 1024
PARAMS = pltpu.CompilerParams(vmem_limit_bytes=VMEM_LIMIT)
FIRST_PARAMS = pltpu.CompilerParams(vmem_limit_bytes=60 * 1024 * 1024)
EXTRA = 16
BF16 = jnp.bfloat16
F32 = jnp.float32


def mirrored(value, steps):
    count = lax.axis_size("blk")
    pairs = [(k, (k + steps * (1 - 2 * (k & 1))) % count) for k in range(count)]
    return lax.ppermute(value, "blk", pairs)


def after(value, *others):
    return lax.optimization_barrier((value, *others))[0]


def swapped(value, axis, mask):
    count = lax.axis_size(axis)
    return lax.ppermute(value, axis, [(source, source ^ mask) for source in range(count)])


def spec_smem():
    return pl.BlockSpec(memory_space=pltpu.SMEM)


def spec_vmem():
    return pl.BlockSpec(memory_space=pltpu.VMEM)


def spec_hbm():
    return pl.BlockSpec(memory_space=pltpu.HBM)


def cost(flops, bytes_accessed):
    return pl.CostEstimate(flops=flops, bytes_accessed=bytes_accessed, transcendentals=0)


def split_kernel(panel_blocks, cycle, cols_hbm, count_hbm, feats_hbm, *refs):
    cols_ref, count_ref, place_ref, sems = refs[-4:]
    outs = refs[:-4]
    group = len(outs)
    rows, width = feats_hbm.shape[0], outs[0].shape[1]
    block_rows, slots = cols_ref.shape
    rank = lax.axis_index("repl")
    center = lax.axis_index("blk")
    small = [
        pltpu.make_async_copy(cols_hbm, cols_ref, sems.at[group]),
        pltpu.make_async_copy(count_hbm, count_ref, sems.at[group + 1]),
    ]
    large = []
    for d, out_ref in enumerate(outs):
        start = pl.multiple_of((rank ^ d) * width, width)
        large.append(
            pltpu.make_async_copy(
                feats_hbm.at[:, pl.ds(start, width)], out_ref.at[pl.ds(0, rows)], sems.at[d]
            )
        )
    for copy in small + large:
        copy.start()
    for copy in small:
        copy.wait()
    sign = 1 - 2 * (center & 1)
    cols = cols_ref[...]
    offset = (cols // panel_blocks - center) & (cycle - 1)
    offset = jnp.where(offset > REACH, offset - cycle, offset) * sign
    place = (offset + REACH) * panel_blocks + (cols & (panel_blocks - 1))
    row = lax.broadcasted_iota(jnp.int32, cols.shape, 0)
    slot = lax.broadcasted_iota(jnp.int32, cols.shape, 1)
    live = jnp.zeros(cols.shape, jnp.int32)
    for r in range(block_rows):
        live = jnp.where(row == r, count_ref[r], live)
    place = jnp.where(slot < live, place, SPAN * panel_blocks)
    place_ref[...] = jnp.zeros_like(place_ref)
    place_ref[pl.ds(0, block_rows), pl.ds(0, slots)] = place.astype(F32)
    for out_ref in outs:
        out_ref[pl.ds(rows, EXTRA), :] = place_ref[...].astype(BF16)
    for copy in large:
        copy.wait()


def split_columns(feats, tile_cols, tile_count, panel_blocks, cycle, group):
    rows, columns = feats.shape
    width = columns // group
    return pl.pallas_call(
        functools.partial(split_kernel, panel_blocks, cycle),
        in_specs=[spec_hbm()] * 3,
        out_shape=[jax.ShapeDtypeStruct((rows + EXTRA, width), feats.dtype)] * group,
        scratch_shapes=[
            pltpu.VMEM(tile_cols.shape, jnp.int32),
            pltpu.SMEM(tile_count.shape, jnp.int32),
            pltpu.VMEM((EXTRA, width), F32),
            pltpu.SemaphoreType.DMA((group + 2,)),
        ],
        compiler_params=FIRST_PARAMS,
        cost_estimate=cost(0, 2 * rows * columns * 2),
    )(tile_cols, tile_count, feats)


def place_rows(piece, rows, block_rows, spare):
    place = piece[pl.ds(rows, EXTRA), :].astype(F32).astype(jnp.int32)[:block_rows]
    return jnp.where(place < spare, place ^ (lax.axis_index("repl") * block_rows), place)


def join_near_kernel(block_rows, spare, own_hbm, *refs):
    *pieces, part_ref, index_ref, own_ref, sem = refs
    copy = pltpu.make_async_copy(own_hbm, own_ref, sem)
    copy.start()
    rows = own_ref.shape[0] - EXTRA
    for d, piece in enumerate(pieces, 1):
        part_ref[pl.ds(d * rows, rows), :] = piece[pl.ds(0, rows), :]
        place = place_rows(piece, rows, block_rows, spare)
        index_ref[pl.ds(d * block_rows, block_rows), :] = place
    copy.wait()
    part_ref[pl.ds(0, rows), :] = own_ref[pl.ds(0, rows), :]
    index_ref[pl.ds(0, block_rows), :] = place_rows(own_ref, rows, block_rows, spare)


def join_near(pieces, block_rows, spare):
    rows, width = pieces[0].shape
    count = len(pieces)
    shape = (count * (rows - EXTRA), width)
    return pl.pallas_call(
        functools.partial(join_near_kernel, block_rows, spare),
        in_specs=[spec_hbm()] + [spec_vmem()] * (count - 1),
        out_shape=[
            jax.ShapeDtypeStruct(shape, BF16),
            jax.ShapeDtypeStruct((count * block_rows, width), jnp.int32),
        ],
        scratch_shapes=[pltpu.VMEM((rows, width), BF16), pltpu.SemaphoreType.DMA(())],
        compiler_params=PARAMS,
        cost_estimate=cost(0, 4 * shape[0] * width),
    )(*pieces)


def join_far_kernel(block_rows, spare, near_ref, near_index_ref, *refs):
    *pieces, part_ref, index_ref, whole_ref = refs
    begin = near_ref.shape[0]
    begin_index = near_index_ref.shape[0]
    rows = part_ref.shape[0] // len(pieces)
    whole_ref[pl.ds(0, begin), :] = near_ref[...]
    index_ref[pl.ds(0, begin_index), :] = near_index_ref[...]
    for d, piece in enumerate(pieces):
        values = piece[pl.ds(0, rows), :]
        part_ref[pl.ds(d * rows, rows), :] = values
        whole_ref[pl.ds(begin + d * rows, rows), :] = values
        place = place_rows(piece, rows, block_rows, spare)
        index_ref[pl.ds(begin_index + d * block_rows, block_rows), :] = place


def join_far(near_rows, near_index, pieces, block_rows, spare):
    rows, width = pieces[0].shape
    count = len(pieces)
    shape = (count * (rows - EXTRA), width)
    return pl.pallas_call(
        functools.partial(join_far_kernel, block_rows, spare),
        in_specs=[spec_vmem()] * (count + 2),
        out_shape=[
            jax.ShapeDtypeStruct(shape, BF16),
            jax.ShapeDtypeStruct((near_index.shape[0] + count * block_rows, width), jnp.int32),
            jax.ShapeDtypeStruct((near_rows.shape[0] + shape[0], width), BF16),
        ],
        compiler_params=PARAMS,
        cost_estimate=cost(0, 8 * shape[0] * width),
    )(near_rows, near_index, *pieces)


def window_kernel(places, *refs):
    pieces = refs[: len(places)]
    window, sems = refs[-2:]
    copies = [
        pltpu.make_async_copy(piece, window.at[pl.ds(place, piece.shape[0])], sems.at[n])
        for n, (piece, place) in enumerate(zip(pieces, places))
    ]
    for copy in copies:
        copy.start()
    if len(places) > 1:
        window[window.shape[0] - 1] = jnp.zeros(window.shape[1:], window.dtype)
    for copy in copies:
        copy.wait()


def window_with(pieces, places, blocks, window=None):
    _, tile, width = pieces[0].shape
    begun = [] if window is None else [window]
    return pl.pallas_call(
        functools.partial(window_kernel, places),
        in_specs=[spec_vmem()] * (len(pieces) + len(begun)),
        out_specs=spec_vmem(),
        out_shape=jax.ShapeDtypeStruct((blocks, tile, width), BF16),
        input_output_aliases={len(pieces): 0} if begun else {},
        scratch_shapes=[pltpu.SemaphoreType.DMA((len(pieces),))],
        compiler_params=PARAMS,
        cost_estimate=cost(0, 4 * sum(math.prod(piece.shape) for piece in pieces)),
    )(*pieces, *begun)


def stack_kernel(*refs):
    *pieces, out_ref, sems = refs
    copies = []
    base = 0
    for n, piece in enumerate(pieces):
        size = piece.shape[0]
        copies.append(pltpu.make_async_copy(piece, out_ref.at[pl.ds(base, size)], sems.at[n]))
        base += size
    for copy in copies:
        copy.start()
    for copy in copies:
        copy.wait()


def stacked(pieces):
    shape = (sum(piece.shape[0] for piece in pieces), *pieces[0].shape[1:])
    return pl.pallas_call(
        stack_kernel,
        in_specs=[spec_vmem()] * len(pieces),
        out_shape=jax.ShapeDtypeStruct(shape, BF16),
        scratch_shapes=[pltpu.SemaphoreType.DMA((len(pieces),))],
        compiler_params=PARAMS,
        cost_estimate=cost(0, 4 * math.prod(shape)),
    )(*pieces)


def gather_kernel(group, index, window, *refs):
    outs = refs[-group:]
    vals = refs[:-group]
    block_rows = outs[0].shape[0]
    part = vals[-1].shape[0]

    @pl.loop(0, part)
    def _(i):
        row = 0
        for val in vals:
            for b in range(0, val.shape[0], part):
                slots = range(val.shape[1])
                lhs = jnp.concatenate([val[b + i, s] for s in slots], axis=1)
                rhs = jnp.concatenate([window[index[row + i, s]] for s in slots], axis=0)
                made = jnp.dot(lhs, rhs, preferred_element_type=F32).astype(BF16)
                outs[row // block_rows][row % block_rows + i] = made
                row += part


def sparse_gather(index, vals, window, group):
    rows = sum(val.shape[0] for val in vals)
    slots = vals[0].shape[1]
    blocks, _, width = window.shape
    return pl.pallas_call(
        functools.partial(gather_kernel, group),
        in_specs=[spec_smem()] + [spec_vmem()] * (len(vals) + 1),
        out_shape=[jax.ShapeDtypeStruct((rows // group, TILE, width), BF16)] * group,
        compiler_params=PARAMS,
        cost_estimate=cost(
            rows * slots * TILE * TILE * width * 2,
            rows * slots * TILE * TILE * 2 + blocks * TILE * width * 2,
        ),
    )(index, window, *vals)


def prepare_kernel(group, weight_ref, rows_ref, turned_ref):
    width = weight_ref.shape[0] // group
    rank = lax.axis_index("repl")
    for d in range(group):
        start = pl.multiple_of((rank ^ d) * width, width)
        chunk = weight_ref[pl.ds(start, width), :]
        rows_ref[pl.ds(d * width, width), :] = chunk
        turned_ref[:, pl.ds(d * width, width)] = chunk.T


def prepared(weight, group):
    rows, columns = weight.shape
    return pl.pallas_call(
        functools.partial(prepare_kernel, group),
        in_specs=[spec_vmem()],
        out_shape=[
            jax.ShapeDtypeStruct((rows, columns), BF16),
            jax.ShapeDtypeStruct((columns, rows), BF16),
        ],
        compiler_params=PARAMS,
        cost_estimate=cost(0, 6 * rows * columns),
    )(weight)


def dense_kernel(group, *refs):
    parts = refs[:group]
    weight_ref, turned_ref, cotangent_ref, output_ref, slope_ref = refs[group : group + 5]
    backs = refs[group + 5 :]
    blocks, tile, width = parts[0].shape
    steps = 2
    blocks = blocks // steps
    rows = blocks * tile

    for g in range(steps):
        at = pl.ds(g * rows, rows)
        blocks_at = pl.ds(g * blocks, blocks)
        aggregate = jnp.concatenate([p[blocks_at].reshape(rows, width) for p in parts], axis=1)
        preact = jnp.dot(aggregate, weight_ref[...], preferred_element_type=F32)
        sigma = jax.nn.sigmoid(preact)
        output_ref[at, :] = (preact * sigma).astype(BF16)
        slope = sigma * (1.0 + preact * (1.0 - sigma))
        slope = (cotangent_ref[at, :].astype(F32) * slope).astype(BF16)
        slope_ref[at, :] = slope
        backward = jnp.dot(slope, turned_ref[...], preferred_element_type=F32).astype(BF16)
        for d in range(group):
            piece = backward[:, d * width : (d + 1) * width]
            backs[d][blocks_at] = piece.reshape(blocks, tile, width)


def dense(parts, weight, turned, cotangent):
    group = len(parts)
    node_rows, feat_out = cotangent.shape
    feat_in = weight.shape[0]
    return pl.pallas_call(
        functools.partial(dense_kernel, group),
        in_specs=[spec_vmem()] * (group + 3),
        out_shape=[jax.ShapeDtypeStruct((node_rows, feat_out), BF16)] * 2
        + [jax.ShapeDtypeStruct(parts[0].shape, BF16)] * group,
        compiler_params=PARAMS,
        cost_estimate=cost(
            4 * node_rows * feat_in * feat_out,
            2 * (5 * node_rows * feat_out + 2 * feat_in * feat_out),
        ),
    )(*parts, weight, turned, cotangent)


def term_kernel(slope_ref, *refs):
    group = len(refs) // 2
    slope = slope_ref[...]
    for d in range(group):
        part = refs[d][...].reshape(slope.shape[0], -1)
        term = lax.dot_general(part, slope, (((0,), (0,)), ((), ())), preferred_element_type=F32)
        refs[group + d][...] = term.astype(BF16)


def weight_terms(parts, slope):
    group = len(parts)
    width = parts[0].shape[-1]
    node_rows, feat_out = slope.shape
    return pl.pallas_call(
        term_kernel,
        in_specs=[spec_vmem()] * (group + 1),
        out_shape=[jax.ShapeDtypeStruct((width, feat_out), BF16)] * group,
        compiler_params=PARAMS,
        cost_estimate=cost(
            2 * node_rows * width * group * feat_out, 2 * 3 * node_rows * feat_out
        ),
    )(slope, *parts)


def scatter_kernel(group, cuts, index, *refs):
    total = refs[-1]
    outs = refs[-1 - len(cuts) : -1]
    backs = refs[-1 - len(cuts) - group : -1 - len(cuts)]
    vals = refs[: -1 - len(cuts) - group]
    block_rows = backs[0].shape[0]
    part = vals[-1].shape[0]
    total[...] = jnp.zeros_like(total)

    @pl.loop(0, part)
    def _(i):
        row = 0
        for val in vals:
            for b in range(0, val.shape[0], part):
                turned = backs[row // block_rows][row % block_rows + i].T
                for s in range(0, val.shape[1], 2):
                    rhs = jnp.concatenate([val[b + i, s], val[b + i, s + 1]], axis=1)
                    made = jnp.dot(turned, rhs, preferred_element_type=F32)
                    total[index[row + i, s]] += made[:, :TILE]
                    total[index[row + i, s + 1]] += made[:, TILE:]
                row += part

    for out_ref, (start, size) in zip(outs, cuts):
        out_ref[...] = total[pl.ds(start, size)].astype(BF16)


def sparse_scatter(index, vals, backs, cuts):
    group = len(backs)
    rows = sum(val.shape[0] for val in vals)
    slots = vals[0].shape[1]
    width = backs[0].shape[-1]
    return pl.pallas_call(
        functools.partial(scatter_kernel, group, cuts),
        in_specs=[spec_smem()] + [spec_vmem()] * (len(vals) + group),
        out_shape=[jax.ShapeDtypeStruct((size, width, TILE), BF16) for _, size in cuts],
        scratch_shapes=[pltpu.VMEM((SPAN * rows + 1, width, TILE), F32)],
        compiler_params=PARAMS,
        cost_estimate=cost(
            rows * slots * TILE * TILE * width * 2,
            rows * slots * TILE * TILE * 2 + 6 * rows * TILE * width * 2,
        ),
    )(index, *vals, *backs)


def sum_kernel(bases, size, *refs):
    terms = refs[: len(bases)]
    for n, out_ref in enumerate(refs[len(bases) :]):
        total = jnp.zeros(out_ref.shape, F32)
        for ref, base in zip(terms, bases):
            total += ref[pl.ds(base + n * size, size)].astype(F32)
        out_ref[...] = total.astype(BF16)


def summed(terms, bases, size, count):
    shape = (size, *terms[0].shape[1:])
    return pl.pallas_call(
        functools.partial(sum_kernel, bases, size),
        in_specs=[spec_vmem()] * len(terms),
        out_shape=[jax.ShapeDtypeStruct(shape, BF16)] * count,
        compiler_params=PARAMS,
        cost_estimate=cost(0, count * math.prod(shape) * 2 * (len(terms) + 1)),
    )(*terms)


def place_kernel(rank_ref, *refs):
    out_ref = refs[-1]
    for d, ref in enumerate(refs[:-1]):
        blocks, width, tile = ref.shape
        start = pl.multiple_of((rank_ref[0] ^ d) * width, width)
        for b in range(blocks):
            out_ref[pl.ds(b * tile, tile), pl.ds(start, width)] = ref[b].T


def placed(rank, parts):
    blocks, width, tile = parts[0].shape
    shape = (blocks * tile, width * len(parts))
    return pl.pallas_call(
        place_kernel,
        in_specs=[spec_smem()] + [spec_vmem()] * len(parts),
        out_shape=jax.ShapeDtypeStruct(shape, BF16),
        compiler_params=PARAMS,
        cost_estimate=cost(0, 2 * 2 * shape[0] * shape[1]),
    )(rank, *parts)


def rows_kernel(scale, rank_ref, *refs):
    out_ref = refs[-1]
    for d, ref in enumerate(refs[:-1]):
        size = ref.shape[0]
        start = pl.multiple_of((rank_ref[0] ^ d) * size, size)
        out_ref[pl.ds(start, size), :] = ref[...].astype(F32) * scale


def rows_placed(rank, parts, scale):
    size, columns = parts[0].shape
    return pl.pallas_call(
        functools.partial(rows_kernel, scale),
        in_specs=[spec_smem()] + [spec_vmem()] * len(parts),
        out_shape=jax.ShapeDtypeStruct((size * len(parts), columns), F32),
        compiler_params=PARAMS,
        cost_estimate=cost(0, 6 * size * len(parts) * columns),
    )(rank, *parts)


def local(feats, weight, tile_vals, tile_cols, tile_count, cotangent):
    node_rows = feats.shape[0]
    cycle = lax.axis_size("blk")
    group = lax.axis_size("repl")
    assert group & (group - 1) == 0 and cycle & (cycle - 1) == 0
    block_rows = node_rows // TILE
    panel_blocks = block_rows * group
    spare = SPAN * panel_blocks
    far_side = group // 2
    where = jnp.reshape(lax.axis_index("repl"), (1,)).astype(jnp.int32)

    sent = split_columns(feats, tile_cols, tile_count, panel_blocks, cycle, group)
    mine = [sent[0]] + [swapped(sent[d], "repl", d) for d in range(1, group)]
    half = block_rows // 2
    ready = after(tile_vals, mine[1])
    own_vals = [ready[:half], ready[half:]]
    mine[far_side] = after(mine[far_side], *own_vals)
    near_rows, near_index = join_near(mine[:far_side], block_rows, spare)
    far_rows, index, rows = join_far(
        near_rows, near_index, mine[far_side:], block_rows, spare
    )
    near_part, far_part, panel = [
        value.reshape(-1, TILE, value.shape[-1]) for value in (near_rows, far_rows, rows)
    ]

    ahead_near = mirrored(near_part, -2)
    ahead_far = mirrored(after(far_part, ahead_near), -2)
    ahead = stacked([ahead_near, ahead_far])
    beside = mirrored(panel, 1)
    behind = mirrored(after(panel, ahead_far), 2)
    relayed = mirrored(after(ahead, beside), 1)
    places = [n * panel_blocks for n in range(SPAN)]
    window = window_with([behind, panel, beside, ahead], [places[n] for n in (0, 2, 3, 4)], spare + 1)
    window = window_with([relayed], [places[1]], spare + 1, window)

    carried = [swapped(after(part, mine[far_side]), "repl", far_side) for part in own_vals]
    near = range(1, far_side)
    vals = own_vals + [swapped(after(tile_vals, sent[1]), "repl", d) for d in near]
    vals += carried + [swapped(part, "repl", d) for d in near for part in carried]
    columns = sparse_gather(index, vals, window, group)
    aggregate = [columns[0]] + [swapped(columns[d], "repl", d) for d in range(1, group)]

    made = dense(aggregate, *prepared(after(weight, panel), group), cotangent)
    output, slope, backs = made[0], made[1], made[2:]
    backs = [backs[0]] + [swapped(backs[d], "repl", d) for d in range(1, group)]

    terms = weight_terms(aggregate, after(slope, backs[1]))
    arrived = [swapped(terms[d], "repl", d) for d in range(1, group)]
    backs[0] = after(backs[0], terms[0])
    chunk = terms[0].astype(F32)
    for term in arrived:
        chunk = chunk + term.astype(F32)
    rounded = lax.optimization_barrier(chunk.astype(BF16))

    member = panel_blocks // 2
    cuts = [(places[n], panel_blocks) for n in (0, 1, 2, 4)]
    cuts += [(places[3] + member, member), (places[3], member)]
    far, relay, own, joined, *beside_shares = sparse_scatter(index, vals, backs, cuts)
    relay_in = mirrored(relay, 1)
    far_in = mirrored(far, -2)
    (joined,) = summed([joined, relay_in], [0, 0], panel_blocks, 1)
    joined_in = mirrored(after(joined, far_in), 2)

    masks = [1 << n for n in range(cycle.bit_length() - 1)]
    masks[:2] = masks[1::-1]
    sums = [after(rounded, own)]
    others = []
    beside_in = [mirrored(beside_shares[0], 1)]
    for mask in masks:
        others.append(swapped(sums[-1], "blk", mask))
        if mask == masks[-1]:
            break
        base = after(sums[-1], joined if mask == masks[0] else beside_in[0])
        chunk = base.astype(F32) + others[-1].astype(F32)
        sums.append(lax.optimization_barrier(chunk.astype(BF16)))
        if mask == masks[0]:
            beside_in.append(mirrored(after(beside_shares[1], sums[-1]), 1))
    owned = []
    for n in (1, 0):
        terms = [own, far_in, joined_in, beside_in[1 - n]]
        base = n * member
        owned = [*summed(terms, [base, base, base, 0], block_rows, far_side), *owned]
    gathered = [owned[0]] + [swapped(owned[d], "repl", d) for d in range(1, group)]
    grad_rows = placed(where, gathered)
    chunk = after(sums[-1], owned[far_side]).astype(F32) + others[-1].astype(F32)
    rounded = lax.optimization_barrier(chunk.astype(BF16))
    chunks = [rounded] + [swapped(rounded, "repl", d) for d in range(1, group)]
    scale = 1.0 / math.sqrt(node_rows * group * cycle)
    weight_grad = rows_placed(after(where, grad_rows), chunks, scale)
    return (output, weight_grad, grad_rows)


def solution(mesh):
    in_specs = (
        P(("blk", "repl"), None),
        P(),
        P(("blk", "repl"), None, None, None),
        P(("blk", "repl"), None),
        P(("blk", "repl")),
        P(("blk", "repl"), None),
    )
    out_specs = (P(("blk", "repl"), None), P(), P(("blk", "repl"), None))
    return jax.shard_map(local, mesh=mesh, in_specs=in_specs, out_specs=out_specs, check_vma=False)
```

```python
import functools
import math

import jax
import jax.numpy as jnp
from jax import lax
from jax.experimental import pallas as pl
from jax.experimental.pallas import tpu as pltpu
from jax.sharding import PartitionSpec as P

TILE = 128
REACH = 2
SPAN = 2 * REACH + 1
VMEM_LIMIT = 32 * 1024 * 1024
PARAMS = pltpu.CompilerParams(vmem_limit_bytes=VMEM_LIMIT)
FIRST_PARAMS = pltpu.CompilerParams(vmem_limit_bytes=60 * 1024 * 1024)
EXTRA = 16
BF16 = jnp.bfloat16
F32 = jnp.float32


def mirrored(value, steps):
    count = lax.axis_size("blk")
    pairs = [(k, (k + steps * (1 - 2 * (k & 1))) % count) for k in range(count)]
    return lax.ppermute(value, "blk", pairs)


def after(value, *others):
    return lax.optimization_barrier((value, *others))[0]


def swapped(value, axis, mask):
    count = lax.axis_size(axis)
    return lax.ppermute(value, axis, [(source, source ^ mask) for source in range(count)])


def spec_smem():
    return pl.BlockSpec(memory_space=pltpu.SMEM)


def spec_vmem():
    return pl.BlockSpec(memory_space=pltpu.VMEM)


def spec_hbm():
    return pl.BlockSpec(memory_space=pltpu.HBM)


def cost(flops, bytes_accessed):
    return pl.CostEstimate(flops=flops, bytes_accessed=bytes_accessed, transcendentals=0)


def split_kernel(panel_blocks, cycle, cols_hbm, count_hbm, feats_hbm, *refs):
    cols_ref, count_ref, place_ref, sems = refs[-4:]
    outs = refs[:-4]
    group = len(outs)
    rows, width = feats_hbm.shape[0], outs[0].shape[1]
    block_rows, slots = cols_ref.shape
    rank = lax.axis_index("repl")
    center = lax.axis_index("blk")
    small = [
        pltpu.make_async_copy(cols_hbm, cols_ref, sems.at[group]),
        pltpu.make_async_copy(count_hbm, count_ref, sems.at[group + 1]),
    ]
    large = []
    for d, out_ref in enumerate(outs):
        start = pl.multiple_of((rank ^ d) * width, width)
        large.append(
            pltpu.make_async_copy(
                feats_hbm.at[:, pl.ds(start, width)], out_ref.at[pl.ds(0, rows)], sems.at[d]
            )
        )
    for copy in small + large:
        copy.start()
    for copy in small:
        copy.wait()
    sign = 1 - 2 * (center & 1)
    cols = cols_ref[...]
    offset = (cols // panel_blocks - center) & (cycle - 1)
    offset = jnp.where(offset > REACH, offset - cycle, offset) * sign
    place = (offset + REACH) * panel_blocks + (cols & (panel_blocks - 1))
    row = lax.broadcasted_iota(jnp.int32, cols.shape, 0)
    slot = lax.broadcasted_iota(jnp.int32, cols.shape, 1)
    live = jnp.zeros(cols.shape, jnp.int32)
    for r in range(block_rows):
        live = jnp.where(row == r, count_ref[r], live)
    place = jnp.where(slot < live, place, SPAN * panel_blocks)
    place_ref[...] = jnp.zeros_like(place_ref)
    place_ref[pl.ds(0, block_rows), pl.ds(0, slots)] = place.astype(F32)
    for out_ref in outs:
        out_ref[pl.ds(rows, EXTRA), :] = place_ref[...].astype(BF16)
    for copy in large:
        copy.wait()


def split_columns(feats, tile_cols, tile_count, panel_blocks, cycle, group):
    rows, columns = feats.shape
    width = columns // group
    return pl.pallas_call(
        functools.partial(split_kernel, panel_blocks, cycle),
        in_specs=[spec_hbm()] * 3,
        out_shape=[jax.ShapeDtypeStruct((rows + EXTRA, width), feats.dtype)] * group,
        scratch_shapes=[
            pltpu.VMEM(tile_cols.shape, jnp.int32),
            pltpu.SMEM(tile_count.shape, jnp.int32),
            pltpu.VMEM((EXTRA, width), F32),
            pltpu.SemaphoreType.DMA((group + 2,)),
        ],
        compiler_params=FIRST_PARAMS,
        cost_estimate=cost(0, 2 * rows * columns * 2),
    )(tile_cols, tile_count, feats)


def place_rows(piece, rows, block_rows, spare):
    place = piece[pl.ds(rows, EXTRA), :].astype(F32).astype(jnp.int32)[:block_rows]
    return jnp.where(place < spare, place ^ (lax.axis_index("repl") * block_rows), place)


def join_near_kernel(block_rows, spare, own_hbm, *refs):
    *pieces, part_ref, index_ref, own_ref, sem = refs
    copy = pltpu.make_async_copy(own_hbm, own_ref, sem)
    copy.start()
    rows = own_ref.shape[0] - EXTRA
    for d, piece in enumerate(pieces, 1):
        part_ref[pl.ds(d * rows, rows), :] = piece[pl.ds(0, rows), :]
        place = place_rows(piece, rows, block_rows, spare)
        index_ref[pl.ds(d * block_rows, block_rows), :] = place
    copy.wait()
    part_ref[pl.ds(0, rows), :] = own_ref[pl.ds(0, rows), :]
    index_ref[pl.ds(0, block_rows), :] = place_rows(own_ref, rows, block_rows, spare)


def join_near(pieces, block_rows, spare):
    rows, width = pieces[0].shape
    count = len(pieces)
    shape = (count * (rows - EXTRA), width)
    return pl.pallas_call(
        functools.partial(join_near_kernel, block_rows, spare),
        in_specs=[spec_hbm()] + [spec_vmem()] * (count - 1),
        out_shape=[
            jax.ShapeDtypeStruct(shape, BF16),
            jax.ShapeDtypeStruct((count * block_rows, width), jnp.int32),
        ],
        scratch_shapes=[pltpu.VMEM((rows, width), BF16), pltpu.SemaphoreType.DMA(())],
        compiler_params=PARAMS,
        cost_estimate=cost(0, 4 * shape[0] * width),
    )(*pieces)


def join_far_kernel(block_rows, spare, near_ref, near_index_ref, *refs):
    *pieces, part_ref, index_ref, whole_ref = refs
    begin = near_ref.shape[0]
    begin_index = near_index_ref.shape[0]
    rows = part_ref.shape[0] // len(pieces)
    whole_ref[pl.ds(0, begin), :] = near_ref[...]
    index_ref[pl.ds(0, begin_index), :] = near_index_ref[...]
    for d, piece in enumerate(pieces):
        values = piece[pl.ds(0, rows), :]
        part_ref[pl.ds(d * rows, rows), :] = values
        whole_ref[pl.ds(begin + d * rows, rows), :] = values
        place = place_rows(piece, rows, block_rows, spare)
        index_ref[pl.ds(begin_index + d * block_rows, block_rows), :] = place


def join_far(near_rows, near_index, pieces, block_rows, spare):
    rows, width = pieces[0].shape
    count = len(pieces)
    shape = (count * (rows - EXTRA), width)
    return pl.pallas_call(
        functools.partial(join_far_kernel, block_rows, spare),
        in_specs=[spec_vmem()] * (count + 2),
        out_shape=[
            jax.ShapeDtypeStruct(shape, BF16),
            jax.ShapeDtypeStruct((near_index.shape[0] + count * block_rows, width), jnp.int32),
            jax.ShapeDtypeStruct((near_rows.shape[0] + shape[0], width), BF16),
        ],
        compiler_params=PARAMS,
        cost_estimate=cost(0, 8 * shape[0] * width),
    )(near_rows, near_index, *pieces)


def window_kernel(places, *refs):
    pieces = refs[: len(places)]
    window, sems = refs[-2:]
    copies = [
        pltpu.make_async_copy(piece, window.at[pl.ds(place, piece.shape[0])], sems.at[n])
        for n, (piece, place) in enumerate(zip(pieces, places))
    ]
    for copy in copies:
        copy.start()
    if len(places) > 1:
        window[window.shape[0] - 1] = jnp.zeros(window.shape[1:], window.dtype)
    for copy in copies:
        copy.wait()


def window_with(pieces, places, blocks, window=None):
    _, tile, width = pieces[0].shape
    begun = [] if window is None else [window]
    return pl.pallas_call(
        functools.partial(window_kernel, places),
        in_specs=[spec_vmem()] * (len(pieces) + len(begun)),
        out_specs=spec_vmem(),
        out_shape=jax.ShapeDtypeStruct((blocks, tile, width), BF16),
        input_output_aliases={len(pieces): 0} if begun else {},
        scratch_shapes=[pltpu.SemaphoreType.DMA((len(pieces),))],
        compiler_params=PARAMS,
        cost_estimate=cost(0, 4 * sum(math.prod(piece.shape) for piece in pieces)),
    )(*pieces, *begun)


def stack_kernel(*refs):
    *pieces, out_ref, sems = refs
    copies = []
    base = 0
    for n, piece in enumerate(pieces):
        size = piece.shape[0]
        copies.append(pltpu.make_async_copy(piece, out_ref.at[pl.ds(base, size)], sems.at[n]))
        base += size
    for copy in copies:
        copy.start()
    for copy in copies:
        copy.wait()


def stacked(pieces):
    shape = (sum(piece.shape[0] for piece in pieces), *pieces[0].shape[1:])
    return pl.pallas_call(
        stack_kernel,
        in_specs=[spec_vmem()] * len(pieces),
        out_shape=jax.ShapeDtypeStruct(shape, BF16),
        scratch_shapes=[pltpu.SemaphoreType.DMA((len(pieces),))],
        compiler_params=PARAMS,
        cost_estimate=cost(0, 4 * math.prod(shape)),
    )(*pieces)


def gather_kernel(group, index, window, *refs):
    outs = refs[-group:]
    vals = refs[:-group]
    block_rows = outs[0].shape[0]
    part = vals[-1].shape[0]

    @pl.loop(0, part)
    def _(i):
        row = 0
        for val in vals:
            for b in range(0, val.shape[0], part):
                slots = range(val.shape[1])
                lhs = jnp.concatenate([val[b + i, s] for s in slots], axis=1)
                rhs = jnp.concatenate([window[index[row + i, s]] for s in slots], axis=0)
                made = jnp.dot(lhs, rhs, preferred_element_type=F32).astype(BF16)
                outs[row // block_rows][row % block_rows + i] = made
                row += part


def sparse_gather(index, vals, window, group):
    rows = sum(val.shape[0] for val in vals)
    slots = vals[0].shape[1]
    blocks, _, width = window.shape
    return pl.pallas_call(
        functools.partial(gather_kernel, group),
        in_specs=[spec_smem()] + [spec_vmem()] * (len(vals) + 1),
        out_shape=[jax.ShapeDtypeStruct((rows // group, TILE, width), BF16)] * group,
        compiler_params=PARAMS,
        cost_estimate=cost(
            rows * slots * TILE * TILE * width * 2,
            rows * slots * TILE * TILE * 2 + blocks * TILE * width * 2,
        ),
    )(index, window, *vals)


def prepare_kernel(group, weight_ref, rows_ref, turned_ref):
    width = weight_ref.shape[0] // group
    rank = lax.axis_index("repl")
    for d in range(group):
        start = pl.multiple_of((rank ^ d) * width, width)
        chunk = weight_ref[pl.ds(start, width), :]
        rows_ref[pl.ds(d * width, width), :] = chunk
        turned_ref[:, pl.ds(d * width, width)] = chunk.T


def prepared(weight, group):
    rows, columns = weight.shape
    return pl.pallas_call(
        functools.partial(prepare_kernel, group),
        in_specs=[spec_vmem()],
        out_shape=[
            jax.ShapeDtypeStruct((rows, columns), BF16),
            jax.ShapeDtypeStruct((columns, rows), BF16),
        ],
        compiler_params=PARAMS,
        cost_estimate=cost(0, 6 * rows * columns),
    )(weight)


def dense_kernel(group, *refs):
    parts = refs[:group]
    weight_ref, turned_ref, cotangent_ref, output_ref, slope_ref = refs[group : group + 5]
    backs = refs[group + 5 :]
    blocks, tile, width = parts[0].shape
    steps = 2
    blocks = blocks // steps
    rows = blocks * tile

    for g in range(steps):
        at = pl.ds(g * rows, rows)
        blocks_at = pl.ds(g * blocks, blocks)
        aggregate = jnp.concatenate([p[blocks_at].reshape(rows, width) for p in parts], axis=1)
        preact = jnp.dot(aggregate, weight_ref[...], preferred_element_type=F32)
        sigma = jax.nn.sigmoid(preact)
        output_ref[at, :] = (preact * sigma).astype(BF16)
        slope = sigma * (1.0 + preact * (1.0 - sigma))
        slope = (cotangent_ref[at, :].astype(F32) * slope).astype(BF16)
        slope_ref[at, :] = slope
        backward = jnp.dot(slope, turned_ref[...], preferred_element_type=F32).astype(BF16)
        for d in range(group):
            piece = backward[:, d * width : (d + 1) * width]
            backs[d][blocks_at] = piece.reshape(blocks, tile, width)


def dense(parts, weight, turned, cotangent):
    group = len(parts)
    node_rows, feat_out = cotangent.shape
    feat_in = weight.shape[0]
    return pl.pallas_call(
        functools.partial(dense_kernel, group),
        in_specs=[spec_vmem()] * (group + 3),
        out_shape=[jax.ShapeDtypeStruct((node_rows, feat_out), BF16)] * 2
        + [jax.ShapeDtypeStruct(parts[0].shape, BF16)] * group,
        compiler_params=PARAMS,
        cost_estimate=cost(
            4 * node_rows * feat_in * feat_out,
            2 * (5 * node_rows * feat_out + 2 * feat_in * feat_out),
        ),
    )(*parts, weight, turned, cotangent)


def term_kernel(slope_ref, *refs):
    group = len(refs) // 2
    slope = slope_ref[...]
    for d in range(group):
        part = refs[d][...].reshape(slope.shape[0], -1)
        term = lax.dot_general(part, slope, (((0,), (0,)), ((), ())), preferred_element_type=F32)
        refs[group + d][...] = term.astype(BF16)


def weight_terms(parts, slope):
    group = len(parts)
    width = parts[0].shape[-1]
    node_rows, feat_out = slope.shape
    return pl.pallas_call(
        term_kernel,
        in_specs=[spec_vmem()] * (group + 1),
        out_shape=[jax.ShapeDtypeStruct((width, feat_out), BF16)] * group,
        compiler_params=PARAMS,
        cost_estimate=cost(
            2 * node_rows * width * group * feat_out, 2 * 3 * node_rows * feat_out
        ),
    )(slope, *parts)


def scatter_kernel(group, cuts, index, *refs):
    total = refs[-1]
    outs = refs[-1 - len(cuts) : -1]
    backs = refs[-1 - len(cuts) - group : -1 - len(cuts)]
    vals = refs[: -1 - len(cuts) - group]
    block_rows = backs[0].shape[0]
    part = vals[-1].shape[0]
    total[...] = jnp.zeros_like(total)

    @pl.loop(0, part)
    def _(i):
        row = 0
        for val in vals:
            for b in range(0, val.shape[0], part):
                turned = backs[row // block_rows][row % block_rows + i].T
                for s in range(0, val.shape[1], 2):
                    rhs = jnp.concatenate([val[b + i, s], val[b + i, s + 1]], axis=1)
                    made = jnp.dot(turned, rhs, preferred_element_type=F32)
                    total[index[row + i, s]] += made[:, :TILE]
                    total[index[row + i, s + 1]] += made[:, TILE:]
                row += part

    for out_ref, (start, size) in zip(outs, cuts):
        out_ref[...] = total[pl.ds(start, size)].astype(BF16)


def sparse_scatter(index, vals, backs, cuts):
    group = len(backs)
    rows = sum(val.shape[0] for val in vals)
    slots = vals[0].shape[1]
    width = backs[0].shape[-1]
    return pl.pallas_call(
        functools.partial(scatter_kernel, group, cuts),
        in_specs=[spec_smem()] + [spec_vmem()] * (len(vals) + group),
        out_shape=[jax.ShapeDtypeStruct((size, width, TILE), BF16) for _, size in cuts],
        scratch_shapes=[pltpu.VMEM((SPAN * rows + 1, width, TILE), F32)],
        compiler_params=PARAMS,
        cost_estimate=cost(
            rows * slots * TILE * TILE * width * 2,
            rows * slots * TILE * TILE * 2 + 6 * rows * TILE * width * 2,
        ),
    )(index, *vals, *backs)


def sum_kernel(bases, size, *refs):
    terms = refs[: len(bases)]
    for n, out_ref in enumerate(refs[len(bases) :]):
        total = jnp.zeros(out_ref.shape, F32)
        for ref, base in zip(terms, bases):
            total += ref[pl.ds(base + n * size, size)].astype(F32)
        out_ref[...] = total.astype(BF16)


def summed(terms, bases, size, count):
    shape = (size, *terms[0].shape[1:])
    return pl.pallas_call(
        functools.partial(sum_kernel, bases, size),
        in_specs=[spec_vmem()] * len(terms),
        out_shape=[jax.ShapeDtypeStruct(shape, BF16)] * count,
        compiler_params=PARAMS,
        cost_estimate=cost(0, count * math.prod(shape) * 2 * (len(terms) + 1)),
    )(*terms)


def place_kernel(rank_ref, *refs):
    out_ref = refs[-1]
    for d, ref in enumerate(refs[:-1]):
        blocks, width, tile = ref.shape
        start = pl.multiple_of((rank_ref[0] ^ d) * width, width)
        for b in range(blocks):
            out_ref[pl.ds(b * tile, tile), pl.ds(start, width)] = ref[b].T


def placed(rank, parts):
    blocks, width, tile = parts[0].shape
    shape = (blocks * tile, width * len(parts))
    return pl.pallas_call(
        place_kernel,
        in_specs=[spec_smem()] + [spec_vmem()] * len(parts),
        out_shape=jax.ShapeDtypeStruct(shape, BF16),
        compiler_params=PARAMS,
        cost_estimate=cost(0, 2 * 2 * shape[0] * shape[1]),
    )(rank, *parts)


def rows_kernel(scale, rank_ref, *refs):
    out_ref = refs[-1]
    for d, ref in enumerate(refs[:-1]):
        size = ref.shape[0]
        start = pl.multiple_of((rank_ref[0] ^ d) * size, size)
        out_ref[pl.ds(start, size), :] = ref[...].astype(F32) * scale


def rows_placed(rank, parts, scale):
    size, columns = parts[0].shape
    return pl.pallas_call(
        functools.partial(rows_kernel, scale),
        in_specs=[spec_smem()] + [spec_vmem()] * len(parts),
        out_shape=jax.ShapeDtypeStruct((size * len(parts), columns), F32),
        compiler_params=PARAMS,
        cost_estimate=cost(0, 6 * size * len(parts) * columns),
    )(rank, *parts)


def local(feats, weight, tile_vals, tile_cols, tile_count, cotangent):
    node_rows = feats.shape[0]
    cycle = lax.axis_size("blk")
    group = lax.axis_size("repl")
    assert group & (group - 1) == 0 and cycle & (cycle - 1) == 0
    block_rows = node_rows // TILE
    panel_blocks = block_rows * group
    spare = SPAN * panel_blocks
    far_side = group // 2
    where = jnp.reshape(lax.axis_index("repl"), (1,)).astype(jnp.int32)

    sent = split_columns(feats, tile_cols, tile_count, panel_blocks, cycle, group)
    mine = [sent[0]] + [swapped(sent[d], "repl", d) for d in range(1, group)]
    half = block_rows // 2
    ready = after(tile_vals, mine[1])
    own_vals = [ready[:half], ready[half:]]
    mine[far_side] = after(mine[far_side], *own_vals)
    near_rows, near_index = join_near(mine[:far_side], block_rows, spare)
    far_rows, index, rows = join_far(
        near_rows, near_index, mine[far_side:], block_rows, spare
    )
    near_part, far_part, panel = [
        value.reshape(-1, TILE, value.shape[-1]) for value in (near_rows, far_rows, rows)
    ]

    ahead_near = mirrored(near_part, -2)
    ahead_far = mirrored(after(far_part, ahead_near), -2)
    ahead = stacked([ahead_near, ahead_far])
    beside = mirrored(panel, 1)
    behind = mirrored(after(panel, ahead_far), 2)
    relayed = mirrored(after(ahead, beside), 1)
    places = [n * panel_blocks for n in range(SPAN)]
    window = window_with([behind, panel, beside, ahead], [places[n] for n in (0, 2, 3, 4)], spare + 1)
    window = window_with([relayed], [places[1]], spare + 1, window)

    carried = [swapped(after(part, mine[far_side]), "repl", far_side) for part in own_vals]
    near = range(1, far_side)
    vals = own_vals + [swapped(after(tile_vals, sent[1]), "repl", d) for d in near]
    vals += carried + [swapped(part, "repl", d) for d in near for part in carried]
    columns = sparse_gather(index, vals, window, group)
    aggregate = [columns[0]] + [swapped(columns[d], "repl", d) for d in range(1, group)]

    made = dense(aggregate, *prepared(after(weight, panel), group), cotangent)
    output, slope, backs = made[0], made[1], made[2:]
    backs = [backs[0]] + [swapped(backs[d], "repl", d) for d in range(1, group)]

    terms = weight_terms(aggregate, after(slope, backs[1]))
    arrived = [swapped(terms[d], "repl", d) for d in range(1, group)]
    backs[0] = after(backs[0], terms[0])
    chunk = terms[0].astype(F32)
    for term in arrived:
        chunk = chunk + term.astype(F32)
    rounded = lax.optimization_barrier(chunk.astype(BF16))

    member = panel_blocks // 2
    cuts = [(places[n], panel_blocks) for n in (0, 1, 2, 4)]
    cuts += [(places[3] + member, member), (places[3], member)]
    far, relay, own, joined, *beside_shares = sparse_scatter(index, vals, backs, cuts)
    relay_in = mirrored(relay, 1)
    far_in = mirrored(far, -2)
    (joined,) = summed([joined, relay_in], [0, 0], panel_blocks, 1)
    joined_in = mirrored(after(joined, far_in), 2)

    masks = [1 << n for n in range(cycle.bit_length() - 1)]
    masks[:2] = masks[1::-1]
    sums = [after(rounded, own)]
    others = []
    beside_in = [mirrored(beside_shares[0], 1)]
    for mask in masks:
        others.append(swapped(sums[-1], "blk", mask))
        if mask == masks[-1]:
            break
        base = after(sums[-1], joined if mask == masks[0] else beside_in[0])
        chunk = base.astype(F32) + others[-1].astype(F32)
        sums.append(lax.optimization_barrier(chunk.astype(BF16)))
        if mask == masks[0]:
            beside_in.append(mirrored(after(beside_shares[1], sums[-1]), 1))
    owned = []
    for n in (1, 0):
        terms = [own, far_in, joined_in, beside_in[1 - n]]
        base = n * member
        owned = [*summed(terms, [base, base, base, 0], block_rows, far_side), *owned]
    gathered = [owned[0]] + [swapped(owned[d], "repl", d) for d in range(1, group)]
    grad_rows = placed(where, gathered)
    chunk = after(sums[-1], owned[far_side]).astype(F32) + others[-1].astype(F32)
    rounded = lax.optimization_barrier(chunk.astype(BF16))
    chunks = {0: rounded}
    mask = far_side
    while mask:
        for d in sorted(chunks):
            chunks[d | mask] = swapped(chunks[d], "repl", mask)
        mask //= 2
    chunks = [chunks[d] for d in range(group)]
    scale = 1.0 / math.sqrt(node_rows * group * cycle)
    weight_grad = rows_placed(after(where, grad_rows), chunks, scale)
    return (output, weight_grad, grad_rows)


def solution(mesh):
    in_specs = (
        P(("blk", "repl"), None),
        P(),
        P(("blk", "repl"), None, None, None),
        P(("blk", "repl"), None),
        P(("blk", "repl")),
        P(("blk", "repl"), None),
    )
    out_specs = (P(("blk", "repl"), None), P(), P(("blk", "repl"), None))
    return jax.shard_map(local, mesh=mesh, in_specs=in_specs, out_specs=out_specs, check_vma=False)
```
